32 devices in a mesh: shard: 4 (over x, core), ctx: 8 (over z, y).
Axes of the slice: x: 2, y: 2, z: 4, core: 2. Of those that a mesh axis runs over, the one named last changes fastest.
Arguments:
- inputs: bfloat16 [8, 1024, 512], P('shard', 'ctx'), may hold values from -6 to 6
- memory: bfloat16 [8, 20, 512], P('shard'), may hold values from -6 to 6
- lengths: int32 [8], P('shard'), may hold values from 128 to 1024, as said below
- w_query: bfloat16 [512, 512], P('shard'), may hold values from -0.25 to 0.25
- w_key: bfloat16 [512, 512], P('shard'), may hold values from -0.25 to 0.25
- w_value: bfloat16 [512, 512], P('shard'), may hold values from -0.25 to 0.25
- w_out: bfloat16 [512, 512], P('shard'), may hold values from -6 to 6
- w_up: bfloat16 [512, 2048], P('shard'), may hold values from -0.25 to 0.25
- w_down: bfloat16 [2048, 512], P('shard'), may hold values from -0.125 to 0.125
- b_query: bfloat16 [512], P('shard'), may hold values from -3 to 3
- b_value: bfloat16 [512], P('shard'), may hold values from -0.0625 to 0.0625
- b_out: bfloat16 [512], P('shard'), may hold values from -3 to 3
- b_up: bfloat16 [2048], P('shard'), may hold values from -3 to 3
- b_down: bfloat16 [512], P('shard'), may hold values from -3 to 3
- first_gain: bfloat16 [512], P('shard'), may hold values from 0.5 to 1.5
- first_bias: bfloat16 [512], P('shard'), may hold values from -3 to 3
- second_gain: bfloat16 [512], P('shard'), may hold values from 0.5 to 1.5
- second_bias: bfloat16 [512], P('shard'), may hold values from -3 to 3
- out_grad: bfloat16 [8, 1024, 512], P('shard', 'ctx'), may hold values from -6 to 6
Outputs:
- layer_out: bfloat16 [8, 1024, 512], P('shard', 'ctx')
- input_grad: float32 [8, 1024, 512], P('shard', 'ctx')
- memory_grad: float32 [8, 20, 512], P('shard')
- grad_w_query: float32 [512, 512], P('shard')
- grad_w_key: float32 [512, 512], P('shard')
- grad_w_value: float32 [512, 512], P('shard')
- grad_w_out: float32 [512, 512], P('shard')
- grad_w_up: float32 [512, 2048], P('shard')
- grad_w_down: float32 [2048, 512], P('shard')
- grad_b_query: float32 [512], P('shard')
- grad_b_value: float32 [512], P('shard')
- grad_b_out: float32 [512], P('shard')
- grad_b_up: float32 [2048], P('shard')
- grad_b_down: float32 [512], P('shard')
- grad_first_gain: float32 [512], P('shard')
- grad_first_bias: float32 [512], P('shard')
- grad_second_gain: float32 [512], P('shard')
- grad_second_bias: float32 [512], P('shard')
- stream_rms: float32 [8, 3], P('shard')
The draws below stay inside these ranges and needn't reach their ends.
Inputs may be any that keep to these rules, and one draw needn't show every extreme that they name: `lengths`: in every draw one sequence is 1024 tokens long.
All inputs are finite; a program needn't handle non-finite values.
Results may differ from the reference program's by a relative error of at most 0.02.
Values may be sent and summed in bfloat16 or wider, within the bound.
A program may use at most 192 MiB of HBM per device.

```python
import jax
import jax.numpy as jnp
from jax import lax

D = 512
HEADS = 8
HEAD_DIM = 64
FF = 2048
MEM = 20
SEQS = 8
LENGTH = 1024


def draw_lengths(key, part):
    drawn = jax.random.randint(key, (SEQS,), LENGTH // 8, LENGTH + 1)
    longest = jax.random.randint(jax.random.fold_in(key, 7), (), 0, SEQS)
    return jnp.where(jnp.arange(SEQS) == longest, LENGTH, drawn).astype(jnp.int32)


def shard_levels(own_key, shape, shards, low, top_value):
    level, own = 1.0, jax.random.fold_in(own_key, 6)
    for dim, shards_of in shards:
        heights = jnp.exp(jax.random.uniform(jax.random.fold_in(own, dim), (shards_of,), jnp.float32, low / len(shards), top_value / len(shards)))
        level = level * jnp.repeat(heights, shape[dim] // shards_of).reshape([-1 if axis == dim else 1 for axis in range(len(shape))])
    return level


def normal_values(rng, dims, deviation, bound, split=(), kind=jnp.bfloat16):
    values = deviation * jax.random.normal(rng, dims, jnp.float32)
    if split:
        values = values * shard_levels(rng, dims, split, -0.22, 0.18)
    return jnp.clip(values, -bound, bound).astype(kind)


def setup_inputs(seed: int = 0) -> dict:
    splits = jax.random.split(jax.random.key(seed), 20)
    inputs = normal_values(splits[0], (SEQS, LENGTH, D), 1.0, 6.0, ((0, 4), (1, 8)))
    memory = normal_values(splits[1], (SEQS, MEM, D), 1.0, 6.0, ((0, 4),))
    lengths = draw_lengths(jax.random.fold_in(splits[19], 71), 0)
    w_query = normal_values(splits[3], (D, D), D ** -0.5, 0.25, ((0, 4),))
    w_key = normal_values(splits[4], (D, D), D ** -0.5, 0.25, ((0, 4),))
    w_value = normal_values(splits[5], (D, D), D ** -0.5, 0.25, ((0, 4),))
    w_out = normal_values(splits[6], (D, D), ((LENGTH // (5 * D) + 1) ** 0.5), 6.0, ((0, 4),))
    w_up = normal_values(splits[7], (D, FF), D ** -0.5, 0.25, ((0, 4),))
    w_down = normal_values(splits[8], (FF, D), FF ** -0.5, 0.125, ((0, 4),))
    b_query = normal_values(splits[9], (D,), 0.5, 3.0, ((0, 4),))
    b_value = normal_values(splits[10], (D,), (0.25 / (D * (LENGTH // (5 * D) + 1)) ** 0.5), 0.0625, ((0, 4),))
    b_out = normal_values(splits[11], (D,), 0.5, 3.0, ((0, 4),))
    b_up = normal_values(splits[12], (FF,), 0.5, 3.0, ((0, 4),))
    b_down = normal_values(splits[13], (D,), 0.5, 3.0, ((0, 4),))
    first_gain = jnp.clip(1.0 + 0.1 * jax.random.normal(splits[14], (D,), jnp.float32), 0.5, 1.5).astype(jnp.bfloat16)
    first_bias = normal_values(splits[15], (D,), 0.5, 3.0, ((0, 4),))
    second_gain = jnp.clip(1.0 + 0.1 * jax.random.normal(splits[16], (D,), jnp.float32), 0.5, 1.5).astype(jnp.bfloat16)
    second_bias = normal_values(splits[17], (D,), 0.5, 3.0, ((0, 4),))
    out_grad = normal_values(splits[18], (SEQS, LENGTH, D), 1.0, 6.0, ((0, 4), (1, 8)))
    return dict(inputs=inputs, memory=memory, lengths=lengths, w_query=w_query, w_key=w_key, w_value=w_value, w_out=w_out, w_up=w_up, w_down=w_down, b_query=b_query, b_value=b_value, b_out=b_out, b_up=b_up, b_down=b_down, first_gain=first_gain, first_bias=first_bias, second_gain=second_gain, second_bias=second_bias, out_grad=out_grad)


@jax.custom_vjp
def low(v):
    return lax.optimization_barrier(v.astype(jnp.bfloat16)).astype(jnp.float32)

@jax.custom_vjp
def low_back(v):
    return v

def low_keep(v):
    return (low(v), None)

def low_pass(kept, grad):
    return (grad,)

def back_keep(v):
    return (v, None)

def back_low(kept, grad):
    return (low(grad),)
low.defvjp(low_keep, low_pass)
low_back.defvjp(back_keep, back_low)
eps = 1e-05
highest = lax.Precision.HIGHEST

def exact_dot(operand, second):
    return jnp.dot(operand, second, precision=highest, preferred_element_type=jnp.float32)

def layer_norm(matrix, gain, offset):
    row_mean = lax.optimization_barrier(jnp.mean(matrix, axis=-1, keepdims=True))
    centered = matrix - row_mean
    variance = lax.optimization_barrier(jnp.mean(centered * centered, axis=-1, keepdims=True))
    return centered * lax.rsqrt(variance + eps) * gain + offset

def attend_block(query_block, key_all, value_all, key_valid):
    block_len = query_block.shape[0]
    query_heads = query_block.reshape(block_len, HEADS, HEAD_DIM)
    key_heads = key_all.reshape(-1, HEADS, HEAD_DIM)
    value_heads = value_all.reshape(-1, HEADS, HEAD_DIM)
    scores = jnp.einsum('qhd,khd->qhk', query_heads, key_heads, precision=highest) * HEAD_DIM ** (-0.5)
    scores = low_back(scores)
    scores = jnp.where(key_valid[None, None, :], scores, -1e+30)
    row_max = lax.optimization_barrier(jnp.max(scores, axis=-1, keepdims=True))
    exponent = jnp.exp(scores - row_max)
    attn_probs = low(exponent / lax.optimization_barrier(jnp.sum(exponent, axis=-1, keepdims=True)))
    mixed = jnp.einsum('qhk,khd->qhd', attn_probs, value_heads, precision=highest)
    return mixed.reshape(block_len, HEADS * HEAD_DIM)

def sequence_forward(weights, seq_inputs, seq_memory, seq_length):
    w_query, w_key, w_value, w_out, w_up, w_down, b_query, b_value, b_out, b_up, b_down, first_gain, first_bias, second_gain, second_bias = weights
    query = low(low_back(exact_dot(seq_inputs, w_query) + b_query))
    key = low(low_back(exact_dot(seq_inputs, w_key)))
    value = low(low_back(exact_dot(seq_inputs, w_value) + b_value))
    mem_key = low(low_back(exact_dot(seq_memory, w_key)))
    mem_value = low(low_back(exact_dot(seq_memory, w_value) + b_value))
    key_all = jnp.concatenate([mem_key, key], axis=0)
    value_all = jnp.concatenate([mem_value, value], axis=0)
    positions = jnp.arange(LENGTH, dtype=jnp.int32)
    token_valid = positions < seq_length
    key_valid = jnp.concatenate([jnp.ones((MEM,), dtype=bool), token_valid])
    block_rows = min(512, LENGTH)
    blocks = query.reshape(LENGTH // block_rows, block_rows, D)

    def one_block(query_block):
        return attend_block(query_block, key_all, value_all, key_valid)
    mixed = lax.map(jax.checkpoint(one_block), blocks).reshape(LENGTH, D)
    attended = low(low_back(mixed))
    branch = low_back(exact_dot(attended, w_out) + b_out)
    normed = layer_norm(seq_inputs + branch, first_gain, first_bias)
    pre_act = low_back(exact_dot(low(normed), w_up) + b_up)
    hidden = low(jax.nn.gelu(pre_act, approximate=True))
    ffn_out = low_back(exact_dot(hidden, w_down) + b_down)
    output = layer_norm(normed + ffn_out, second_gain, second_bias)
    valid_rows = token_valid.astype(jnp.float32)[:, None]
    squares = jnp.stack([jnp.sum(valid_rows * seq_inputs * seq_inputs), jnp.sum(valid_rows * branch * branch), jnp.sum(valid_rows * ffn_out * ffn_out)])
    rms_values = jnp.sqrt(squares / (seq_length.astype(jnp.float32) * D))
    return (output, rms_values)

def reference(inputs, memory, lengths, w_query, w_key, w_value, w_out, w_up, w_down, b_query, b_value, b_out, b_up, b_down, first_gain, first_bias, second_gain, second_bias, out_grad):
    params = (w_query.astype(jnp.float32), w_key.astype(jnp.float32), w_value.astype(jnp.float32), w_out.astype(jnp.float32), w_up.astype(jnp.float32), w_down.astype(jnp.float32), b_query.astype(jnp.float32), b_value.astype(jnp.float32), b_out.astype(jnp.float32), b_up.astype(jnp.float32), b_down.astype(jnp.float32), first_gain.astype(jnp.float32), first_bias.astype(jnp.float32), second_gain.astype(jnp.float32), second_bias.astype(jnp.float32))

    def whole_layer(weights, inputs_in, memory_in):

        def per_sequence(carried, sequence_in):
            seq_inputs, seq_memory, seq_length = sequence_in
            output, rms_values = sequence_forward(weights, seq_inputs, seq_memory, seq_length)
            return (carried, (output, rms_values))
        carried, (outputs, rms_all) = lax.scan(per_sequence, jnp.zeros((), jnp.float32), (inputs_in, memory_in, lengths))
        return (outputs, rms_all)
    outputs, pullback, stream_rms = jax.vjp(whole_layer, params, inputs.astype(jnp.float32), memory.astype(jnp.float32), has_aux=True)
    grads_w, input_grad, memory_grad = pullback(out_grad.astype(jnp.float32))
    return (outputs.astype(jnp.bfloat16), input_grad, memory_grad, grads_w[0], grads_w[1], grads_w[2], grads_w[3], grads_w[4], grads_w[5], grads_w[6], grads_w[7], grads_w[8], grads_w[9], grads_w[10], grads_w[11], grads_w[12], grads_w[13], grads_w[14], stream_rms)
```

```python
import math

import jax
import jax.numpy as jnp
from jax import lax
from jax.experimental import pallas as pl
from jax.experimental.pallas import tpu as pltpu
from jax.sharding import PartitionSpec as P

HEADS = 8
HEAD_DIM = 64
MEM_ROWS = 20
GELU_SCALE = math.sqrt(2 / math.pi)


eps = 1e-05


def matmul(operand, second):
    return jnp.dot(operand, second, preferred_element_type=jnp.float32)


def outer_sum(operand, second):
    return lax.dot_general(
        operand, second, (((0,), (0,)), ((), ())), preferred_element_type=jnp.float32
    )


def back_product(operand, second):
    return lax.dot_general(
        operand, second, (((1,), (1,)), ((), ())), preferred_element_type=jnp.float32
    )


def to_float(tensor):
    return tensor.astype(jnp.float32)


def smooth_act(values):
    return jax.nn.gelu(values, approximate=True)


def split_heads(tensor):
    return tensor.reshape(tensor.shape[0], tensor.shape[1], HEADS, HEAD_DIM)


def head_scores(queries, key_heads):
    return jnp.einsum(
        "sqhd,skhd->sqhk", queries, key_heads, preferred_element_type=jnp.float32
    ) * HEAD_DIM ** (-0.5)


def norm_forward(matrix, gain, offset):
    row_mean = jnp.mean(matrix, axis=-1, keepdims=True)
    centered = matrix - row_mean
    inverse = lax.rsqrt(jnp.mean(centered * centered, axis=-1, keepdims=True) + eps)
    unit_rows = centered * inverse
    return (unit_rows * gain + offset, unit_rows, inverse)


def norm_backward(cotangent, unit_rows, inverse, gain):
    scaled = cotangent * gain
    centered_grad = (
        scaled
        - jnp.mean(scaled, axis=-1, keepdims=True)
        - unit_rows * jnp.mean(scaled * unit_rows, axis=-1, keepdims=True)
    )
    return (
        inverse * centered_grad,
        jnp.sum(cotangent * unit_rows, axis=0),
        jnp.sum(cotangent, axis=0),
    )


def in_blocks(update, carried, arrays, first_row, slice_dim):
    piece_rows = arrays[0].shape[slice_dim]
    block_len = math.gcd(piece_rows, 1024)
    if block_len == piece_rows:
        return update(carried, arrays, first_row)

    def one_block(current, number):
        block_start = number * block_len
        sliced = tuple(
            (
                lax.dynamic_slice_in_dim(tensor, block_start, block_len, slice_dim)
                for tensor in arrays
            )
        )
        return (update(current, sliced, first_row + block_start), None)

    carried, unused = lax.scan(
        one_block, carried, jnp.arange(piece_rows // block_len, dtype=jnp.int32)
    )
    return carried


def softmax_update(carried, pieces, first_row, queries, lengths):
    row_max, row_total, weighted = carried
    key_piece, value_piece = pieces
    piece_rows = key_piece.shape[1]
    scores = head_scores(queries, split_heads(key_piece))
    key_mask = (first_row + jnp.arange(piece_rows, dtype=jnp.int32))[None, :] < lengths[:, None]
    scores = jnp.where(key_mask[:, None, None, :], scores, -1e30)
    new_max = jnp.maximum(row_max, jnp.max(scores, axis=-1))
    factor = jnp.exp(row_max - new_max)
    exponent = jnp.exp(scores - new_max[..., None])
    row_total = row_total * factor + jnp.sum(exponent, axis=-1)
    weighted = weighted * factor[..., None] + jnp.einsum(
        "sqhk,skhd->sqhd",
        exponent.astype(jnp.bfloat16),
        split_heads(value_piece),
        preferred_element_type=jnp.float32,
    )
    return (new_max, row_total, weighted)


def query_update(grad_q, pieces, first_row, queries, grad_heads, log_total, row_delta, lengths):
    key_piece, value_piece = pieces
    piece_rows = key_piece.shape[1]
    key_heads = split_heads(key_piece)
    scores = head_scores(queries, key_heads)
    key_mask = (first_row + jnp.arange(piece_rows, dtype=jnp.int32))[None, :] < lengths[:, None]
    scores = jnp.where(key_mask[:, None, None, :], scores, -1e30)
    attn_probs = jnp.exp(scores - log_total[..., None])
    value_dots = jnp.einsum(
        "sqhd,skhd->sqhk", grad_heads, split_heads(value_piece), preferred_element_type=jnp.float32
    )
    d_scores = (attn_probs * (value_dots - row_delta[..., None])).astype(jnp.bfloat16)
    return grad_q + jnp.einsum(
        "sqhk,skhd->sqhd", d_scores, key_heads, preferred_element_type=jnp.float32
    ) * HEAD_DIM ** (-0.5)


def key_update(carried, pieces, first_row, key_heads, value_heads, log_all, delta_all, key_mask):
    grad_k, grad_v = carried
    query_piece, grad_piece = pieces
    piece_rows = query_piece.shape[1]
    log_total = lax.dynamic_slice_in_dim(log_all, first_row, piece_rows, 1)
    row_delta = lax.dynamic_slice_in_dim(delta_all, first_row, piece_rows, 1)
    queries = split_heads(query_piece)
    grad_heads = split_heads(grad_piece)
    scores = head_scores(queries, key_heads)
    scores = jnp.where(key_mask[:, None, None, :], scores, -1e30)
    attn_probs = jnp.exp(scores - log_total[..., None])
    grad_v = grad_v + jnp.einsum(
        "sqhk,sqhd->skhd",
        attn_probs.astype(jnp.bfloat16),
        grad_heads,
        preferred_element_type=jnp.float32,
    )
    value_dots = jnp.einsum(
        "sqhd,skhd->sqhk", grad_heads, value_heads, preferred_element_type=jnp.float32
    )
    d_scores = (attn_probs * (value_dots - row_delta[..., None])).astype(jnp.bfloat16)
    grad_k = grad_k + jnp.einsum(
        "sqhk,sqhd->skhd", d_scores, queries, preferred_element_type=jnp.float32
    ) * HEAD_DIM ** (-0.5)
    return (grad_k, grad_v)


def local(
    inputs,
    memory,
    lengths,
    w_query,
    w_key,
    w_value,
    w_out,
    w_up,
    w_down,
    b_query,
    b_value,
    b_out,
    b_up,
    b_down,
    first_gain,
    first_bias,
    second_gain,
    second_bias,
    out_grad,
):
    gathered = (
        lax.all_gather(w_query, "shard", axis=0, tiled=True),
        lax.all_gather(w_key, "shard", axis=0, tiled=True),
        lax.all_gather(w_value, "shard", axis=0, tiled=True),
        lax.all_gather(w_out, "shard", axis=0, tiled=True),
        lax.all_gather(w_up, "shard", axis=0, tiled=True),
        lax.all_gather(w_down, "shard", axis=0, tiled=True),
        lax.all_gather(b_query, "shard", axis=0, tiled=True),
        lax.all_gather(b_value, "shard", axis=0, tiled=True),
        lax.all_gather(b_out, "shard", axis=0, tiled=True),
        lax.all_gather(b_up, "shard", axis=0, tiled=True),
        lax.all_gather(b_down, "shard", axis=0, tiled=True),
        lax.all_gather(first_gain, "shard", axis=0, tiled=True),
        lax.all_gather(first_bias, "shard", axis=0, tiled=True),
        lax.all_gather(second_gain, "shard", axis=0, tiled=True),
        lax.all_gather(second_bias, "shard", axis=0, tiled=True),
    )
    (
        full_query,
        full_key,
        full_value,
        full_out,
        full_up,
        full_down,
        bias_query,
        bias_value,
        bias_out,
        bias_up,
        bias_down,
        gain_one,
        offset_one,
        gain_two,
        offset_two,
    ) = gathered
    seq_count, local_len, features = inputs.shape
    mem_rows = memory.shape[1]
    token_rows = inputs.reshape(seq_count * local_len, features)
    mem_flat = memory.reshape(seq_count * mem_rows, features)
    query = (
        (matmul(token_rows, full_query) + to_float(bias_query))
        .astype(jnp.bfloat16)
        .reshape(seq_count, local_len, features)
    )
    key = matmul(token_rows, full_key).astype(jnp.bfloat16).reshape(seq_count, local_len, features)
    value = (
        (matmul(token_rows, full_value) + to_float(bias_value))
        .astype(jnp.bfloat16)
        .reshape(seq_count, local_len, features)
    )
    mem_key = matmul(mem_flat, full_key).astype(jnp.bfloat16).reshape(seq_count, mem_rows, features)
    mem_value = (
        (matmul(mem_flat, full_value) + to_float(bias_value))
        .astype(jnp.bfloat16)
        .reshape(seq_count, mem_rows, features)
    )
    query_heads = split_heads(query)
    mem_key_heads = split_heads(mem_key)
    mem_value_heads = split_heads(mem_value)
    position_zero = lax.axis_index("ctx") * local_len
    key_mask = (position_zero + jnp.arange(local_len, dtype=jnp.int32))[None, :] < lengths[:, None]
    mem_scores = head_scores(query_heads, mem_key_heads)
    mem_max = jnp.max(mem_scores, axis=-1)
    mem_exponent = jnp.exp(mem_scores - mem_max[..., None])
    start_state = (
        mem_max,
        jnp.sum(mem_exponent, axis=-1),
        jnp.einsum(
            "sqhk,skhd->sqhd",
            mem_exponent.astype(jnp.bfloat16),
            mem_value_heads,
            preferred_element_type=jnp.float32,
        ),
    )

    def forward_step(carried, pieces, first_row):
        return softmax_update(carried, pieces, first_row, query_heads, lengths)

    row_max, row_total, weighted = in_blocks(
        forward_step,
        start_state,
        (
            lax.all_gather(key, "ctx", axis=1, tiled=True),
            lax.all_gather(value, "ctx", axis=1, tiled=True),
        ),
        jnp.int32(0),
        1,
    )
    log_total = row_max + jnp.log(row_total)
    attended_full = (weighted / row_total[..., None]).reshape(seq_count, local_len, features)
    attended = attended_full.astype(jnp.bfloat16).reshape(seq_count * local_len, features)
    branch = matmul(attended, full_out) + to_float(bias_out)
    normed, unit_one, inverse_one = norm_forward(
        to_float(token_rows) + branch, to_float(gain_one), to_float(offset_one)
    )
    normed_low = normed.astype(jnp.bfloat16)
    pre_act = matmul(normed_low, full_up) + to_float(bias_up)
    activated, act_pullback = jax.vjp(smooth_act, pre_act)
    hidden = activated.astype(jnp.bfloat16)
    ffn_out = matmul(hidden, full_down) + to_float(bias_down)
    output_rows, unit_two, inverse_two = norm_forward(
        normed + ffn_out, to_float(gain_two), to_float(offset_two)
    )
    layer_out = output_rows.astype(jnp.bfloat16).reshape(seq_count, local_len, features)
    valid_rows = key_mask.astype(jnp.float32)
    input_squares = jnp.sum(jnp.square(to_float(inputs)), axis=2)
    branch_squares = jnp.sum(jnp.square(branch), axis=1).reshape(seq_count, local_len)
    ffn_squares = jnp.sum(jnp.square(ffn_out), axis=1).reshape(seq_count, local_len)
    squares = jnp.stack(
        [
            jnp.sum(valid_rows * input_squares, axis=1),
            jnp.sum(valid_rows * branch_squares, axis=1),
            jnp.sum(valid_rows * ffn_squares, axis=1),
        ],
        axis=1,
    )
    squares = lax.psum(squares, "ctx")
    stream_rms = jnp.sqrt(squares / (lengths.astype(jnp.float32)[:, None] * features))
    back_query, back_key, back_value, back_out, back_up, back_down, back_gain_one, back_gain_two = (
        lax.all_gather(w_query, "shard", axis=0, tiled=True),
        lax.all_gather(w_key, "shard", axis=0, tiled=True),
        lax.all_gather(w_value, "shard", axis=0, tiled=True),
        lax.all_gather(w_out, "shard", axis=0, tiled=True),
        lax.all_gather(w_up, "shard", axis=0, tiled=True),
        lax.all_gather(w_down, "shard", axis=0, tiled=True),
        lax.all_gather(first_gain, "shard", axis=0, tiled=True),
        lax.all_gather(second_gain, "shard", axis=0, tiled=True),
    )
    cotangent = to_float(out_grad).reshape(seq_count * local_len, features)
    grad_two, grad_gain_two, grad_offset_two = norm_backward(
        cotangent, unit_two, inverse_two, to_float(back_gain_two)
    )
    grad_ffn = grad_two.astype(jnp.bfloat16)
    grad_bias_down = jnp.sum(grad_ffn, axis=0, dtype=jnp.float32)
    grad_full_down = outer_sum(hidden, grad_ffn)
    grad_hidden = back_product(grad_ffn, back_down)
    grad_pre = act_pullback(grad_hidden)[0].astype(jnp.bfloat16)
    grad_bias_up = jnp.sum(grad_pre, axis=0, dtype=jnp.float32)
    grad_full_up = outer_sum(normed_low, grad_pre)
    grad_normed = grad_two + back_product(grad_pre, back_up)
    grad_one, grad_gain_one, grad_offset_one = norm_backward(
        grad_normed, unit_one, inverse_one, to_float(back_gain_one)
    )
    grad_branch = grad_one.astype(jnp.bfloat16)
    grad_bias_out = jnp.sum(grad_branch, axis=0, dtype=jnp.float32)
    grad_full_out = outer_sum(attended, grad_branch)
    grad_att = (
        back_product(grad_branch, back_out)
        .astype(jnp.bfloat16)
        .reshape(seq_count, local_len, features)
    )
    row_delta = jnp.sum(
        (to_float(grad_att) * attended_full).reshape(seq_count, local_len, HEADS, HEAD_DIM), axis=-1
    )
    log_all, delta_all = (
        lax.all_gather(log_total, "ctx", axis=1, tiled=True),
        lax.all_gather(row_delta, "ctx", axis=1, tiled=True),
    )
    grad_heads = split_heads(grad_att)
    mem_probs = jnp.exp(head_scores(query_heads, mem_key_heads) - log_total[..., None])
    mem_dots = jnp.einsum(
        "sqhd,skhd->sqhk", grad_heads, mem_value_heads, preferred_element_type=jnp.float32
    )
    mem_dscores = (mem_probs * (mem_dots - row_delta[..., None])).astype(jnp.bfloat16)
    start_query = jnp.einsum(
        "sqhk,skhd->sqhd", mem_dscores, mem_key_heads, preferred_element_type=jnp.float32
    ) * HEAD_DIM ** (-0.5)
    mem_grad_key = jnp.einsum(
        "sqhk,sqhd->skhd", mem_dscores, query_heads, preferred_element_type=jnp.float32
    ) * HEAD_DIM ** (-0.5)
    mem_grad_value = jnp.einsum(
        "sqhk,sqhd->skhd",
        mem_probs.astype(jnp.bfloat16),
        grad_heads,
        preferred_element_type=jnp.float32,
    )
    key_heads = split_heads(key)
    value_heads = split_heads(value)
    empty_grads = jnp.zeros(key_heads.shape, jnp.float32)

    def query_step(carried, pieces, first_row):
        return query_update(
            carried, pieces, first_row, query_heads, grad_heads, log_total, row_delta, lengths
        )

    def key_step(carried, pieces, first_row):
        return key_update(
            carried, pieces, first_row, key_heads, value_heads, log_all, delta_all, key_mask
        )

    grad_q = in_blocks(
        query_step,
        start_query,
        (
            lax.all_gather(key, "ctx", axis=1, tiled=True),
            lax.all_gather(value, "ctx", axis=1, tiled=True),
        ),
        jnp.int32(0),
        1,
    )
    grad_k, grad_v = in_blocks(
        key_step,
        (empty_grads, empty_grads),
        (
            lax.all_gather(query, "ctx", axis=1, tiled=True),
            lax.all_gather(grad_att, "ctx", axis=1, tiled=True),
        ),
        jnp.int32(0),
        1,
    )
    mem_key_sum, mem_value_sum = lax.psum((mem_grad_key, mem_grad_value), "ctx")
    mem_key_low = mem_key_sum.reshape(seq_count * mem_rows, features).astype(jnp.bfloat16)
    mem_value_low = mem_value_sum.reshape(seq_count * mem_rows, features).astype(jnp.bfloat16)
    first_only = (lax.axis_index("ctx") == 0).astype(jnp.float32)
    grad_q_low = grad_q.reshape(seq_count * local_len, features).astype(jnp.bfloat16)
    grad_k_low = grad_k.reshape(seq_count * local_len, features).astype(jnp.bfloat16)
    grad_v_low = grad_v.reshape(seq_count * local_len, features).astype(jnp.bfloat16)
    grad_full_query = outer_sum(token_rows, grad_q_low)
    grad_full_key = outer_sum(token_rows, grad_k_low) + first_only * outer_sum(
        mem_flat, mem_key_low
    )
    grad_full_value = outer_sum(token_rows, grad_v_low) + first_only * outer_sum(
        mem_flat, mem_value_low
    )
    grad_bias_query = jnp.sum(grad_q_low, axis=0, dtype=jnp.float32)
    grad_bias_value = jnp.sum(grad_v_low, axis=0, dtype=jnp.float32) + first_only * jnp.sum(
        mem_value_low, axis=0, dtype=jnp.float32
    )
    input_grad = (
        grad_one
        + back_product(grad_q_low, back_query)
        + back_product(grad_k_low, back_key)
        + back_product(grad_v_low, back_value)
    ).reshape(seq_count, local_len, features)
    memory_grad = (
        back_product(mem_key_low, back_key) + back_product(mem_value_low, back_value)
    ).reshape(seq_count, mem_rows, features)
    owned_parts = (
        lax.psum_scatter(
            grad_full_query.astype(jnp.bfloat16), "shard", scatter_dimension=0, tiled=True
        ).astype(jnp.float32),
        lax.psum_scatter(
            grad_full_key.astype(jnp.bfloat16), "shard", scatter_dimension=0, tiled=True
        ).astype(jnp.float32),
        lax.psum_scatter(
            grad_full_value.astype(jnp.bfloat16), "shard", scatter_dimension=0, tiled=True
        ).astype(jnp.float32),
        lax.psum_scatter(
            grad_full_out.astype(jnp.bfloat16), "shard", scatter_dimension=0, tiled=True
        ).astype(jnp.float32),
        lax.psum_scatter(
            grad_full_up.astype(jnp.bfloat16), "shard", scatter_dimension=0, tiled=True
        ).astype(jnp.float32),
        lax.psum_scatter(
            grad_full_down.astype(jnp.bfloat16), "shard", scatter_dimension=0, tiled=True
        ).astype(jnp.float32),
        lax.psum_scatter(
            grad_bias_query.astype(jnp.bfloat16), "shard", scatter_dimension=0, tiled=True
        ).astype(jnp.float32),
        lax.psum_scatter(
            grad_bias_value.astype(jnp.bfloat16), "shard", scatter_dimension=0, tiled=True
        ).astype(jnp.float32),
        lax.psum_scatter(
            grad_bias_out.astype(jnp.bfloat16), "shard", scatter_dimension=0, tiled=True
        ).astype(jnp.float32),
        lax.psum_scatter(
            grad_bias_up.astype(jnp.bfloat16), "shard", scatter_dimension=0, tiled=True
        ).astype(jnp.float32),
        lax.psum_scatter(
            grad_bias_down.astype(jnp.bfloat16), "shard", scatter_dimension=0, tiled=True
        ).astype(jnp.float32),
        lax.psum_scatter(
            grad_gain_one.astype(jnp.bfloat16), "shard", scatter_dimension=0, tiled=True
        ).astype(jnp.float32),
        lax.psum_scatter(
            grad_offset_one.astype(jnp.bfloat16), "shard", scatter_dimension=0, tiled=True
        ).astype(jnp.float32),
        lax.psum_scatter(
            grad_gain_two.astype(jnp.bfloat16), "shard", scatter_dimension=0, tiled=True
        ).astype(jnp.float32),
        lax.psum_scatter(
            grad_offset_two.astype(jnp.bfloat16), "shard", scatter_dimension=0, tiled=True
        ).astype(jnp.float32),
    )
    (
        part_query,
        part_key,
        part_value,
        part_out,
        part_up,
        part_down,
        part_bias_query,
        part_bias_value,
        part_bias_out,
        part_bias_up,
        part_bias_down,
        part_gain_one,
        part_offset_one,
        part_gain_two,
        part_offset_two,
    ) = owned_parts
    summed_grads = lax.psum(
        (
            part_query,
            part_key,
            part_value,
            part_out,
            part_up,
            part_down,
            part_bias_query,
            part_bias_value,
            part_bias_out,
            part_bias_up,
            part_bias_down,
            part_gain_one,
            part_offset_one,
            part_gain_two,
            part_offset_two,
        ),
        "ctx",
    )
    (
        sum_query,
        sum_key,
        sum_value,
        sum_out,
        sum_up,
        sum_down,
        sum_bias_query,
        sum_bias_value,
        sum_bias_out,
        sum_bias_up,
        sum_bias_down,
        sum_gain_one,
        sum_offset_one,
        sum_gain_two,
        sum_offset_two,
    ) = summed_grads
    return (
        layer_out,
        input_grad,
        memory_grad,
        sum_query,
        sum_key,
        sum_value,
        sum_out,
        sum_up,
        sum_down,
        sum_bias_query,
        sum_bias_value,
        sum_bias_out,
        sum_bias_up,
        sum_bias_down,
        sum_gain_one,
        sum_offset_one,
        sum_gain_two,
        sum_offset_two,
        stream_rms,
    )


MESH_ID = pl.DeviceIdType.MESH
LANES = 128
MEM_PAD = 32
ROW_KINDS = 16
SLOTS = 104


def flipped(index, offset, bits):
    total = 0
    for bit in range(bits):
        digit = lax.rem(lax.div(index, 2**bit), 2)
        if offset >> bit & 1:
            digit = 1 - digit
        total = total + digit * 2**bit
    return total


class Copies:
    def __init__(self, send_sems, recv_sems):
        self.send_sems, self.recv_sems = send_sems, recv_sems
        self.started = []

    def send(self, src, dst, device):
        slot = len(self.started)
        copy = pltpu.make_async_remote_copy(
            src_ref=src,
            dst_ref=dst,
            send_sem=self.send_sems.at[slot],
            recv_sem=self.recv_sems.at[slot],
            device_id=device,
            device_id_type=MESH_ID,
        )
        copy.start()
        self.started.append(copy)
        return copy

    def local(self, src, dst):
        slot = len(self.started)
        copy = pltpu.make_async_copy(src, dst, self.send_sems.at[slot])
        copy.start()
        self.started.append(None)
        return copy

    def finish(self):
        for copy in self.started:
            if copy is not None:
                copy.wait_send()


def layer_kernel(
    x_ref,
    g_ref,
    mem_ref,
    len_ref,
    vec_ref,
    wq_ref,
    wk_ref,
    wv_ref,
    wo_ref,
    wu_ref,
    wd_ref,
    o_layer,
    o_input,
    o_mem,
    o_fin,
    o_qkv,
    o_vec,
    o_rms,
    tokens,
    tokens_t,
    w_heads,
    w_out,
    w_up,
    w_down,
    vecs,
    q_scaled,
    q_aug,
    k_aug,
    v_mask,
    k_turned,
    v_turned,
    probs,
    d_scores,
    mixed_t,
    mixed,
    att,
    hidden,
    act_slope,
    d_pre,
    d_att,
    d_mixed,
    partial,
    got_core,
    got_x,
    got_y,
    got_z,
    got_far,
    final,
    head_part,
    head_core,
    head_x,
    head_far,
    head_all,
    vec_part,
    dx_part,
    dx_got,
    dx_far_sum,
    dx_far,
    mem_part,
    mem_far,
    squares,
    send_sems,
    recv_sems,
):
    bf16, f32 = jnp.bfloat16, jnp.float32
    shard, ctx = lax.axis_index("shard"), lax.axis_index("ctx")
    span, width = x_ref.shape[1], x_ref.shape[2]
    spans = 8
    length_all = span * spans
    keys = length_all + MEM_PAD
    x_half, core = lax.div(shard, 2), lax.rem(shard, 2)
    upper, pair = lax.div(ctx, 4), lax.rem(ctx, 4)
    y_side = lax.rem(ctx, 2)
    z_side = lax.rem(lax.div(ctx, 2) + upper, 2)

    def shard_peer(offset):
        return {"shard": flipped(shard, offset, 2), "ctx": ctx}

    def ctx_peer(offset):
        return {"shard": shard, "ctx": flipped(ctx, offset, 3)}

    def span_rows(index):
        return pl.ds(pl.multiple_of(index * span, span), span)

    def pair_lanes(index, size=LANES):
        return pl.ds(pl.multiple_of(index * LANES, LANES), size)

    copies = Copies(send_sems, recv_sems)

    barrier = pltpu.get_barrier_semaphore()
    for offset in (1, 2, 3):
        pl.semaphore_signal(barrier, inc=1, device_id=shard_peer(offset), device_id_type=MESH_ID)
    for offset in range(1, 8):
        pl.semaphore_signal(barrier, inc=1, device_id=ctx_peer(offset), device_id_type=MESH_ID)
    pl.semaphore_wait(barrier, 10)

    far_tokens = copies.send(x_ref.at[1 - upper], tokens.at[span_rows(ctx)], ctx_peer(6))
    head_copies = []
    my_rows = pl.ds(pl.multiple_of(shard * LANES, LANES), LANES)
    for offset in (2, 3, 1):
        for part, ref in enumerate((wq_ref, wk_ref, wv_ref)):
            head_copies.append(
                copies.send(
                    ref.at[:, pair_lanes(pair)],
                    w_heads.at[my_rows, pl.ds(part * LANES, LANES)],
                    shard_peer(offset),
                )
            )
        head_copies.append(copies.send(vec_ref, vecs.at[shard], shard_peer(offset)))
    near_tokens = [
        copies.send(x_ref.at[upper], tokens.at[span_rows(ctx)], ctx_peer(offset))
        for offset in (3, 2, 1)
    ]
    local_copies = [
        copies.local(ref.at[:, pair_lanes(pair)], w_heads.at[my_rows, pl.ds(part * LANES, LANES)])
        for part, ref in enumerate((wq_ref, wk_ref, wv_ref))
    ]
    local_copies.append(copies.local(vec_ref, vecs.at[shard]))
    local_copies.append(copies.local(x_ref.at[upper], tokens.at[span_rows(ctx)]))

    def rows_of(ref, index):
        rows = ref.shape[0] // 4
        return ref.at[pl.ds(pl.multiple_of(index * rows, LANES), rows)]

    full_weights = ((wo_ref, w_out), (wu_ref, w_up), (wd_ref, w_down))
    from_x = [
        copies.send(ref, rows_of(full, shard), shard_peer(2)) for ref, full in full_weights
    ]
    from_core = [
        copies.send(ref, rows_of(full, shard), shard_peer(1)) for ref, full in full_weights
    ]
    own_weights = [copies.local(ref, rows_of(full, shard)) for ref, full in full_weights]

    far_tokens.wait_recv()
    partner_rows = span_rows(flipped(ctx, 6, 3))
    passed_tokens = [
        copies.send(tokens.at[partner_rows], tokens.at[partner_rows], ctx_peer(offset))
        for offset in (3, 2, 1)
    ]

    for copy in local_copies:
        copy.wait()
    for copy in head_copies + near_tokens + passed_tokens:
        copy.wait_recv()

    def full_vec(kind):
        return jnp.concatenate([vecs[owner, kind : kind + 1, :] for owner in range(4)], axis=1)

    length = len_ref[upper]
    lane = lax.broadcasted_iota(jnp.int32, (span * 2, LANES), 1)

    def put_query(rows, projected):
        scaled = (projected + vecs[pair, 0:1, :]).astype(bf16).astype(f32) * (HEAD_DIM**-0.5)
        q_scaled[rows, :] = scaled.astype(bf16)
        q_aug[0, rows, :] = jnp.where(
            lane < HEAD_DIM, scaled, jnp.where(lane == HEAD_DIM, 1.0, 0.0)
        ).astype(bf16)
        q_aug[1, rows, :] = jnp.where(
            lane >= HEAD_DIM, scaled, jnp.where(lane == 0, 1.0, 0.0)
        ).astype(bf16)

    def put_key_value(rows, key, value, left_out):
        lanes = lax.broadcasted_iota(jnp.int32, key.shape, 1)
        key = key.astype(bf16).astype(f32)
        value = (value + vecs[pair, 1:2, :]).astype(bf16).astype(f32)
        k_aug[0, rows, :] = jnp.where(
            lanes < HEAD_DIM, key, jnp.where(lanes == HEAD_DIM, left_out, 0.0)
        ).astype(bf16)
        k_aug[1, rows, :] = jnp.where(
            lanes >= HEAD_DIM, key, jnp.where(lanes == 0, left_out, 0.0)
        ).astype(bf16)
        v_mask[0, rows, :] = jnp.where(lanes < HEAD_DIM, value, 0.0).astype(bf16)
        v_mask[1, rows, :] = jnp.where(lanes >= HEAD_DIM, value, 0.0).astype(bf16)
        k_turned[:, rows] = key.T.astype(bf16)
        v_turned[:, rows] = value.T.astype(bf16)

    for block in range(4):
        rows = pl.ds(block * span * 2, span * 2)
        projected = matmul(tokens[rows, :], w_heads[...])
        put_query(rows, projected[:, :LANES])
        position = block * span * 2 + lax.broadcasted_iota(jnp.int32, (span * 2, LANES), 0)
        put_key_value(
            rows,
            projected[:, LANES : 2 * LANES],
            projected[:, 2 * LANES :],
            jnp.where(position < length, 0.0, -1e30),
        )
    projected = matmul(mem_ref[upper], w_heads[:, LANES:])
    position = lax.broadcasted_iota(jnp.int32, (MEM_PAD, LANES), 0)
    put_key_value(
        pl.ds(length_all, MEM_PAD),
        projected[:, :LANES],
        projected[:, LANES:],
        jnp.where(position < MEM_ROWS, 0.0, -1e30),
    )

    att_copies = []
    for high in (3, 2, 1, 0):
        block = lax.div(flipped(ctx, 2 * high, 3), 2)
        rows = pl.ds(pl.multiple_of(block * span * 2, span * 2), span * 2)
        for head in range(2):
            scores = back_product(k_aug[head], q_aug[head, rows, :])
            exponent = jnp.exp(scores - jnp.max(scores, axis=0, keepdims=True))
            total = jnp.sum(exponent, axis=0, keepdims=True)
            weights = (exponent * (1.0 / total)).astype(bf16)
            probs[head, :, rows] = weights
            half = pl.ds(head * HEAD_DIM, HEAD_DIM)
            mixed_t[half, rows] = matmul(v_turned[half, :], weights)
        mixed[rows, :] = mixed_t[:, rows].T.astype(bf16)
        for low in (0, 1):
            offset = 2 * high + low
            source = mixed.at[span_rows(flipped(ctx, offset, 3))]
            target = att.at[span_rows(upper), pair_lanes(pair)]
            if offset:
                att_copies.append(copies.send(source, target, ctx_peer(offset)))
            else:
                own_att = copies.local(source, target)

    passed_weights = []
    for copy, (_, full) in zip(from_x, full_weights):
        copy.wait_recv()
        source = rows_of(full, flipped(shard, 2, 2))
        passed_weights.append(copies.send(source, source, shard_peer(1)))
    for block in range(4):
        rows = pl.ds(block * span * 2, span * 2)
        tokens_t[:, rows] = tokens[rows, :].astype(f32).T.astype(bf16)
    for copy in own_weights:
        copy.wait()
    for copy in from_core + passed_weights:
        copy.wait_recv()
    own_att.wait()
    for copy in att_copies:
        copy.wait_recv()

    seqs = x_ref.shape[0]
    local_rows = seqs * span
    own_x = x_ref[...].reshape(local_rows, width).astype(f32)
    branch = matmul(att[...], w_out[...]) + full_vec(2)
    normed, unit_one, inverse_one = norm_forward(own_x + branch, full_vec(4), full_vec(5))
    normed_low = normed.astype(bf16)
    ffn_out = jnp.zeros((local_rows, width), f32)
    for chunk in range(4):
        columns = pl.ds(chunk * width, width)
        bias = jnp.concatenate([vecs[chunk, 8 + i : 9 + i, :] for i in range(4)], axis=1)
        pre_act = matmul(normed_low, w_up[:, columns]) + bias
        square = pre_act * pre_act
        bent = jnp.tanh(GELU_SCALE * pre_act * (1.0 + 0.044715 * square))
        hidden[:, columns] = (0.5 * pre_act * (1.0 + bent)).astype(bf16)
        act_slope[:, columns] = 0.5 * (1.0 + bent) + 0.5 * pre_act * (1.0 - bent * bent) * (
            GELU_SCALE * (1.0 + 3 * 0.044715 * square)
        )
        ffn_out = ffn_out + matmul(hidden[:, columns], w_down[columns, :])
    ffn_out = ffn_out + full_vec(3)
    output, unit_two, inverse_two = norm_forward(normed + ffn_out, full_vec(6), full_vec(7))
    o_layer[...] = output.astype(bf16)

    cotangent = g_ref[...].reshape(local_rows, width).astype(f32)
    d_two, grad_second_gain, grad_second_bias = norm_backward(
        cotangent, unit_two, inverse_two, full_vec(6)
    )
    d_ffn = d_two.astype(bf16)
    d_normed = d_two
    grads_up_bias = []
    for chunk in range(4):
        columns = pl.ds(chunk * width, width)
        d_hidden = back_product(d_ffn, w_down[columns, :])
        d_chunk = (d_hidden * act_slope[:, columns]).astype(bf16)
        d_pre[:, columns] = d_chunk
        grads_up_bias.append(jnp.sum(d_chunk.astype(f32), axis=0, keepdims=True))
        d_normed = d_normed + back_product(d_chunk, w_up[:, columns])
    d_one, grad_first_gain, grad_first_bias = norm_backward(
        d_normed, unit_one, inverse_one, full_vec(4)
    )
    o_input[...] = d_one
    d_branch = d_one.astype(bf16)
    d_att[...] = back_product(d_branch, w_out[...]).astype(bf16)

    d_copies = []
    for offset in (6, 7, 4, 5, 2, 3, 1, 0):
        peer = flipped(ctx, offset, 3)
        source = d_att.at[span_rows(lax.div(peer, 4)), pair_lanes(lax.rem(peer, 4))]
        target = d_mixed.at[span_rows(ctx)]
        if offset:
            d_copies.append(copies.send(source, target, ctx_peer(offset)))
        else:
            own_d = copies.local(source, target)

    row_id = lax.broadcasted_iota(jnp.int32, (8, LANES), 0)
    tile = jnp.zeros((8, LANES), f32)
    for seq in range(seqs):
        position = ctx * span + lax.broadcasted_iota(jnp.int32, (span, 1), 0)
        valid = jnp.where(position < len_ref[seq], 1.0, 0.0)
        for kind, values in enumerate((own_x, branch, ffn_out)):
            piece = values[seq * span : (seq + 1) * span]
            row_sum = jnp.sum(piece * piece, axis=1, keepdims=True) * valid
            tile = tile + jnp.where(
                row_id == seq * 3 + kind, jnp.sum(row_sum, axis=0, keepdims=True), 0.0
            )
    squares[ctx] = tile
    square_copies = [
        copies.send(squares.at[ctx], squares.at[ctx], ctx_peer(offset))
        for offset in (6, 7, 4, 5, 2, 3, 1)
    ]

    chunks = ((0, width), (width, width), (2 * width, LANES))
    depth = [dict() for _ in chunks]

    def add_rows(target, first, rows):
        total = target[...].astype(f32) + first[...].astype(f32)
        target[...] = total.astype(bf16)

    def core_send(number):
        start, rows = chunks[number]
        depth[number]["core"] = [
            copies.send(
                partial.at[2 * side + 1 - core, pl.ds(start, rows)],
                got_core.at[side, pl.ds(start, rows)],
                shard_peer(1),
            )
            for side in range(2)
        ]

    def x_send(number):
        start, rows = chunks[number]
        for side, copy in enumerate(depth[number]["core"]):
            copy.wait_recv()
            add_rows(
                got_core.at[side, pl.ds(start, rows)],
                partial.at[2 * side + core, pl.ds(start, rows)],
                rows,
            )
        depth[number]["x"] = copies.send(
            got_core.at[1 - x_half, pl.ds(start, rows)],
            got_x.at[pl.ds(start, rows)],
            shard_peer(2),
        )

    def y_send(number):
        start, rows = chunks[number]
        depth[number]["x"].wait_recv()
        add_rows(got_x.at[pl.ds(start, rows)], got_core.at[x_half, pl.ds(start, rows)], rows)
        half = rows // 2
        depth[number]["y"] = copies.send(
            got_x.at[pl.ds(pl.multiple_of(start + (1 - y_side) * half, half), half)],
            got_y.at[pl.ds(start // 2, half)],
            ctx_peer(1),
        )

    def z_send(number):
        start, rows = chunks[number]
        half, quarter = rows // 2, rows // 4
        depth[number]["y"].wait_recv()
        add_rows(
            got_y.at[pl.ds(start // 2, half)],
            got_x.at[pl.ds(pl.multiple_of(start + y_side * half, half), half)],
            half,
        )
        depth[number]["z"] = copies.send(
            got_y.at[
                pl.ds(pl.multiple_of(start // 2 + (1 - z_side) * quarter, quarter), quarter)
            ],
            got_z.at[pl.ds(start // 4, quarter)],
            ctx_peer(2),
        )

    def far_send(number):
        start, rows = chunks[number]
        quarter = rows // 4
        depth[number]["z"].wait_recv()
        add_rows(
            got_z.at[pl.ds(start // 4, quarter)],
            got_y.at[pl.ds(pl.multiple_of(start // 2 + z_side * quarter, quarter), quarter)],
            quarter,
        )
        depth[number]["far"] = copies.send(
            got_z.at[pl.ds(start // 4, quarter)],
            got_far.at[pl.ds(start // 4, quarter)],
            ctx_peer(6),
        )

    def z_gather(number):
        start, rows = chunks[number]
        half, quarter = rows // 2, rows // 4
        depth[number]["far"].wait_recv()
        place = pl.ds(pl.multiple_of(start + y_side * half + z_side * quarter, quarter), quarter)
        here = pl.ds(start // 4, quarter)
        final[place, :] = (got_z[here, :].astype(f32) + got_far[here, :].astype(f32)).astype(bf16)
        depth[number]["z gather"] = copies.send(final.at[place], final.at[place], ctx_peer(2))

    def y_gather(number):
        start, rows = chunks[number]
        half = rows // 2
        depth[number]["z gather"].wait_recv()
        place = pl.ds(pl.multiple_of(start + y_side * half, half), half)
        depth[number]["y gather"] = copies.send(final.at[place], final.at[place], ctx_peer(1))

    for owner in range(4):
        partial[owner, :width, :] = outer_sum(
            hidden[:, owner * width : (owner + 1) * width], d_ffn
        ).astype(bf16)
    core_send(0)
    for chunk in range(4):
        grad_up = outer_sum(normed_low, d_pre[:, chunk * width : (chunk + 1) * width]).astype(bf16)
        for owner in range(4):
            partial[owner, width + chunk * LANES : width + (chunk + 1) * LANES, :] = grad_up[
                owner * LANES : (owner + 1) * LANES
            ]
    core_send(1)
    grad_out = outer_sum(att[...], d_branch).astype(bf16)
    for owner in range(4):
        partial[owner, 2 * width :, :] = grad_out[owner * LANES : (owner + 1) * LANES]
    core_send(2)
    x_send(0)
    x_send(1)
    x_send(2)

    grad_down_bias = jnp.sum(d_ffn.astype(f32), axis=0, keepdims=True)
    grad_out_bias = jnp.sum(d_branch.astype(f32), axis=0, keepdims=True)
    vec_part[...] = jnp.zeros_like(vec_part)
    wide_grads = (
        grad_out_bias,
        grad_down_bias,
        grad_first_gain,
        grad_first_bias,
        grad_second_gain,
        grad_second_bias,
    )
    for owner in range(4):
        for kind, values in enumerate(wide_grads):
            vec_part[owner, 2 + kind : 3 + kind, :] = values.reshape(1, width)[
                :, owner * LANES : (owner + 1) * LANES
            ]
        for piece in range(4):
            vec_part[owner, 8 + piece : 9 + piece, :] = grads_up_bias[owner][
                :, piece * LANES : (piece + 1) * LANES
            ]

    own_d.wait()
    for copy in d_copies:
        copy.wait_recv()
    d_turned = d_mixed[...].astype(f32).T * mixed_t[...]
    for head in range(2):
        half = slice(head * HEAD_DIM, (head + 1) * HEAD_DIM)
        delta = jnp.sum(d_turned[half], axis=0, keepdims=True)
        for block in range(4):
            rows = slice(block * span * 2, (block + 1) * span * 2)
            dots = back_product(v_mask[head], d_mixed[rows, :])
            weights = probs[head, :, rows].astype(f32)
            d_scores[head, :, rows] = (weights * (dots - delta[:, rows])).astype(bf16)
    y_send(0)
    key_lane = lax.broadcasted_iota(jnp.int32, (keys, LANES), 1)
    grad_value = jnp.where(
        key_lane < HEAD_DIM, matmul(probs[0], d_mixed[...]), matmul(probs[1], d_mixed[...])
    ).astype(bf16)
    grad_key = jnp.where(
        key_lane < HEAD_DIM, matmul(d_scores[0], q_scaled[...]), matmul(d_scores[1], q_scaled[...])
    ).astype(bf16)
    grad_query = jnp.concatenate(
        [
            matmul(k_turned[:HEAD_DIM, :], d_scores[0]),
            matmul(k_turned[HEAD_DIM:, :], d_scores[1]),
        ],
        axis=0,
    ) * (HEAD_DIM**-0.5)
    grad_query = grad_query.T.astype(bf16)
    joined = jnp.concatenate([grad_query, grad_key[:length_all], grad_value[:length_all]], axis=1)
    mem_joined = jnp.concatenate([grad_key[length_all:], grad_value[length_all:]], axis=1)

    for block in range(4):
        rows = slice(block * span * 2, (block + 1) * span * 2)
        dx_part[rows, :] = back_product(joined[rows], w_heads[...]).astype(bf16)
    dx_copies = [[], []]
    for order, mirror in enumerate((6, 0)):
        for offset in (3, 2, 1):
            source = dx_part.at[span_rows(flipped(ctx, offset ^ mirror, 3))]
            dx_copies[order].append(
                copies.send(source, dx_got.at[order, offset - 1], ctx_peer(offset))
            )
    mem_part[pair] = back_product(mem_joined, w_heads[:, LANES:]).astype(bf16)
    mem_copies = [
        copies.send(mem_part.at[pair], mem_part.at[pair], ctx_peer(offset)) for offset in (3, 2, 1)
    ]
    y_send(1)

    grad_heads = matmul(tokens_t[...], joined)
    mem_grad = outer_sum(mem_ref[upper], mem_joined)
    for owner in range(4):
        rows = slice(owner * LANES, (owner + 1) * LANES)
        head_part[owner, :LANES, :LANES] = grad_heads[rows, :LANES].astype(bf16)
        head_part[owner, :LANES, LANES:] = (grad_heads[rows, LANES:] + mem_grad[rows]).astype(bf16)
    query_bias = jnp.sum(grad_query.astype(f32), axis=0, keepdims=True)
    value_bias = jnp.sum(grad_value.astype(f32), axis=0, keepdims=True)
    for owner in range(4):
        mine = pair == owner
        vec_part[owner, 0:1, :] = jnp.where(mine, query_bias, 0.0)
        vec_part[owner, 1:2, :] = jnp.where(mine, value_bias, 0.0)
        head_part[owner, LANES:, :] = jnp.zeros((ROW_KINDS, 3 * LANES), bf16)
        head_part[owner, LANES:, :LANES] = vec_part[owner].astype(bf16)
    head_core_copies = [
        copies.send(head_part.at[2 * side + 1 - core], head_core.at[side], shard_peer(1))
        for side in range(2)
    ]
    y_send(2)
    z_send(0)
    for side, copy in enumerate(head_core_copies):
        copy.wait_recv()
        add_rows(head_core.at[side], head_part.at[2 * side + core], LANES)
    head_x_copy = copies.send(head_core.at[1 - x_half], head_x, shard_peer(2))
    z_send(1)

    for copy in dx_copies[0]:
        copy.wait_recv()
    far_rows = span_rows(flipped(ctx, 6, 3))
    dx_far_sum[...] = (
        dx_part[far_rows, :].astype(f32)
        + dx_got[0, 0].astype(f32)
        + dx_got[0, 1].astype(f32)
        + dx_got[0, 2].astype(f32)
    ).astype(bf16)
    dx_far_copy = copies.send(dx_far_sum, dx_far, ctx_peer(6))
    for copy in mem_copies:
        copy.wait_recv()
    mem_far[upper] = (
        mem_part[0].astype(f32)
        + mem_part[1].astype(f32)
        + mem_part[2].astype(f32)
        + mem_part[3].astype(f32)
    ).astype(bf16)
    mem_far_copy = copies.send(mem_far.at[upper], mem_far.at[upper], ctx_peer(6))
    head_x_copy.wait_recv()
    add_rows(head_x, head_core.at[x_half], LANES)
    head_far_copy = copies.send(head_x, head_far, ctx_peer(4))
    z_send(2)
    far_send(0)
    far_send(1)
    far_send(2)

    for copy in dx_copies[1]:
        copy.wait_recv()
    near = pl.ds(pl.multiple_of(upper * span, span), span)
    o_input[near, :] = (
        o_input[near, :]
        + dx_part[span_rows(ctx), :].astype(f32)
        + dx_got[1, 0].astype(f32)
        + dx_got[1, 1].astype(f32)
        + dx_got[1, 2].astype(f32)
    )
    head_far_copy.wait_recv()
    head_all[pair] = (head_x[...].astype(f32) + head_far[...].astype(f32)).astype(bf16)
    head_copies = [
        copies.send(head_all.at[pair], head_all.at[pair], ctx_peer(offset)) for offset in (3, 2, 1)
    ]
    z_gather(0)
    z_gather(1)
    z_gather(2)
    dx_far_copy.wait_recv()
    far = pl.ds(pl.multiple_of((1 - upper) * span, span), span)
    o_input[far, :] = o_input[far, :] + dx_far[...].astype(f32)
    mem_far_copy.wait_recv()
    o_mem[...] = mem_far[...].astype(f32)
    for copy in square_copies:
        copy.wait_recv()
    total = squares[0]
    for other in range(1, spans):
        total = total + squares[other]
    valid_tokens = jnp.where(row_id < 3, len_ref[0], len_ref[1]).astype(f32)
    o_rms[...] = jnp.sqrt(total / (valid_tokens * width))
    y_gather(0)
    y_gather(1)
    y_gather(2)
    for copy in head_copies:
        copy.wait_recv()
    for owner in range(4):
        for part in range(3):
            o_qkv[part, :, owner * LANES : (owner + 1) * LANES] = head_all[
                owner, :LANES, part * LANES : (part + 1) * LANES
            ]
    o_vec[...] = (
        head_all[0, LANES:, :LANES].astype(f32)
        + head_all[1, LANES:, :LANES].astype(f32)
        + head_all[2, LANES:, :LANES].astype(f32)
        + head_all[3, LANES:, :LANES].astype(f32)
    )
    for number in range(len(chunks)):
        depth[number]["y gather"].wait_recv()
    o_fin[...] = final[...]
    copies.finish()


def fast_layer(
    inputs,
    memory,
    lengths,
    w_query,
    w_key,
    w_value,
    w_out,
    w_up,
    w_down,
    b_query,
    b_value,
    b_out,
    b_up,
    b_down,
    first_gain,
    first_bias,
    second_gain,
    second_bias,
    out_grad,
):
    bf16, f32 = jnp.bfloat16, jnp.float32
    seqs, span, width = inputs.shape
    length_all, keys = 8 * span, 8 * span + MEM_PAD
    hidden_width = w_up.shape[1]
    vec = jnp.concatenate(
        [
            jnp.stack(
                [
                    b_query,
                    b_value,
                    b_out,
                    b_down,
                    first_gain,
                    first_bias,
                    second_gain,
                    second_bias,
                ]
            ),
            b_up.reshape(4, LANES),
            jnp.zeros((4, LANES), bf16),
        ]
    ).astype(f32)
    padded = jnp.pad(memory, ((0, 0), (0, MEM_PAD - memory.shape[1]), (0, 0)))
    vmem, anywhere = pl.BlockSpec(memory_space=pltpu.VMEM), pl.BlockSpec(memory_space=pl.ANY)
    smem = pl.BlockSpec(memory_space=pltpu.SMEM)
    stacked = 2 * width + LANES
    scratch = [
        ((length_all, width), bf16),
        ((width, length_all), bf16),
        ((width, 3 * LANES), bf16),
        ((width, width), bf16),
        ((width, hidden_width), bf16),
        ((hidden_width, width), bf16),
        ((4, ROW_KINDS, LANES), f32),
        ((length_all, LANES), bf16),
        ((2, length_all, LANES), bf16),
        ((2, keys, LANES), bf16),
        ((2, keys, LANES), bf16),
        ((LANES, keys), bf16),
        ((LANES, keys), bf16),
        ((2, keys, length_all), bf16),
        ((2, keys, length_all), bf16),
        ((LANES, length_all), f32),
        ((length_all, LANES), bf16),
        ((seqs * span, width), bf16),
        ((seqs * span, hidden_width), bf16),
        ((seqs * span, hidden_width), f32),
        ((seqs * span, hidden_width), bf16),
        ((seqs * span, width), bf16),
        ((length_all, LANES), bf16),
        ((4, stacked, width), bf16),
        ((2, stacked, width), bf16),
        ((stacked, width), bf16),
        ((stacked // 2, width), bf16),
        ((stacked // 4, width), bf16),
        ((stacked // 4, width), bf16),
        ((stacked, width), bf16),
        ((4, LANES + ROW_KINDS, 3 * LANES), bf16),
        ((2, LANES + ROW_KINDS, 3 * LANES), bf16),
        ((LANES + ROW_KINDS, 3 * LANES), bf16),
        ((LANES + ROW_KINDS, 3 * LANES), bf16),
        ((4, LANES + ROW_KINDS, 3 * LANES), bf16),
        ((4, ROW_KINDS, LANES), f32),
        ((length_all, width), bf16),
        ((2, 3, span, width), bf16),
        ((span, width), bf16),
        ((span, width), bf16),
        ((4, MEM_PAD, width), bf16),
        ((2, MEM_PAD, width), bf16),
        ((8, 8, LANES), f32),
    ]
    layer, input_grad, mem_grad, weight_grads, head_grads, vec_grads, rms = pl.pallas_call(
        layer_kernel,
        out_shape=[
            jax.ShapeDtypeStruct((seqs * span, width), bf16),
            jax.ShapeDtypeStruct((seqs * span, width), f32),
            jax.ShapeDtypeStruct((2, MEM_PAD, width), f32),
            jax.ShapeDtypeStruct((stacked, width), bf16),
            jax.ShapeDtypeStruct((3, LANES, width), bf16),
            jax.ShapeDtypeStruct((ROW_KINDS, LANES), f32),
            jax.ShapeDtypeStruct((8, LANES), f32),
        ],
        in_specs=[vmem, vmem, vmem, smem, vmem] + [anywhere] * 6,
        out_specs=[vmem] * 7,
        scratch_shapes=[pltpu.VMEM(shape, kind) for shape, kind in scratch]
        + [pltpu.SemaphoreType.DMA((SLOTS,)), pltpu.SemaphoreType.DMA((SLOTS,))],
        compiler_params=pltpu.CompilerParams(
            collective_id=0, has_side_effects=True, vmem_limit_bytes=60 * 2**20
        ),
        name="layer",
    )(inputs, out_grad, padded, lengths, vec, w_query, w_key, w_value, w_out, w_up, w_down)
    return (
        layer.reshape(seqs, span, width),
        input_grad.reshape(seqs, span, width),
        mem_grad[:, : memory.shape[1]],
        head_grads[0].astype(f32),
        head_grads[1].astype(f32),
        head_grads[2].astype(f32),
        weight_grads[2 * width :].astype(f32),
        weight_grads[width : 2 * width]
        .reshape(4, LANES, width)
        .transpose(1, 0, 2)
        .reshape(LANES, hidden_width)
        .astype(f32),
        weight_grads[:width].astype(f32),
        vec_grads[0],
        vec_grads[1],
        vec_grads[2],
        vec_grads[8:12].reshape(4 * LANES),
        vec_grads[3],
        vec_grads[4],
        vec_grads[5],
        vec_grads[6],
        vec_grads[7],
        rms[:6, 0].reshape(2, 3),
    )


def takes_fast_plan(mesh, inputs, memory, w_up):
    return (
        mesh.shape["shard"] == 4
        and mesh.shape["ctx"] == 8
        and inputs.shape == (2, LANES, HEADS * HEAD_DIM)
        and memory.shape[1] == MEM_ROWS
        and w_up.shape == (LANES, 4 * HEADS * HEAD_DIM)
    )


def solution(mesh):
    in_specs = (
        P("shard", "ctx", None),
        P("shard", None, None),
        P("shard"),
        P("shard", None),
        P("shard", None),
        P("shard", None),
        P("shard", None),
        P("shard", None),
        P("shard", None),
        P("shard"),
        P("shard"),
        P("shard"),
        P("shard"),
        P("shard"),
        P("shard"),
        P("shard"),
        P("shard"),
        P("shard"),
        P("shard", "ctx", None),
    )
    out_specs = (
        P("shard", "ctx", None),
        P("shard", "ctx", None),
        P("shard", None, None),
        P("shard", None),
        P("shard", None),
        P("shard", None),
        P("shard", None),
        P("shard", None),
        P("shard", None),
        P("shard"),
        P("shard"),
        P("shard"),
        P("shard"),
        P("shard"),
        P("shard"),
        P("shard"),
        P("shard"),
        P("shard"),
        P("shard", None),
    )

    def layer(*arrays):
        if takes_fast_plan(mesh, arrays[0], arrays[1], arrays[7]):
            return fast_layer(*arrays)
        return local(*arrays)

    return jax.shard_map(layer, mesh=mesh, in_specs=in_specs, out_specs=out_specs, check_vma=False)
```

```python
import math

import jax
import jax.numpy as jnp
from jax import lax
from jax.experimental import pallas as pl
from jax.experimental.pallas import tpu as pltpu
from jax.sharding import PartitionSpec as P

HEADS = 8
HEAD_DIM = 64
MEM_ROWS = 20
GELU_SCALE = math.sqrt(2 / math.pi)


eps = 1e-05


def matmul(operand, second):
    return jnp.dot(operand, second, preferred_element_type=jnp.float32)


def outer_sum(operand, second):
    return lax.dot_general(
        operand, second, (((0,), (0,)), ((), ())), preferred_element_type=jnp.float32
    )


def back_product(operand, second):
    return lax.dot_general(
        operand, second, (((1,), (1,)), ((), ())), preferred_element_type=jnp.float32
    )


def to_float(tensor):
    return tensor.astype(jnp.float32)


def smooth_act(values):
    return jax.nn.gelu(values, approximate=True)


def split_heads(tensor):
    return tensor.reshape(tensor.shape[0], tensor.shape[1], HEADS, HEAD_DIM)


def head_scores(queries, key_heads):
    return jnp.einsum(
        "sqhd,skhd->sqhk", queries, key_heads, preferred_element_type=jnp.float32
    ) * HEAD_DIM ** (-0.5)


def norm_forward(matrix, gain, offset):
    row_mean = jnp.mean(matrix, axis=-1, keepdims=True)
    centered = matrix - row_mean
    inverse = lax.rsqrt(jnp.mean(centered * centered, axis=-1, keepdims=True) + eps)
    unit_rows = centered * inverse
    return (unit_rows * gain + offset, unit_rows, inverse)


def norm_backward(cotangent, unit_rows, inverse, gain):
    scaled = cotangent * gain
    centered_grad = (
        scaled
        - jnp.mean(scaled, axis=-1, keepdims=True)
        - unit_rows * jnp.mean(scaled * unit_rows, axis=-1, keepdims=True)
    )
    return (
        inverse * centered_grad,
        jnp.sum(cotangent * unit_rows, axis=0),
        jnp.sum(cotangent, axis=0),
    )


def in_blocks(update, carried, arrays, first_row, slice_dim):
    piece_rows = arrays[0].shape[slice_dim]
    block_len = math.gcd(piece_rows, 1024)
    if block_len == piece_rows:
        return update(carried, arrays, first_row)

    def one_block(current, number):
        block_start = number * block_len
        sliced = tuple(
            (
                lax.dynamic_slice_in_dim(tensor, block_start, block_len, slice_dim)
                for tensor in arrays
            )
        )
        return (update(current, sliced, first_row + block_start), None)

    carried, unused = lax.scan(
        one_block, carried, jnp.arange(piece_rows // block_len, dtype=jnp.int32)
    )
    return carried


def softmax_update(carried, pieces, first_row, queries, lengths):
    row_max, row_total, weighted = carried
    key_piece, value_piece = pieces
    piece_rows = key_piece.shape[1]
    scores = head_scores(queries, split_heads(key_piece))
    key_mask = (first_row + jnp.arange(piece_rows, dtype=jnp.int32))[None, :] < lengths[:, None]
    scores = jnp.where(key_mask[:, None, None, :], scores, -1e30)
    new_max = jnp.maximum(row_max, jnp.max(scores, axis=-1))
    factor = jnp.exp(row_max - new_max)
    exponent = jnp.exp(scores - new_max[..., None])
    row_total = row_total * factor + jnp.sum(exponent, axis=-1)
    weighted = weighted * factor[..., None] + jnp.einsum(
        "sqhk,skhd->sqhd",
        exponent.astype(jnp.bfloat16),
        split_heads(value_piece),
        preferred_element_type=jnp.float32,
    )
    return (new_max, row_total, weighted)


def query_update(grad_q, pieces, first_row, queries, grad_heads, log_total, row_delta, lengths):
    key_piece, value_piece = pieces
    piece_rows = key_piece.shape[1]
    key_heads = split_heads(key_piece)
    scores = head_scores(queries, key_heads)
    key_mask = (first_row + jnp.arange(piece_rows, dtype=jnp.int32))[None, :] < lengths[:, None]
    scores = jnp.where(key_mask[:, None, None, :], scores, -1e30)
    attn_probs = jnp.exp(scores - log_total[..., None])
    value_dots = jnp.einsum(
        "sqhd,skhd->sqhk", grad_heads, split_heads(value_piece), preferred_element_type=jnp.float32
    )
    d_scores = (attn_probs * (value_dots - row_delta[..., None])).astype(jnp.bfloat16)
    return grad_q + jnp.einsum(
        "sqhk,skhd->sqhd", d_scores, key_heads, preferred_element_type=jnp.float32
    ) * HEAD_DIM ** (-0.5)


def key_update(carried, pieces, first_row, key_heads, value_heads, log_all, delta_all, key_mask):
    grad_k, grad_v = carried
    query_piece, grad_piece = pieces
    piece_rows = query_piece.shape[1]
    log_total = lax.dynamic_slice_in_dim(log_all, first_row, piece_rows, 1)
    row_delta = lax.dynamic_slice_in_dim(delta_all, first_row, piece_rows, 1)
    queries = split_heads(query_piece)
    grad_heads = split_heads(grad_piece)
    scores = head_scores(queries, key_heads)
    scores = jnp.where(key_mask[:, None, None, :], scores, -1e30)
    attn_probs = jnp.exp(scores - log_total[..., None])
    grad_v = grad_v + jnp.einsum(
        "sqhk,sqhd->skhd",
        attn_probs.astype(jnp.bfloat16),
        grad_heads,
        preferred_element_type=jnp.float32,
    )
    value_dots = jnp.einsum(
        "sqhd,skhd->sqhk", grad_heads, value_heads, preferred_element_type=jnp.float32
    )
    d_scores = (attn_probs * (value_dots - row_delta[..., None])).astype(jnp.bfloat16)
    grad_k = grad_k + jnp.einsum(
        "sqhk,sqhd->skhd", d_scores, queries, preferred_element_type=jnp.float32
    ) * HEAD_DIM ** (-0.5)
    return (grad_k, grad_v)


def local(
    inputs,
    memory,
    lengths,
    w_query,
    w_key,
    w_value,
    w_out,
    w_up,
    w_down,
    b_query,
    b_value,
    b_out,
    b_up,
    b_down,
    first_gain,
    first_bias,
    second_gain,
    second_bias,
    out_grad,
):
    gathered = (
        lax.all_gather(w_query, "shard", axis=0, tiled=True),
        lax.all_gather(w_key, "shard", axis=0, tiled=True),
        lax.all_gather(w_value, "shard", axis=0, tiled=True),
        lax.all_gather(w_out, "shard", axis=0, tiled=True),
        lax.all_gather(w_up, "shard", axis=0, tiled=True),
        lax.all_gather(w_down, "shard", axis=0, tiled=True),
        lax.all_gather(b_query, "shard", axis=0, tiled=True),
        lax.all_gather(b_value, "shard", axis=0, tiled=True),
        lax.all_gather(b_out, "shard", axis=0, tiled=True),
        lax.all_gather(b_up, "shard", axis=0, tiled=True),
        lax.all_gather(b_down, "shard", axis=0, tiled=True),
        lax.all_gather(first_gain, "shard", axis=0, tiled=True),
        lax.all_gather(first_bias, "shard", axis=0, tiled=True),
        lax.all_gather(second_gain, "shard", axis=0, tiled=True),
        lax.all_gather(second_bias, "shard", axis=0, tiled=True),
    )
    (
        full_query,
        full_key,
        full_value,
        full_out,
        full_up,
        full_down,
        bias_query,
        bias_value,
        bias_out,
        bias_up,
        bias_down,
        gain_one,
        offset_one,
        gain_two,
        offset_two,
    ) = gathered
    seq_count, local_len, features = inputs.shape
    mem_rows = memory.shape[1]
    token_rows = inputs.reshape(seq_count * local_len, features)
    mem_flat = memory.reshape(seq_count * mem_rows, features)
    query = (
        (matmul(token_rows, full_query) + to_float(bias_query))
        .astype(jnp.bfloat16)
        .reshape(seq_count, local_len, features)
    )
    key = matmul(token_rows, full_key).astype(jnp.bfloat16).reshape(seq_count, local_len, features)
    value = (
        (matmul(token_rows, full_value) + to_float(bias_value))
        .astype(jnp.bfloat16)
        .reshape(seq_count, local_len, features)
    )
    mem_key = matmul(mem_flat, full_key).astype(jnp.bfloat16).reshape(seq_count, mem_rows, features)
    mem_value = (
        (matmul(mem_flat, full_value) + to_float(bias_value))
        .astype(jnp.bfloat16)
        .reshape(seq_count, mem_rows, features)
    )
    query_heads = split_heads(query)
    mem_key_heads = split_heads(mem_key)
    mem_value_heads = split_heads(mem_value)
    position_zero = lax.axis_index("ctx") * local_len
    key_mask = (position_zero + jnp.arange(local_len, dtype=jnp.int32))[None, :] < lengths[:, None]
    mem_scores = head_scores(query_heads, mem_key_heads)
    mem_max = jnp.max(mem_scores, axis=-1)
    mem_exponent = jnp.exp(mem_scores - mem_max[..., None])
    start_state = (
        mem_max,
        jnp.sum(mem_exponent, axis=-1),
        jnp.einsum(
            "sqhk,skhd->sqhd",
            mem_exponent.astype(jnp.bfloat16),
            mem_value_heads,
            preferred_element_type=jnp.float32,
        ),
    )

    def forward_step(carried, pieces, first_row):
        return softmax_update(carried, pieces, first_row, query_heads, lengths)

    row_max, row_total, weighted = in_blocks(
        forward_step,
        start_state,
        (
            lax.all_gather(key, "ctx", axis=1, tiled=True),
            lax.all_gather(value, "ctx", axis=1, tiled=True),
        ),
        jnp.int32(0),
        1,
    )
    log_total = row_max + jnp.log(row_total)
    attended_full = (weighted / row_total[..., None]).reshape(seq_count, local_len, features)
    attended = attended_full.astype(jnp.bfloat16).reshape(seq_count * local_len, features)
    branch = matmul(attended, full_out) + to_float(bias_out)
    normed, unit_one, inverse_one = norm_forward(
        to_float(token_rows) + branch, to_float(gain_one), to_float(offset_one)
    )
    normed_low = normed.astype(jnp.bfloat16)
    pre_act = matmul(normed_low, full_up) + to_float(bias_up)
    activated, act_pullback = jax.vjp(smooth_act, pre_act)
    hidden = activated.astype(jnp.bfloat16)
    ffn_out = matmul(hidden, full_down) + to_float(bias_down)
    output_rows, unit_two, inverse_two = norm_forward(
        normed + ffn_out, to_float(gain_two), to_float(offset_two)
    )
    layer_out = output_rows.astype(jnp.bfloat16).reshape(seq_count, local_len, features)
    valid_rows = key_mask.astype(jnp.float32)
    input_squares = jnp.sum(jnp.square(to_float(inputs)), axis=2)
    branch_squares = jnp.sum(jnp.square(branch), axis=1).reshape(seq_count, local_len)
    ffn_squares = jnp.sum(jnp.square(ffn_out), axis=1).reshape(seq_count, local_len)
    squares = jnp.stack(
        [
            jnp.sum(valid_rows * input_squares, axis=1),
            jnp.sum(valid_rows * branch_squares, axis=1),
            jnp.sum(valid_rows * ffn_squares, axis=1),
        ],
        axis=1,
    )
    squares = lax.psum(squares, "ctx")
    stream_rms = jnp.sqrt(squares / (lengths.astype(jnp.float32)[:, None] * features))
    back_query, back_key, back_value, back_out, back_up, back_down, back_gain_one, back_gain_two = (
        lax.all_gather(w_query, "shard", axis=0, tiled=True),
        lax.all_gather(w_key, "shard", axis=0, tiled=True),
        lax.all_gather(w_value, "shard", axis=0, tiled=True),
        lax.all_gather(w_out, "shard", axis=0, tiled=True),
        lax.all_gather(w_up, "shard", axis=0, tiled=True),
        lax.all_gather(w_down, "shard", axis=0, tiled=True),
        lax.all_gather(first_gain, "shard", axis=0, tiled=True),
        lax.all_gather(second_gain, "shard", axis=0, tiled=True),
    )
    cotangent = to_float(out_grad).reshape(seq_count * local_len, features)
    grad_two, grad_gain_two, grad_offset_two = norm_backward(
        cotangent, unit_two, inverse_two, to_float(back_gain_two)
    )
    grad_ffn = grad_two.astype(jnp.bfloat16)
    grad_bias_down = jnp.sum(grad_ffn, axis=0, dtype=jnp.float32)
    grad_full_down = outer_sum(hidden, grad_ffn)
    grad_hidden = back_product(grad_ffn, back_down)
    grad_pre = act_pullback(grad_hidden)[0].astype(jnp.bfloat16)
    grad_bias_up = jnp.sum(grad_pre, axis=0, dtype=jnp.float32)
    grad_full_up = outer_sum(normed_low, grad_pre)
    grad_normed = grad_two + back_product(grad_pre, back_up)
    grad_one, grad_gain_one, grad_offset_one = norm_backward(
        grad_normed, unit_one, inverse_one, to_float(back_gain_one)
    )
    grad_branch = grad_one.astype(jnp.bfloat16)
    grad_bias_out = jnp.sum(grad_branch, axis=0, dtype=jnp.float32)
    grad_full_out = outer_sum(attended, grad_branch)
    grad_att = (
        back_product(grad_branch, back_out)
        .astype(jnp.bfloat16)
        .reshape(seq_count, local_len, features)
    )
    row_delta = jnp.sum(
        (to_float(grad_att) * attended_full).reshape(seq_count, local_len, HEADS, HEAD_DIM), axis=-1
    )
    log_all, delta_all = (
        lax.all_gather(log_total, "ctx", axis=1, tiled=True),
        lax.all_gather(row_delta, "ctx", axis=1, tiled=True),
    )
    grad_heads = split_heads(grad_att)
    mem_probs = jnp.exp(head_scores(query_heads, mem_key_heads) - log_total[..., None])
    mem_dots = jnp.einsum(
        "sqhd,skhd->sqhk", grad_heads, mem_value_heads, preferred_element_type=jnp.float32
    )
    mem_dscores = (mem_probs * (mem_dots - row_delta[..., None])).astype(jnp.bfloat16)
    start_query = jnp.einsum(
        "sqhk,skhd->sqhd", mem_dscores, mem_key_heads, preferred_element_type=jnp.float32
    ) * HEAD_DIM ** (-0.5)
    mem_grad_key = jnp.einsum(
        "sqhk,sqhd->skhd", mem_dscores, query_heads, preferred_element_type=jnp.float32
    ) * HEAD_DIM ** (-0.5)
    mem_grad_value = jnp.einsum(
        "sqhk,sqhd->skhd",
        mem_probs.astype(jnp.bfloat16),
        grad_heads,
        preferred_element_type=jnp.float32,
    )
    key_heads = split_heads(key)
    value_heads = split_heads(value)
    empty_grads = jnp.zeros(key_heads.shape, jnp.float32)

    def query_step(carried, pieces, first_row):
        return query_update(
            carried, pieces, first_row, query_heads, grad_heads, log_total, row_delta, lengths
        )

    def key_step(carried, pieces, first_row):
        return key_update(
            carried, pieces, first_row, key_heads, value_heads, log_all, delta_all, key_mask
        )

    grad_q = in_blocks(
        query_step,
        start_query,
        (
            lax.all_gather(key, "ctx", axis=1, tiled=True),
            lax.all_gather(value, "ctx", axis=1, tiled=True),
        ),
        jnp.int32(0),
        1,
    )
    grad_k, grad_v = in_blocks(
        key_step,
        (empty_grads, empty_grads),
        (
            lax.all_gather(query, "ctx", axis=1, tiled=True),
            lax.all_gather(grad_att, "ctx", axis=1, tiled=True),
        ),
        jnp.int32(0),
        1,
    )
    mem_key_sum, mem_value_sum = lax.psum((mem_grad_key, mem_grad_value), "ctx")
    mem_key_low = mem_key_sum.reshape(seq_count * mem_rows, features).astype(jnp.bfloat16)
    mem_value_low = mem_value_sum.reshape(seq_count * mem_rows, features).astype(jnp.bfloat16)
    first_only = (lax.axis_index("ctx") == 0).astype(jnp.float32)
    grad_q_low = grad_q.reshape(seq_count * local_len, features).astype(jnp.bfloat16)
    grad_k_low = grad_k.reshape(seq_count * local_len, features).astype(jnp.bfloat16)
    grad_v_low = grad_v.reshape(seq_count * local_len, features).astype(jnp.bfloat16)
    grad_full_query = outer_sum(token_rows, grad_q_low)
    grad_full_key = outer_sum(token_rows, grad_k_low) + first_only * outer_sum(
        mem_flat, mem_key_low
    )
    grad_full_value = outer_sum(token_rows, grad_v_low) + first_only * outer_sum(
        mem_flat, mem_value_low
    )
    grad_bias_query = jnp.sum(grad_q_low, axis=0, dtype=jnp.float32)
    grad_bias_value = jnp.sum(grad_v_low, axis=0, dtype=jnp.float32) + first_only * jnp.sum(
        mem_value_low, axis=0, dtype=jnp.float32
    )
    input_grad = (
        grad_one
        + back_product(grad_q_low, back_query)
        + back_product(grad_k_low, back_key)
        + back_product(grad_v_low, back_value)
    ).reshape(seq_count, local_len, features)
    memory_grad = (
        back_product(mem_key_low, back_key) + back_product(mem_value_low, back_value)
    ).reshape(seq_count, mem_rows, features)
    owned_parts = (
        lax.psum_scatter(
            grad_full_query.astype(jnp.bfloat16), "shard", scatter_dimension=0, tiled=True
        ).astype(jnp.float32),
        lax.psum_scatter(
            grad_full_key.astype(jnp.bfloat16), "shard", scatter_dimension=0, tiled=True
        ).astype(jnp.float32),
        lax.psum_scatter(
            grad_full_value.astype(jnp.bfloat16), "shard", scatter_dimension=0, tiled=True
        ).astype(jnp.float32),
        lax.psum_scatter(
            grad_full_out.astype(jnp.bfloat16), "shard", scatter_dimension=0, tiled=True
        ).astype(jnp.float32),
        lax.psum_scatter(
            grad_full_up.astype(jnp.bfloat16), "shard", scatter_dimension=0, tiled=True
        ).astype(jnp.float32),
        lax.psum_scatter(
            grad_full_down.astype(jnp.bfloat16), "shard", scatter_dimension=0, tiled=True
        ).astype(jnp.float32),
        lax.psum_scatter(
            grad_bias_query.astype(jnp.bfloat16), "shard", scatter_dimension=0, tiled=True
        ).astype(jnp.float32),
        lax.psum_scatter(
            grad_bias_value.astype(jnp.bfloat16), "shard", scatter_dimension=0, tiled=True
        ).astype(jnp.float32),
        lax.psum_scatter(
            grad_bias_out.astype(jnp.bfloat16), "shard", scatter_dimension=0, tiled=True
        ).astype(jnp.float32),
        lax.psum_scatter(
            grad_bias_up.astype(jnp.bfloat16), "shard", scatter_dimension=0, tiled=True
        ).astype(jnp.float32),
        lax.psum_scatter(
            grad_bias_down.astype(jnp.bfloat16), "shard", scatter_dimension=0, tiled=True
        ).astype(jnp.float32),
        lax.psum_scatter(
            grad_gain_one.astype(jnp.bfloat16), "shard", scatter_dimension=0, tiled=True
        ).astype(jnp.float32),
        lax.psum_scatter(
            grad_offset_one.astype(jnp.bfloat16), "shard", scatter_dimension=0, tiled=True
        ).astype(jnp.float32),
        lax.psum_scatter(
            grad_gain_two.astype(jnp.bfloat16), "shard", scatter_dimension=0, tiled=True
        ).astype(jnp.float32),
        lax.psum_scatter(
            grad_offset_two.astype(jnp.bfloat16), "shard", scatter_dimension=0, tiled=True
        ).astype(jnp.float32),
    )
    (
        part_query,
        part_key,
        part_value,
        part_out,
        part_up,
        part_down,
        part_bias_query,
        part_bias_value,
        part_bias_out,
        part_bias_up,
        part_bias_down,
        part_gain_one,
        part_offset_one,
        part_gain_two,
        part_offset_two,
    ) = owned_parts
    summed_grads = lax.psum(
        (
            part_query,
            part_key,
            part_value,
            part_out,
            part_up,
            part_down,
            part_bias_query,
            part_bias_value,
            part_bias_out,
            part_bias_up,
            part_bias_down,
            part_gain_one,
            part_offset_one,
            part_gain_two,
            part_offset_two,
        ),
        "ctx",
    )
    (
        sum_query,
        sum_key,
        sum_value,
        sum_out,
        sum_up,
        sum_down,
        sum_bias_query,
        sum_bias_value,
        sum_bias_out,
        sum_bias_up,
        sum_bias_down,
        sum_gain_one,
        sum_offset_one,
        sum_gain_two,
        sum_offset_two,
    ) = summed_grads
    return (
        layer_out,
        input_grad,
        memory_grad,
        sum_query,
        sum_key,
        sum_value,
        sum_out,
        sum_up,
        sum_down,
        sum_bias_query,
        sum_bias_value,
        sum_bias_out,
        sum_bias_up,
        sum_bias_down,
        sum_gain_one,
        sum_offset_one,
        sum_gain_two,
        sum_offset_two,
        stream_rms,
    )


MESH_ID = pl.DeviceIdType.MESH
LANES = 128
MEM_PAD = 32
ROW_KINDS = 16
SENDS, ARRIVALS, KEPT = 18, 87, 23
PIECES = ((128, 'xyz'), (128, 'zyx'), (128, 'yxz'), (128, 'yxz'), (256, 'xyz'), (256, 'zyx'), (128, 'yzx'))


def flipped(index, offset, bits):
    total = 0
    for bit in range(bits):
        digit = lax.rem(lax.div(index, 2**bit), 2)
        if offset >> bit & 1:
            digit = 1 - digit
        total = total + digit * 2**bit
    return total


class Copies:
    def __init__(self, send_sems, recv_sems, local_sems, measure):
        self.send_sems, self.recv_sems, self.local_sems = send_sems, recv_sems, local_sems
        self.measure = measure
        self.sent, self.alone, self.received, self.kept = [], [], 0, 0

    def send(self, src, dst, device):
        return self.send_all([(src, dst, device)], dst)

    def send_all(self, items, whole):
        rows = math.prod(whole.shape) * whole.dtype.itemsize // (2 * self.measure.shape[1])
        if rows % 16:
            pool = len(self.sent)
            self.sent.append(None)
            self.alone.append((pool, whole))
        else:
            pool = next(
                (
                    number
                    for number, held in enumerate(self.sent)
                    if held is not None and held + rows <= self.measure.shape[0]
                ),
                len(self.sent),
            )
            if pool == len(self.sent):
                self.sent.append(0)
            self.sent[pool] += rows
        arrival = self.recv_sems.at[self.received]
        self.received += 1
        for src, dst, device in items:
            pltpu.make_async_remote_copy(
                src_ref=src,
                dst_ref=dst,
                send_sem=self.send_sems.at[pool],
                recv_sem=arrival,
                device_id=device,
                device_id_type=MESH_ID,
            ).start()
        return Arrival(whole, arrival)

    def keep(self, items, whole):
        done = self.local_sems.at[self.kept]
        self.kept += 1
        for src, dst in items:
            pltpu.make_async_copy(src, dst, done).start()
        return Arrival(whole, done)

    def finish(self):
        for pool, whole in self.alone:
            Arrival(whole, self.send_sems.at[pool]).wait()
        for pool, rows in enumerate(self.sent):
            if rows is not None:
                Arrival(self.measure.at[pl.ds(0, rows)], self.send_sems.at[pool]).wait()


class Held:
    pass


class Arrival:
    def __init__(self, whole, semaphore):
        self.whole, self.semaphore = whole, semaphore

    def wait(self):
        pltpu.make_async_copy(self.whole, self.whole, self.semaphore).wait()


def layer_kernel(
    x_ref,
    g_ref,
    mem_ref,
    len_ref,
    wq_ref,
    wk_ref,
    wv_ref,
    wo_ref,
    wu_ref,
    wd_ref,
    *refs,
):
    vec_refs, refs = refs[:9], refs[9:]
    (o_layer, o_input, o_mem, o_fin, o_heads, o_rms), refs = refs[:6], refs[6:]
    (
        own_in,
        own_g,
        own_mem,
        mem_in,
        *rest,
    ) = refs
    narrow_in, rest = rest[:8], rest[8:]
    (
        wide_in,
        rms_rows,
        d_branch,
        joined,
        out_rows,
        in_grad,
        tokens,
        tokens_t,
        w_heads,
        w_out,
        w_up,
        w_down,
        vecs,
        q_scaled,
        q_aug,
        k_aug,
        v_mask,
        k_turned,
        v_turned,
        probs,
        d_scores,
        mixed_t,
        inverse_total,
        d_scaled,
        d_scaled_t,
        mixed,
        att,
        hidden,
        act_slope,
        d_pre,
        d_att,
        d_mixed,
        partial,
        got_core,
        got_first,
        got_second,
        got_third,
        got_far,
        final,
        head_part,
        head_core,
        head_x,
        head_far,
        head_all,
        vec_part,
        dx_part,
        dx_got,
        dx_far,
        mem_part,
        mem_far,
        squares,
        send_sems,
        recv_sems,
        local_sems,
    ) = rest
    bf16, f32 = jnp.bfloat16, jnp.float32
    shard, ctx = lax.axis_index("shard"), lax.axis_index("ctx")
    span, width = x_ref.shape[1], x_ref.shape[2]
    spans = 8
    length_all = span * spans
    keys = length_all + MEM_PAD
    x_half, core = lax.div(shard, 2), lax.rem(shard, 2)
    upper, pair = lax.div(ctx, 4), lax.rem(ctx, 4)
    y_side = lax.rem(ctx, 2)
    z_side = lax.rem(lax.div(ctx, 2) + upper, 2)

    def shard_peer(offset):
        return {"shard": flipped(shard, offset, 2), "ctx": ctx}

    def ctx_peer(offset):
        return {"shard": shard, "ctx": flipped(ctx, offset, 3)}

    def span_rows(index):
        return pl.ds(pl.multiple_of(index * span, span), span)

    def pair_lanes(index, size=LANES):
        return pl.ds(pl.multiple_of(index * LANES, LANES), size)

    copies = Copies(send_sems, recv_sems, local_sems, partial.at[0])

    barrier = pltpu.get_barrier_semaphore()
    for offset in (1, 2, 3):
        pl.semaphore_signal(barrier, inc=1, device_id=shard_peer(offset), device_id_type=MESH_ID)
    for offset in range(1, 8):
        pl.semaphore_signal(barrier, inc=1, device_id=ctx_peer(offset), device_id_type=MESH_ID)

    def rows_of(ref, index, start=0, rows=None):
        owned = ref.shape[0] // 4
        return ref.at[pl.ds(pl.multiple_of(index * owned + start, LANES), rows or owned)]

    my_rows = pl.ds(pl.multiple_of(shard * LANES, LANES), LANES)
    head_refs = (wq_ref, wk_ref, wv_ref)
    own_blocks = [
        copies.keep(
            [
                (
                    ref.at[:, pair_lanes(pair)],
                    w_heads.at[my_rows, pl.ds(part * LANES, LANES)],
                )
                for part, ref in enumerate(head_refs)
            ],
            w_heads.at[my_rows],
        ),
        copies.keep([(x_ref.at[upper], tokens.at[span_rows(ctx)])], own_in.at[0]),
    ]
    narrow_copies = [
        copies.keep([(ref, copied)], copied)
        for ref, copied in zip(vec_refs, (*narrow_in, wide_in))
    ]
    full_weights = ((wo_ref, w_out), (wd_ref, w_down), (wu_ref, w_up))
    own_weights = [
        copies.keep([(ref, rows_of(full, shard)) for ref, full in full_weights], partial.at[0]),
        copies.keep([(x_ref, own_in)], own_in),
        copies.keep([(g_ref, own_g)], own_g),
        copies.keep([(mem_ref, mem_in)], mem_in),
    ]
    pl.semaphore_wait(barrier, 10)

    partner = flipped(ctx, 6, 3)
    half_span = span // 2

    def half_rows(index, half):
        return pl.ds(pl.multiple_of(index * span + half * half_span, half_span), half_span)

    far_tokens = [
        copies.send(
            x_ref.at[1 - upper, pl.ds(half * half_span, half_span)],
            tokens.at[half_rows(ctx, half)],
            ctx_peer(6),
        )
        for half in range(2)
    ]
    def near_send(offsets):
        return copies.send_all(
            [
                (x_ref.at[upper], tokens.at[span_rows(ctx)], ctx_peer(offset))
                for offset in offsets
            ],
            tokens.at[pl.ds(0, span * len(offsets))],
        )

    near_pair, near_y = near_send((3, 2)), near_send((1,))

    def send_head_rows(offset):
        return copies.send_all(
            [
                (
                    ref.at[:, pair_lanes(pair)],
                    w_heads.at[my_rows, pl.ds(part * LANES, LANES)],
                    shard_peer(offset),
                )
                for part, ref in enumerate(head_refs)
            ],
            w_heads.at[my_rows],
        )

    x_heads = send_head_rows(2)
    core_heads = send_head_rows(1)
    for copy in narrow_copies:
        copy.wait()
    for kind, ref in enumerate((*narrow_in, wide_in)):
        values = ref[...].astype(f32)
        for piece in range(ref.shape[0] // LANES):
            vecs[shard, kind + piece : kind + piece + 1, :] = values[
                piece * LANES : (piece + 1) * LANES
            ].reshape(1, LANES)
    vec_copies = copies.send_all(
        [(vecs.at[shard], vecs.at[shard], shard_peer(offset)) for offset in (2, 3, 1)],
        vecs.at[pl.ds(0, 3)],
    )
    half_down = wd_ref.shape[0] // 2
    x_out = copies.send(wo_ref, rows_of(w_out, shard), shard_peer(2))
    x_down = copies.send(
        wd_ref.at[pl.ds(pl.multiple_of(y_side * half_down, LANES), half_down)],
        rows_of(w_down, shard, y_side * half_down, half_down),
        shard_peer(2),
    )
    x_up = copies.send(wu_ref, rows_of(w_up, shard), shard_peer(2))
    core_weights = copies.send_all(
        [(ref, rows_of(full, shard), shard_peer(1)) for ref, full in full_weights], partial.at[0]
    )

    for copy in own_weights:
        copy.wait()
    own_mem[...] = jnp.zeros_like(own_mem)
    for seq in range(own_mem.shape[0]):
        own_mem[seq, :MEM_ROWS, :] = mem_in[:, seq, :]

    passed_pair, passed_y = [], []
    for half, copy in enumerate(far_tokens):
        copy.wait()
        place = tokens.at[half_rows(partner, half)]
        passed_pair.append(
            copies.send_all(
                [(place, place, ctx_peer(3)), (place, place, ctx_peer(2))], tokens.at[pl.ds(0, span)]
            )
        )
        passed_y.append(copies.send(place, place, ctx_peer(1)))
    x_heads.wait()
    x_owner = flipped(shard, 2, 2)
    place = rows_of(w_heads, x_owner)
    passed_heads = copies.send(place, place, shard_peer(1))
    x_out.wait()
    x_down.wait()
    place = rows_of(w_down, x_owner, y_side * half_down, half_down)
    y_down = copies.send(place, place, ctx_peer(1))
    passed_early = copies.send_all(
        [(part, part, shard_peer(1)) for part in (rows_of(w_out, x_owner), place)],
        partial.at[0, pl.ds(0, LANES + half_down)],
    )

    for copy in own_blocks:
        copy.wait()
    for copy in (core_heads, passed_heads, vec_copies):
        copy.wait()

    def full_vec(kind):
        return jnp.concatenate([vecs[owner, kind : kind + 1, :] for owner in range(4)], axis=1)

    length = len_ref[upper]
    lane = lax.broadcasted_iota(jnp.int32, (span * 2, LANES), 1)

    def put_query(rows, projected):
        scaled = (projected + vecs[pair, 0:1, :]).astype(bf16).astype(f32) * (HEAD_DIM**-0.5)
        q_scaled[rows, :] = scaled.astype(bf16)
        q_aug[0, rows, :] = jnp.where(
            lane < HEAD_DIM, scaled, jnp.where(lane == HEAD_DIM, 1.0, 0.0)
        ).astype(bf16)
        q_aug[1, rows, :] = jnp.where(
            lane >= HEAD_DIM, scaled, jnp.where(lane == 0, 1.0, 0.0)
        ).astype(bf16)

    def put_key_value(rows, key, value, left_out):
        lanes = lax.broadcasted_iota(jnp.int32, key.shape, 1)
        key = key.astype(bf16).astype(f32)
        value = (value + vecs[pair, 1:2, :]).astype(bf16).astype(f32)
        k_aug[0, rows, :] = jnp.where(
            lanes < HEAD_DIM, key, jnp.where(lanes == HEAD_DIM, left_out, 0.0)
        ).astype(bf16)
        k_aug[1, rows, :] = jnp.where(
            lanes >= HEAD_DIM, key, jnp.where(lanes == 0, left_out, 0.0)
        ).astype(bf16)
        v_mask[0, rows, :] = jnp.where(lanes < HEAD_DIM, value, 0.0).astype(bf16)
        v_mask[1, rows, :] = jnp.where(lanes >= HEAD_DIM, value, 0.0).astype(bf16)
        k_turned[:, rows] = key.T.astype(bf16)
        v_turned[:, rows] = value.T.astype(bf16)

    def block_rows(high):
        block = lax.div(flipped(ctx, 2 * high, 3), 2)
        return block, pl.ds(pl.multiple_of(block * span * 2, span * 2), span * 2)

    arrivals = ([near_y], [near_pair], passed_pair, passed_y)
    for high in (0, 1, 3, 2):
        for copy in arrivals[high]:
            copy.wait()
        block, rows = block_rows(high)
        projected = matmul(tokens[rows, :], w_heads[...])
        put_query(rows, projected[:, :LANES])
        position = block * span * 2 + lax.broadcasted_iota(jnp.int32, (span * 2, LANES), 0)
        put_key_value(
            rows,
            projected[:, LANES : 2 * LANES],
            projected[:, 2 * LANES :],
            jnp.where(position < length, 0.0, -1e30),
        )
    projected = matmul(own_mem[upper], w_heads[:, LANES:])
    position = lax.broadcasted_iota(jnp.int32, (MEM_PAD, LANES), 0)
    put_key_value(
        pl.ds(length_all, MEM_PAD),
        projected[:, :LANES],
        projected[:, LANES:],
        jnp.where(position < MEM_ROWS, 0.0, -1e30),
    )

    att_copies = []
    for high in (3, 2, 1, 0):
        _, rows = block_rows(high)
        for head in range(2):
            scores = back_product(k_aug[head], q_aug[head, rows, :])
            exponent = jnp.exp(scores - jnp.max(scores, axis=0, keepdims=True))
            total = jnp.sum(exponent, axis=0, keepdims=True)
            inverse = 1.0 / total
            inverse_total[head : head + 1, rows] = inverse
            weights = exponent.astype(bf16)
            probs[head, :, rows] = weights
            half = pl.ds(head * HEAD_DIM, HEAD_DIM)
            mixed_t[half, rows] = matmul(v_turned[half, :], weights) * inverse
        mixed[rows, :] = mixed_t[:, rows].T.astype(bf16)
        att_items = []
        for low in (0, 1):
            offset = 2 * high + low
            source = mixed.at[span_rows(flipped(ctx, offset, 3))]
            target = att.at[span_rows(upper), pair_lanes(pair)]
            if offset:
                att_items.append((source, target, ctx_peer(offset)))
            else:
                own_att = copies.keep([(source, target)], source)

        att_copies.append(copies.send_all(att_items, mixed.at[pl.ds(0, span * len(att_items))]))

    y_down.wait()
    x_up.wait()
    places = (
        rows_of(w_up, x_owner),
        rows_of(w_down, x_owner, (1 - y_side) * half_down, half_down),
    )
    passed_weights = copies.send_all(
        [(place, place, shard_peer(1)) for place in places],
        partial.at[0, pl.ds(0, half_down + width)],
    )
    for block in range(4):
        rows = pl.ds(block * span * 2, span * 2)
        tokens_t[:, rows] = tokens[rows, :].astype(f32).T.astype(bf16)
    core_weights.wait()
    passed_early.wait()
    passed_weights.wait()
    own_att.wait()
    for copy in att_copies:
        copy.wait()

    seqs = own_in.shape[0]
    local_rows = seqs * span
    own_x = own_in[...].reshape(local_rows, width).astype(f32)
    branch = matmul(att[...], w_out[...]) + full_vec(2)
    normed, unit_one, inverse_one = norm_forward(own_x + branch, full_vec(4), full_vec(5))
    normed_low = normed.astype(bf16)
    ffn_out = jnp.zeros((local_rows, width), f32)
    for chunk in range(4):
        columns = pl.ds(chunk * width, width)
        bias = jnp.concatenate([vecs[chunk, 8 + i : 9 + i, :] for i in range(4)], axis=1)
        pre_act = matmul(normed_low, w_up[:, columns]) + bias
        square = pre_act * pre_act
        bent = jnp.tanh(GELU_SCALE * pre_act * (1.0 + 0.044715 * square))
        hidden[:, columns] = (0.5 * pre_act * (1.0 + bent)).astype(bf16)
        act_slope[:, columns] = 0.5 * (1.0 + bent) + 0.5 * pre_act * (1.0 - bent * bent) * (
            GELU_SCALE * (1.0 + 3 * 0.044715 * square)
        )
        ffn_out = ffn_out + matmul(hidden[:, columns], w_down[columns, :])
    ffn_out = ffn_out + full_vec(3)
    output, unit_two, inverse_two = norm_forward(normed + ffn_out, full_vec(6), full_vec(7))
    out_rows[...] = output.astype(bf16)

    chunks = []
    first_row = 0
    for rows, order in PIECES:
        chunks.append((first_row, rows, order))
        first_row += rows
    sides = {"x": x_half, "y": y_side, "z": z_side}
    peers = {"x": shard_peer(2), "y": ctx_peer(1), "z": ctx_peer(2)}
    waits = {}
    out_copies = [copies.keep([(out_rows, o_layer)], out_rows)]
    final_items, input_items = [], []

    def arrived(key):
        waits.pop(key).wait()

    def add_rows(target, first):
        target[...] = (target[...].astype(f32) + first[...].astype(f32)).astype(bf16)

    def aligned(start, rows):
        return pl.ds(pl.multiple_of(start, rows), rows)

    def core_send(number):
        start, rows, _ = chunks[number]
        waits["core", number] = copies.send_all(
            [
                (
                    partial.at[2 * side + 1 - core, pl.ds(start, rows)],
                    got_core.at[side, pl.ds(start, rows)],
                    shard_peer(1),
                )
                for side in range(2)
            ],
            partial.at[0, pl.ds(0, 2 * rows)],
        )

    def slabs(number, step):
        start, rows, order = chunks[number]
        if step == 0:
            return [got_core.at[side, pl.ds(start, rows)] for side in range(2)]
        buffer = (got_first, got_second, got_third)[step - 1]
        size = rows >> (step - 1)
        first = start >> (step - 1)
        if "x" in order[:step]:
            return [buffer.at[pl.ds(first, size)]]
        return [buffer.at[pl.ds(first + side * (size // 2), size // 2)] for side in range(2)]

    def split(number, step):
        whole = slabs(number, step)
        axis = chunks[number][2][step]
        side = sides[axis]
        if axis == "x":
            start, rows, _ = chunks[number]
            if step == 0:
                return (
                    [got_core.at[side, pl.ds(start, rows)]],
                    [got_core.at[1 - side, pl.ds(start, rows)]],
                )
            buffer = (got_first, got_second, got_third)[step - 1]
            size, first = rows >> step, start >> (step - 1)
            return (
                [buffer.at[aligned(first + side * size, size)]],
                [buffer.at[aligned(first + (1 - side) * size, size)]],
            )
        half = whole[0].shape[0] // 2
        return (
            [slab.at[aligned(side * half, half)] for slab in whole],
            [slab.at[aligned((1 - side) * half, half)] for slab in whole],
        )

    def halve(number, step):
        if step == 0:
            arrived(("core", number))
            for side, slab in enumerate(slabs(number, 0)):
                start, rows, _ = chunks[number]
                add_rows(slab, partial.at[2 * side + core, pl.ds(start, rows)])
        else:
            join(number, step)
        axis = chunks[number][2][step]
        _, gone = split(number, step)
        start, rows, _ = chunks[number]
        waits[step, number] = copies.send_all(
            [(slab, target, peers[axis]) for slab, target in zip(gone, slabs(number, step + 1))],
            (got_first, got_second, got_third)[step].at[pl.ds(start >> step, rows >> step)],
        )

    def join(number, step):
        arrived((step - 1, number))
        kept, _ = split(number, step - 1)
        for target, slab in zip(slabs(number, step), kept):
            add_rows(target, slab)

    def cross(number):
        join(number, 3)
        start, rows, _ = chunks[number]
        here = pl.ds(start // 4, rows // 4)
        waits["cross", number] = copies.send(got_third.at[here], got_far.at[here], ctx_peer(6))

    def place_of(number, count):
        start, rows, order = chunks[number]
        for axis in order.replace("x", "")[: 2 - count]:
            rows = rows // 2
            start = start + sides[axis] * rows
        return aligned(start, rows)

    def gather(number, count):
        start, rows, order = chunks[number]
        if count == 0:
            arrived(("cross", number))
            here = pl.ds(start // 4, rows // 4)
            final[place_of(number, 0), :] = (
                got_third[here, :].astype(f32) + got_far[here, :].astype(f32)
            ).astype(bf16)
        else:
            arrived(("gather", number))
        place = final.at[place_of(number, count)]
        waits["gather", number] = copies.send(
            place, place, peers[order.replace("x", "")[1 - count]]
        )

    def write_out(number):
        start, rows, _ = chunks[number]
        arrived(("gather", number))
        place = pl.ds(start, rows)
        final_items.append((final.at[place], o_fin.at[place]))
        if len(final_items) == len(chunks):
            out_copies.append(copies.keep(final_items, final))

    def outer_part(number):
        start, rows, _ = chunks[number]
        done = 0
        while done < rows:
            row = start + done
            if row < width:
                size = min(rows - done, width - row)
                for owner in range(4):
                    columns = slice(owner * width + row, owner * width + row + size)
                    partial[owner, row : row + size, :] = outer_sum(
                        hidden[:, columns], held.d_ffn
                    ).astype(bf16)
            else:
                size = LANES
                if row < 2 * width:
                    chunk = (row - width) // LANES
                    grad = outer_sum(
                        held.normed, d_pre[:, chunk * width : (chunk + 1) * width]
                    ).astype(bf16)
                else:
                    grad = outer_sum(att[...], d_branch[...]).astype(bf16)
                for owner in range(4):
                    partial[owner, row : row + size, :] = grad[owner * LANES : (owner + 1) * LANES]
            done += size
        core_send(number)

    held = Held()
    held.normed = normed_low


    def second_norm():
        cotangent = own_g[...].reshape(local_rows, width).astype(f32)
        held.two, held.second_gain, held.second_bias = norm_backward(
            cotangent, unit_two, inverse_two, full_vec(6)
        )
        held.d_ffn = held.two.astype(bf16)

    def first_norm():
        d_normed = held.two
        for chunk in range(4):
            columns = pl.ds(chunk * width, width)
            d_hidden = back_product(held.d_ffn, w_down[columns, :])
            d_chunk = (d_hidden * act_slope[:, columns]).astype(bf16)
            d_pre[:, columns] = d_chunk
            d_normed = d_normed + back_product(d_chunk, w_up[:, columns])
        d_one, held.first_gain, held.first_bias = norm_backward(
            d_normed, unit_one, inverse_one, full_vec(4)
        )
        in_grad[...] = d_one
        d_branch[...] = d_one.astype(bf16)

    def attended_grad():
        held.d_att = []
        for rows_of_seq, offsets in ((1 - upper, (6, 7, 4, 5)), (upper, (2, 3, 1, 0))):
            rows = span_rows(rows_of_seq)
            d_att[rows, :] = back_product(d_branch[rows, :], w_out[...]).astype(bf16)
            items = []
            for offset in offsets:
                peer = flipped(ctx, offset, 3)
                source = d_att.at[rows, pair_lanes(lax.rem(peer, 4))]
                target = d_mixed.at[span_rows(ctx)]
                if offset:
                    items.append((source, target, ctx_peer(offset)))
                else:
                    held.own_d_att = copies.keep([(source, target)], target)
            held.d_att.append(copies.send_all(items, d_mixed.at[pl.ds(0, span * len(items))]))

    def square_sums():
        row_id = lax.broadcasted_iota(jnp.int32, (8, LANES), 0)
        tile = jnp.zeros((8, LANES), f32)
        for seq in range(seqs):
            position = ctx * span + lax.broadcasted_iota(jnp.int32, (span, 1), 0)
            valid = jnp.where(position < len_ref[seq], 1.0, 0.0)
            for kind, values in enumerate((own_x, branch, ffn_out)):
                piece = values[seq * span : (seq + 1) * span]
                row_sum = jnp.sum(piece * piece, axis=1, keepdims=True) * valid
                tile = tile + jnp.where(
                    row_id == seq * 3 + kind, jnp.sum(row_sum, axis=0, keepdims=True), 0.0
                )
        squares[ctx] = tile
        held.squares = copies.send_all(
            [
                (squares.at[ctx], squares.at[ctx], ctx_peer(offset))
                for offset in (6, 7, 4, 5, 2, 3, 1)
            ],
            squares.at[pl.ds(0, 7)],
        )

    def narrow_grads():
        vec_part[...] = jnp.zeros_like(vec_part)
        wide_grads = (
            jnp.sum(d_branch[...].astype(f32), axis=0, keepdims=True),
            jnp.sum(held.d_ffn.astype(f32), axis=0, keepdims=True),
            held.first_gain,
            held.first_bias,
            held.second_gain,
            held.second_bias,
        )
        for owner in range(4):
            for kind, values in enumerate(wide_grads):
                vec_part[owner, 2 + kind : 3 + kind, :] = values.reshape(1, width)[
                    :, owner * LANES : (owner + 1) * LANES
                ]
            columns = pl.ds(owner * width, width)
            bias = jnp.sum(d_pre[:, columns].astype(f32), axis=0, keepdims=True)
            for part in range(4):
                vec_part[owner, 8 + part : 9 + part, :] = bias[
                    :, part * LANES : (part + 1) * LANES
                ]

    def deltas():
        held.own_d_att.wait()
        for copy in held.d_att:
            copy.wait()
        turned = d_mixed[...].astype(f32).T
        products = turned * mixed_t[...]
        held.deltas = []
        for head in range(2):
            half = slice(head * HEAD_DIM, (head + 1) * HEAD_DIM)
            inverse = inverse_total[head : head + 1, :]
            held.deltas.append(jnp.sum(products[half], axis=0, keepdims=True) * inverse)
            d_scaled_t[half, :] = (turned[half] * inverse).astype(bf16)
        d_scaled[...] = d_scaled_t[...].astype(f32).T.astype(bf16)

    def score_grads(head):
        delta = held.deltas[head]
        for block in range(4):
            rows = slice(block * span * 2, (block + 1) * span * 2)
            dots = matmul(v_mask[head], d_scaled_t[:, rows])
            weights = probs[head, :, rows].astype(f32)
            d_scores[head, :, rows] = (weights * (dots - delta[:, rows])).astype(bf16)

    def scores_0():
        score_grads(0)

    def scores_1():
        score_grads(1)

    def key_value_grads():
        key_lane = lax.broadcasted_iota(jnp.int32, (keys, LANES), 1)
        grad_value = jnp.where(
            key_lane < HEAD_DIM, matmul(probs[0], d_scaled[...]), matmul(probs[1], d_scaled[...])
        ).astype(bf16)
        grad_key = jnp.where(
            key_lane < HEAD_DIM,
            matmul(d_scores[0], q_scaled[...]),
            matmul(d_scores[1], q_scaled[...]),
        ).astype(bf16)
        joined[:, LANES : 2 * LANES] = grad_key[:length_all]
        joined[:, 2 * LANES :] = grad_value[:length_all]
        held.memory = jnp.concatenate([grad_key[length_all:], grad_value[length_all:]], axis=1)
        held.value = jnp.sum(grad_value.astype(f32), axis=0, keepdims=True)

    def query_grads():
        grad_query = jnp.concatenate(
            [
                matmul(k_turned[:HEAD_DIM, :], d_scores[0]),
                matmul(k_turned[HEAD_DIM:, :], d_scores[1]),
            ],
            axis=0,
        ) * (HEAD_DIM**-0.5)
        grad_query = grad_query.T.astype(bf16)
        joined[:, :LANES] = grad_query
        held.query = jnp.sum(grad_query.astype(f32), axis=0, keepdims=True)

    def input_part(mirror, order):
        for place, offset in enumerate(order):
            rows = span_rows(flipped(ctx, offset ^ mirror, 3))
            dx_part[
                4 * (mirror == 0) + place
            ] = back_product(joined[rows, :], w_heads[...]).astype(bf16)

    def two(ref, first):
        return ref.at[pl.ds(first, 2)]

    def input_far():
        input_part(6, (0, 2, 1, 3))
        held.far_y = copies.send(two(dx_part, 2), two(dx_got, 0), ctx_peer(1))

    def input_near():
        input_part(0, (0, 2, 1, 3))
        held.near_y = copies.send(two(dx_part, 6), two(dx_got, 2), ctx_peer(1))

    def input_far_z():
        held.far_y.wait()
        add_rows(two(dx_part, 0), two(dx_got, 0))
        held.far_z = copies.send(dx_part.at[1], dx_got.at[4], ctx_peer(2))

    def input_near_z():
        held.near_y.wait()
        add_rows(two(dx_part, 4), two(dx_got, 2))
        held.near_z = copies.send(dx_part.at[5], dx_got.at[5], ctx_peer(2))

    def input_cross():
        held.far_z.wait()
        add_rows(dx_got.at[4], dx_part.at[0])
        held.cross = copies.send(dx_got.at[4], dx_far, ctx_peer(6))

    def write_input_rows(index, parts):
        rows = span_rows(index)
        total = in_grad[rows, :]
        for part in parts:
            total = total + part.astype(f32)
        in_grad[rows, :] = total
        input_items.append((in_grad.at[rows], o_input.at[rows]))
        if len(input_items) == 2:
            out_copies.append(copies.keep(input_items, in_grad))

    def input_near_out():
        held.near_z.wait()
        write_input_rows(upper, (dx_part[4], dx_got[5]))

    def input_far_out():
        held.cross.wait()
        write_input_rows(1 - upper, (dx_far[...],))

    def memory_part():
        mem_part[pair] = back_product(held.memory, w_heads[:, LANES:]).astype(bf16)
        held.mem = copies.send_all(
            [(mem_part.at[pair], mem_part.at[pair], ctx_peer(offset)) for offset in (3, 2, 1)],
            mem_part.at[pl.ds(0, 3)],
        )

    def memory_cross():
        held.mem.wait()
        mem_far[upper] = (
            mem_part[0].astype(f32)
            + mem_part[1].astype(f32)
            + mem_part[2].astype(f32)
            + mem_part[3].astype(f32)
        ).astype(bf16)
        held.mem_far = copies.send(mem_far.at[upper], mem_far.at[upper], ctx_peer(6))

    def memory_out():
        held.mem_far.wait()
        out_copies.append(copies.keep([(mem_far, o_mem)], mem_far))

    def head_grads():
        grad_heads = matmul(tokens_t[...], joined[...])
        mem_grad = outer_sum(own_mem[upper], held.memory)
        for owner in range(4):
            rows = slice(owner * LANES, (owner + 1) * LANES)
            head_part[owner, :LANES, :LANES] = grad_heads[rows, :LANES].astype(bf16)
            head_part[owner, :LANES, LANES:] = (grad_heads[rows, LANES:] + mem_grad[rows]).astype(
                bf16
            )
            mine = pair == owner
            vec_part[owner, 0:1, :] = jnp.where(mine, held.query, 0.0)
            vec_part[owner, 1:2, :] = jnp.where(mine, held.value, 0.0)
            head_part[owner, LANES:, :] = jnp.zeros((ROW_KINDS, 3 * LANES), bf16)
            head_part[owner, LANES:, :LANES] = vec_part[owner].astype(bf16)
        held.head_core = copies.send_all(
            [
                (head_part.at[2 * side + 1 - core], head_core.at[side], shard_peer(1))
                for side in range(2)
            ],
            head_core,
        )

    def head_x_send():
        held.head_core.wait()
        for side in range(2):
            add_rows(head_core.at[side], head_part.at[2 * side + core])
        held.head_x = copies.send(head_core.at[1 - x_half], head_x, shard_peer(2))

    def head_far_send():
        held.head_x.wait()
        add_rows(head_x, head_core.at[x_half])
        held.head_far = copies.send(head_x, head_far, ctx_peer(4))

    def head_gather():
        held.head_far.wait()
        head_all[pair] = (head_x[...].astype(f32) + head_far[...].astype(f32)).astype(bf16)
        held.heads = copies.send(head_all.at[pair], head_all.at[pair], ctx_peer(2))

    def head_spread():
        held.heads.wait()
        places = [head_all.at[index] for index in (pair, flipped(pair, 2, 2))]
        held.heads = copies.send_all(
            [(place, place, ctx_peer(1)) for place in places], head_all.at[pl.ds(0, 2)]
        )

    def head_out():
        held.heads.wait()
        out_copies.append(copies.keep([(head_all, o_heads)], head_all))

    def rms_out():
        held.squares.wait()
        row_id = lax.broadcasted_iota(jnp.int32, (8, LANES), 0)
        total = squares[0]
        for other in range(1, spans):
            total = total + squares[other]
        valid_tokens = jnp.where(row_id < 3, len_ref[0], len_ref[1]).astype(f32)
        rms_rows[...] = jnp.sqrt(total / (valid_tokens * width))
        out_copies.append(copies.keep([(rms_rows, o_rms)], rms_rows))

    second_norm()
    outer_part(0)
    outer_part(1)
    outer_part(2)
    outer_part(3)
    first_norm()
    attended_grad()
    outer_part(4)
    outer_part(5)
    outer_part(6)
    square_sums()
    narrow_grads()
    halve(0, 0)
    halve(1, 0)
    halve(2, 0)
    halve(3, 0)
    halve(4, 0)
    halve(5, 0)
    halve(0, 1)
    halve(6, 0)
    halve(2, 1)
    deltas()
    scores_0()
    halve(1, 1)
    scores_1()
    halve(3, 1)
    key_value_grads()
    halve(0, 2)
    halve(4, 1)
    query_grads()
    halve(2, 2)
    input_far()
    halve(3, 2)
    halve(5, 1)
    halve(6, 1)
    input_near()
    memory_part()
    cross(0)
    head_grads()
    halve(1, 2)
    cross(2)
    cross(3)
    halve(6, 2)
    halve(4, 2)
    gather(0, 0)
    head_x_send()
    cross(1)
    cross(6)
    gather(2, 0)
    gather(3, 0)
    cross(4)
    gather(0, 1)
    gather(1, 0)
    head_far_send()
    input_far_z()
    gather(6, 0)
    gather(2, 1)
    gather(3, 1)
    halve(5, 2)
    gather(4, 0)
    cross(5)
    input_cross()
    head_gather()
    input_near_z()
    gather(6, 1)
    memory_cross()
    gather(4, 1)
    write_out(0)
    gather(1, 1)
    gather(5, 0)
    write_out(2)
    write_out(3)
    write_out(6)
    input_far_out()
    head_spread()
    write_out(4)
    gather(5, 1)
    input_near_out()
    memory_out()
    rms_out()
    write_out(1)
    head_out()
    write_out(5)
    for copy in out_copies:
        copy.wait()
    copies.finish()
    assert (len(copies.sent), copies.received, copies.kept) == (SENDS, ARRIVALS, KEPT)


def outputs_kernel(layer, input_grad, mem_grad, weights, heads, rms, *outs):
    f32 = jnp.float32
    (
        o_layer,
        o_input,
        o_mem,
        o_query,
        o_key,
        o_value,
        o_out,
        o_up,
        o_down,
        o_b_query,
        o_b_value,
        o_b_out,
        o_b_up,
        o_b_down,
        o_first_gain,
        o_first_bias,
        o_second_gain,
        o_second_bias,
        o_rms,
    ) = outs
    width = weights.shape[1]
    o_layer[...] = layer[...].reshape(o_layer.shape)
    o_input[...] = input_grad[...].reshape(o_input.shape)
    for seq in range(o_mem.shape[1]):
        o_mem[:, seq, :] = mem_grad[seq].astype(f32)[:MEM_ROWS]
    o_down[...] = weights[:width, :].astype(f32)
    for chunk in range(4):
        o_up[:, chunk * width : (chunk + 1) * width] = weights[
            width + chunk * LANES : width + (chunk + 1) * LANES, :
        ].astype(f32)
    o_out[...] = weights[2 * width :, :].astype(f32)
    for owner in range(4):
        for part, ref in enumerate((o_query, o_key, o_value)):
            ref[:, owner * LANES : (owner + 1) * LANES] = heads[
                owner, :LANES, part * LANES : (part + 1) * LANES
            ].astype(f32)
    vec = (
        heads[0, LANES:, :LANES].astype(f32)
        + heads[1, LANES:, :LANES].astype(f32)
        + heads[2, LANES:, :LANES].astype(f32)
        + heads[3, LANES:, :LANES].astype(f32)
    )
    narrow = (
        o_b_query,
        o_b_value,
        o_b_out,
        o_b_down,
        o_first_gain,
        o_first_bias,
        o_second_gain,
        o_second_bias,
    )
    for kind, ref in enumerate(narrow):
        ref[...] = vec[kind]
    for piece in range(4):
        o_b_up[piece * LANES : (piece + 1) * LANES] = vec[8 + piece]
    for seq in range(o_rms.shape[0]):
        for kind in range(3):
            o_rms[seq : seq + 1, kind : kind + 1] = rms[seq * 3 + kind : seq * 3 + kind + 1, :1]


def fast_layer(
    inputs,
    memory,
    lengths,
    w_query,
    w_key,
    w_value,
    w_out,
    w_up,
    w_down,
    b_query,
    b_value,
    b_out,
    b_up,
    b_down,
    first_gain,
    first_bias,
    second_gain,
    second_bias,
    out_grad,
):
    bf16, f32 = jnp.bfloat16, jnp.float32
    seqs, span, width = inputs.shape
    length_all, keys = 8 * span, 8 * span + MEM_PAD
    hidden_width = w_up.shape[1]
    narrow = (b_query, b_value, b_out, b_down, first_gain, first_bias, second_gain, second_bias)
    vmem, anywhere = pl.BlockSpec(memory_space=pltpu.VMEM), pl.BlockSpec(memory_space=pl.ANY)
    smem = pl.BlockSpec(memory_space=pltpu.SMEM)
    stacked = 2 * width + LANES
    scratch = [
        ((seqs, span, width), bf16),
        ((seqs, span, width), bf16),
        ((seqs, MEM_PAD, width), bf16),
        ((memory.shape[1], seqs, width), bf16),
        *[(ref.shape, bf16) for ref in (*narrow, b_up)],
        ((8, LANES), f32),
        ((seqs * span, width), bf16),
        ((length_all, 3 * LANES), bf16),
        ((seqs * span, width), bf16),
        ((seqs * span, width), f32),
        ((length_all, width), bf16),
        ((width, length_all), bf16),
        ((width, 3 * LANES), bf16),
        ((width, width), bf16),
        ((width, hidden_width), bf16),
        ((hidden_width, width), bf16),
        ((4, ROW_KINDS, LANES), f32),
        ((length_all, LANES), bf16),
        ((2, length_all, LANES), bf16),
        ((2, keys, LANES), bf16),
        ((2, keys, LANES), bf16),
        ((LANES, keys), bf16),
        ((LANES, keys), bf16),
        ((2, keys, length_all), bf16),
        ((2, keys, length_all), bf16),
        ((LANES, length_all), f32),
        ((8, length_all), f32),
        ((length_all, LANES), bf16),
        ((LANES, length_all), bf16),
        ((length_all, LANES), bf16),
        ((seqs * span, width), bf16),
        ((seqs * span, hidden_width), bf16),
        ((seqs * span, hidden_width), f32),
        ((seqs * span, hidden_width), bf16),
        ((seqs * span, width), bf16),
        ((length_all, LANES), bf16),
        ((4, stacked, width), bf16),
        ((2, stacked, width), bf16),
        ((stacked, width), bf16),
        ((stacked // 2, width), bf16),
        ((stacked // 4, width), bf16),
        ((stacked // 4, width), bf16),
        ((stacked, width), bf16),
        ((4, LANES + ROW_KINDS, 3 * LANES), bf16),
        ((2, LANES + ROW_KINDS, 3 * LANES), bf16),
        ((LANES + ROW_KINDS, 3 * LANES), bf16),
        ((LANES + ROW_KINDS, 3 * LANES), bf16),
        ((4, LANES + ROW_KINDS, 3 * LANES), bf16),
        ((4, ROW_KINDS, LANES), f32),
        ((8, span, width), bf16),
        ((6, span, width), bf16),
        ((span, width), bf16),
        ((4, MEM_PAD, width), bf16),
        ((2, MEM_PAD, width), bf16),
        ((8, 8, LANES), f32),
    ]
    made = pl.pallas_call(
        layer_kernel,
        out_shape=[
            jax.ShapeDtypeStruct((seqs * span, width), bf16),
            jax.ShapeDtypeStruct((seqs * span, width), f32),
            jax.ShapeDtypeStruct((seqs, MEM_PAD, width), bf16),
            jax.ShapeDtypeStruct((stacked, width), bf16),
            jax.ShapeDtypeStruct((4, LANES + ROW_KINDS, 3 * LANES), bf16),
            jax.ShapeDtypeStruct((8, LANES), f32),
        ],
        in_specs=[anywhere] * 3 + [smem] + [anywhere] * 15,
        out_specs=[anywhere] * 6,
        scratch_shapes=[pltpu.VMEM(shape, kind) for shape, kind in scratch]
        + [pltpu.SemaphoreType.DMA((count,)) for count in (SENDS, ARRIVALS, KEPT)],
        compiler_params=pltpu.CompilerParams(
            collective_id=0, has_side_effects=True, vmem_limit_bytes=60 * 2**20
        ),
        name="layer",
    )(
        inputs,
        out_grad,
        memory.transpose(1, 0, 2),
        lengths,
        w_query,
        w_key,
        w_value,
        w_out,
        w_up,
        w_down,
        *narrow,
        b_up,
    )
    mem_rows = memory.shape[1]
    shapes = (
        ((seqs, span, width), bf16),
        ((seqs, span, width), f32),
        ((mem_rows, seqs, width), f32),
        (w_query.shape, f32),
        (w_key.shape, f32),
        (w_value.shape, f32),
        (w_out.shape, f32),
        (w_up.shape, f32),
        (w_down.shape, f32),
        (b_query.shape, f32),
        (b_value.shape, f32),
        (b_out.shape, f32),
        (b_up.shape, f32),
        (b_down.shape, f32),
        (first_gain.shape, f32),
        (first_bias.shape, f32),
        (second_gain.shape, f32),
        (second_bias.shape, f32),
        ((seqs, 3), f32),
    )
    outs = pl.pallas_call(
        outputs_kernel,
        out_shape=[jax.ShapeDtypeStruct(shape, kind) for shape, kind in shapes],
        in_specs=[vmem] * 6,
        out_specs=[vmem] * len(shapes),
        compiler_params=pltpu.CompilerParams(vmem_limit_bytes=60 * 2**20),
        name="outputs",
    )(*made)
    return (*outs[:2], outs[2].transpose(1, 0, 2), *outs[3:])


def takes_fast_plan(mesh, inputs, memory, w_up):
    return (
        mesh.shape["shard"] == 4
        and mesh.shape["ctx"] == 8
        and inputs.shape == (2, LANES, HEADS * HEAD_DIM)
        and memory.shape[1] == MEM_ROWS
        and w_up.shape == (LANES, 4 * HEADS * HEAD_DIM)
    )


def solution(mesh):
    in_specs = (
        P("shard", "ctx", None),
        P("shard", None, None),
        P("shard"),
        P("shard", None),
        P("shard", None),
        P("shard", None),
        P("shard", None),
        P("shard", None),
        P("shard", None),
        P("shard"),
        P("shard"),
        P("shard"),
        P("shard"),
        P("shard"),
        P("shard"),
        P("shard"),
        P("shard"),
        P("shard"),
        P("shard", "ctx", None),
    )
    out_specs = (
        P("shard", "ctx", None),
        P("shard", "ctx", None),
        P("shard", None, None),
        P("shard", None),
        P("shard", None),
        P("shard", None),
        P("shard", None),
        P("shard", None),
        P("shard", None),
        P("shard"),
        P("shard"),
        P("shard"),
        P("shard"),
        P("shard"),
        P("shard"),
        P("shard"),
        P("shard"),
        P("shard"),
        P("shard", None),
    )

    def layer(*arrays):
        if takes_fast_plan(mesh, arrays[0], arrays[1], arrays[7]):
            return fast_layer(*arrays)
        return local(*arrays)

    return jax.shard_map(layer, mesh=mesh, in_specs=in_specs, out_specs=out_specs, check_vma=False)
```

```python
import math

import jax
import jax.numpy as jnp
from jax import lax
from jax.experimental import pallas as pl
from jax.experimental.pallas import tpu as pltpu
from jax.sharding import PartitionSpec as P

HEADS = 8
HEAD_DIM = 64
MEM_ROWS = 20
GELU_SCALE = math.sqrt(2 / math.pi)


eps = 1e-05


def matmul(operand, second):
    return jnp.dot(operand, second, preferred_element_type=jnp.float32)


def outer_sum(operand, second):
    return lax.dot_general(
        operand, second, (((0,), (0,)), ((), ())), preferred_element_type=jnp.float32
    )


def back_product(operand, second):
    return lax.dot_general(
        operand, second, (((1,), (1,)), ((), ())), preferred_element_type=jnp.float32
    )


def to_float(tensor):
    return tensor.astype(jnp.float32)


def smooth_act(values):
    return jax.nn.gelu(values, approximate=True)


def split_heads(tensor):
    return tensor.reshape(tensor.shape[0], tensor.shape[1], HEADS, HEAD_DIM)


def head_scores(queries, key_heads):
    return jnp.einsum(
        "sqhd,skhd->sqhk", queries, key_heads, preferred_element_type=jnp.float32
    ) * HEAD_DIM ** (-0.5)


def norm_forward(matrix, gain, offset):
    row_mean = jnp.mean(matrix, axis=-1, keepdims=True)
    centered = matrix - row_mean
    inverse = lax.rsqrt(jnp.mean(centered * centered, axis=-1, keepdims=True) + eps)
    unit_rows = centered * inverse
    return (unit_rows * gain + offset, unit_rows, inverse)


def norm_backward(cotangent, unit_rows, inverse, gain):
    scaled = cotangent * gain
    centered_grad = (
        scaled
        - jnp.mean(scaled, axis=-1, keepdims=True)
        - unit_rows * jnp.mean(scaled * unit_rows, axis=-1, keepdims=True)
    )
    return (
        inverse * centered_grad,
        jnp.sum(cotangent * unit_rows, axis=0),
        jnp.sum(cotangent, axis=0),
    )


def in_blocks(update, carried, arrays, first_row, slice_dim):
    piece_rows = arrays[0].shape[slice_dim]
    block_len = math.gcd(piece_rows, 1024)
    if block_len == piece_rows:
        return update(carried, arrays, first_row)

    def one_block(current, number):
        block_start = number * block_len
        sliced = tuple(
            (
                lax.dynamic_slice_in_dim(tensor, block_start, block_len, slice_dim)
                for tensor in arrays
            )
        )
        return (update(current, sliced, first_row + block_start), None)

    carried, unused = lax.scan(
        one_block, carried, jnp.arange(piece_rows // block_len, dtype=jnp.int32)
    )
    return carried


def softmax_update(carried, pieces, first_row, queries, lengths):
    row_max, row_total, weighted = carried
    key_piece, value_piece = pieces
    piece_rows = key_piece.shape[1]
    scores = head_scores(queries, split_heads(key_piece))
    key_mask = (first_row + jnp.arange(piece_rows, dtype=jnp.int32))[None, :] < lengths[:, None]
    scores = jnp.where(key_mask[:, None, None, :], scores, -1e30)
    new_max = jnp.maximum(row_max, jnp.max(scores, axis=-1))
    factor = jnp.exp(row_max - new_max)
    exponent = jnp.exp(scores - new_max[..., None])
    row_total = row_total * factor + jnp.sum(exponent, axis=-1)
    weighted = weighted * factor[..., None] + jnp.einsum(
        "sqhk,skhd->sqhd",
        exponent.astype(jnp.bfloat16),
        split_heads(value_piece),
        preferred_element_type=jnp.float32,
    )
    return (new_max, row_total, weighted)


def query_update(grad_q, pieces, first_row, queries, grad_heads, log_total, row_delta, lengths):
    key_piece, value_piece = pieces
    piece_rows = key_piece.shape[1]
    key_heads = split_heads(key_piece)
    scores = head_scores(queries, key_heads)
    key_mask = (first_row + jnp.arange(piece_rows, dtype=jnp.int32))[None, :] < lengths[:, None]
    scores = jnp.where(key_mask[:, None, None, :], scores, -1e30)
    attn_probs = jnp.exp(scores - log_total[..., None])
    value_dots = jnp.einsum(
        "sqhd,skhd->sqhk", grad_heads, split_heads(value_piece), preferred_element_type=jnp.float32
    )
    d_scores = (attn_probs * (value_dots - row_delta[..., None])).astype(jnp.bfloat16)
    return grad_q + jnp.einsum(
        "sqhk,skhd->sqhd", d_scores, key_heads, preferred_element_type=jnp.float32
    ) * HEAD_DIM ** (-0.5)


def key_update(carried, pieces, first_row, key_heads, value_heads, log_all, delta_all, key_mask):
    grad_k, grad_v = carried
    query_piece, grad_piece = pieces
    piece_rows = query_piece.shape[1]
    log_total = lax.dynamic_slice_in_dim(log_all, first_row, piece_rows, 1)
    row_delta = lax.dynamic_slice_in_dim(delta_all, first_row, piece_rows, 1)
    queries = split_heads(query_piece)
    grad_heads = split_heads(grad_piece)
    scores = head_scores(queries, key_heads)
    scores = jnp.where(key_mask[:, None, None, :], scores, -1e30)
    attn_probs = jnp.exp(scores - log_total[..., None])
    grad_v = grad_v + jnp.einsum(
        "sqhk,sqhd->skhd",
        attn_probs.astype(jnp.bfloat16),
        grad_heads,
        preferred_element_type=jnp.float32,
    )
    value_dots = jnp.einsum(
        "sqhd,skhd->sqhk", grad_heads, value_heads, preferred_element_type=jnp.float32
    )
    d_scores = (attn_probs * (value_dots - row_delta[..., None])).astype(jnp.bfloat16)
    grad_k = grad_k + jnp.einsum(
        "sqhk,sqhd->skhd", d_scores, queries, preferred_element_type=jnp.float32
    ) * HEAD_DIM ** (-0.5)
    return (grad_k, grad_v)


def local(
    inputs,
    memory,
    lengths,
    w_query,
    w_key,
    w_value,
    w_out,
    w_up,
    w_down,
    b_query,
    b_value,
    b_out,
    b_up,
    b_down,
    first_gain,
    first_bias,
    second_gain,
    second_bias,
    out_grad,
):
    gathered = (
        lax.all_gather(w_query, "shard", axis=0, tiled=True),
        lax.all_gather(w_key, "shard", axis=0, tiled=True),
        lax.all_gather(w_value, "shard", axis=0, tiled=True),
        lax.all_gather(w_out, "shard", axis=0, tiled=True),
        lax.all_gather(w_up, "shard", axis=0, tiled=True),
        lax.all_gather(w_down, "shard", axis=0, tiled=True),
        lax.all_gather(b_query, "shard", axis=0, tiled=True),
        lax.all_gather(b_value, "shard", axis=0, tiled=True),
        lax.all_gather(b_out, "shard", axis=0, tiled=True),
        lax.all_gather(b_up, "shard", axis=0, tiled=True),
        lax.all_gather(b_down, "shard", axis=0, tiled=True),
        lax.all_gather(first_gain, "shard", axis=0, tiled=True),
        lax.all_gather(first_bias, "shard", axis=0, tiled=True),
        lax.all_gather(second_gain, "shard", axis=0, tiled=True),
        lax.all_gather(second_bias, "shard", axis=0, tiled=True),
    )
    (
        full_query,
        full_key,
        full_value,
        full_out,
        full_up,
        full_down,
        bias_query,
        bias_value,
        bias_out,
        bias_up,
        bias_down,
        gain_one,
        offset_one,
        gain_two,
        offset_two,
    ) = gathered
    seq_count, local_len, features = inputs.shape
    mem_rows = memory.shape[1]
    token_rows = inputs.reshape(seq_count * local_len, features)
    mem_flat = memory.reshape(seq_count * mem_rows, features)
    query = (
        (matmul(token_rows, full_query) + to_float(bias_query))
        .astype(jnp.bfloat16)
        .reshape(seq_count, local_len, features)
    )
    key = matmul(token_rows, full_key).astype(jnp.bfloat16).reshape(seq_count, local_len, features)
    value = (
        (matmul(token_rows, full_value) + to_float(bias_value))
        .astype(jnp.bfloat16)
        .reshape(seq_count, local_len, features)
    )
    mem_key = matmul(mem_flat, full_key).astype(jnp.bfloat16).reshape(seq_count, mem_rows, features)
    mem_value = (
        (matmul(mem_flat, full_value) + to_float(bias_value))
        .astype(jnp.bfloat16)
        .reshape(seq_count, mem_rows, features)
    )
    query_heads = split_heads(query)
    mem_key_heads = split_heads(mem_key)
    mem_value_heads = split_heads(mem_value)
    position_zero = lax.axis_index("ctx") * local_len
    key_mask = (position_zero + jnp.arange(local_len, dtype=jnp.int32))[None, :] < lengths[:, None]
    mem_scores = head_scores(query_heads, mem_key_heads)
    mem_max = jnp.max(mem_scores, axis=-1)
    mem_exponent = jnp.exp(mem_scores - mem_max[..., None])
    start_state = (
        mem_max,
        jnp.sum(mem_exponent, axis=-1),
        jnp.einsum(
            "sqhk,skhd->sqhd",
            mem_exponent.astype(jnp.bfloat16),
            mem_value_heads,
            preferred_element_type=jnp.float32,
        ),
    )

    def forward_step(carried, pieces, first_row):
        return softmax_update(carried, pieces, first_row, query_heads, lengths)

    row_max, row_total, weighted = in_blocks(
        forward_step,
        start_state,
        (
            lax.all_gather(key, "ctx", axis=1, tiled=True),
            lax.all_gather(value, "ctx", axis=1, tiled=True),
        ),
        jnp.int32(0),
        1,
    )
    log_total = row_max + jnp.log(row_total)
    attended_full = (weighted / row_total[..., None]).reshape(seq_count, local_len, features)
    attended = attended_full.astype(jnp.bfloat16).reshape(seq_count * local_len, features)
    branch = matmul(attended, full_out) + to_float(bias_out)
    normed, unit_one, inverse_one = norm_forward(
        to_float(token_rows) + branch, to_float(gain_one), to_float(offset_one)
    )
    normed_low = normed.astype(jnp.bfloat16)
    pre_act = matmul(normed_low, full_up) + to_float(bias_up)
    activated, act_pullback = jax.vjp(smooth_act, pre_act)
    hidden = activated.astype(jnp.bfloat16)
    ffn_out = matmul(hidden, full_down) + to_float(bias_down)
    output_rows, unit_two, inverse_two = norm_forward(
        normed + ffn_out, to_float(gain_two), to_float(offset_two)
    )
    layer_out = output_rows.astype(jnp.bfloat16).reshape(seq_count, local_len, features)
    valid_rows = key_mask.astype(jnp.float32)
    input_squares = jnp.sum(jnp.square(to_float(inputs)), axis=2)
    branch_squares = jnp.sum(jnp.square(branch), axis=1).reshape(seq_count, local_len)
    ffn_squares = jnp.sum(jnp.square(ffn_out), axis=1).reshape(seq_count, local_len)
    squares = jnp.stack(
        [
            jnp.sum(valid_rows * input_squares, axis=1),
            jnp.sum(valid_rows * branch_squares, axis=1),
            jnp.sum(valid_rows * ffn_squares, axis=1),
        ],
        axis=1,
    )
    squares = lax.psum(squares, "ctx")
    stream_rms = jnp.sqrt(squares / (lengths.astype(jnp.float32)[:, None] * features))
    back_query, back_key, back_value, back_out, back_up, back_down, back_gain_one, back_gain_two = (
        lax.all_gather(w_query, "shard", axis=0, tiled=True),
        lax.all_gather(w_key, "shard", axis=0, tiled=True),
        lax.all_gather(w_value, "shard", axis=0, tiled=True),
        lax.all_gather(w_out, "shard", axis=0, tiled=True),
        lax.all_gather(w_up, "shard", axis=0, tiled=True),
        lax.all_gather(w_down, "shard", axis=0, tiled=True),
        lax.all_gather(first_gain, "shard", axis=0, tiled=True),
        lax.all_gather(second_gain, "shard", axis=0, tiled=True),
    )
    cotangent = to_float(out_grad).reshape(seq_count * local_len, features)
    grad_two, grad_gain_two, grad_offset_two = norm_backward(
        cotangent, unit_two, inverse_two, to_float(back_gain_two)
    )
    grad_ffn = grad_two.astype(jnp.bfloat16)
    grad_bias_down = jnp.sum(grad_ffn, axis=0, dtype=jnp.float32)
    grad_full_down = outer_sum(hidden, grad_ffn)
    grad_hidden = back_product(grad_ffn, back_down)
    grad_pre = act_pullback(grad_hidden)[0].astype(jnp.bfloat16)
    grad_bias_up = jnp.sum(grad_pre, axis=0, dtype=jnp.float32)
    grad_full_up = outer_sum(normed_low, grad_pre)
    grad_normed = grad_two + back_product(grad_pre, back_up)
    grad_one, grad_gain_one, grad_offset_one = norm_backward(
        grad_normed, unit_one, inverse_one, to_float(back_gain_one)
    )
    grad_branch = grad_one.astype(jnp.bfloat16)
    grad_bias_out = jnp.sum(grad_branch, axis=0, dtype=jnp.float32)
    grad_full_out = outer_sum(attended, grad_branch)
    grad_att = (
        back_product(grad_branch, back_out)
        .astype(jnp.bfloat16)
        .reshape(seq_count, local_len, features)
    )
    row_delta = jnp.sum(
        (to_float(grad_att) * attended_full).reshape(seq_count, local_len, HEADS, HEAD_DIM), axis=-1
    )
    log_all, delta_all = (
        lax.all_gather(log_total, "ctx", axis=1, tiled=True),
        lax.all_gather(row_delta, "ctx", axis=1, tiled=True),
    )
    grad_heads = split_heads(grad_att)
    mem_probs = jnp.exp(head_scores(query_heads, mem_key_heads) - log_total[..., None])
    mem_dots = jnp.einsum(
        "sqhd,skhd->sqhk", grad_heads, mem_value_heads, preferred_element_type=jnp.float32
    )
    mem_dscores = (mem_probs * (mem_dots - row_delta[..., None])).astype(jnp.bfloat16)
    start_query = jnp.einsum(
        "sqhk,skhd->sqhd", mem_dscores, mem_key_heads, preferred_element_type=jnp.float32
    ) * HEAD_DIM ** (-0.5)
    mem_grad_key = jnp.einsum(
        "sqhk,sqhd->skhd", mem_dscores, query_heads, preferred_element_type=jnp.float32
    ) * HEAD_DIM ** (-0.5)
    mem_grad_value = jnp.einsum(
        "sqhk,sqhd->skhd",
        mem_probs.astype(jnp.bfloat16),
        grad_heads,
        preferred_element_type=jnp.float32,
    )
    key_heads = split_heads(key)
    value_heads = split_heads(value)
    empty_grads = jnp.zeros(key_heads.shape, jnp.float32)

    def query_step(carried, pieces, first_row):
        return query_update(
            carried, pieces, first_row, query_heads, grad_heads, log_total, row_delta, lengths
        )

    def key_step(carried, pieces, first_row):
        return key_update(
            carried, pieces, first_row, key_heads, value_heads, log_all, delta_all, key_mask
        )

    grad_q = in_blocks(
        query_step,
        start_query,
        (
            lax.all_gather(key, "ctx", axis=1, tiled=True),
            lax.all_gather(value, "ctx", axis=1, tiled=True),
        ),
        jnp.int32(0),
        1,
    )
    grad_k, grad_v = in_blocks(
        key_step,
        (empty_grads, empty_grads),
        (
            lax.all_gather(query, "ctx", axis=1, tiled=True),
            lax.all_gather(grad_att, "ctx", axis=1, tiled=True),
        ),
        jnp.int32(0),
        1,
    )
    mem_key_sum, mem_value_sum = lax.psum((mem_grad_key, mem_grad_value), "ctx")
    mem_key_low = mem_key_sum.reshape(seq_count * mem_rows, features).astype(jnp.bfloat16)
    mem_value_low = mem_value_sum.reshape(seq_count * mem_rows, features).astype(jnp.bfloat16)
    first_only = (lax.axis_index("ctx") == 0).astype(jnp.float32)
    grad_q_low = grad_q.reshape(seq_count * local_len, features).astype(jnp.bfloat16)
    grad_k_low = grad_k.reshape(seq_count * local_len, features).astype(jnp.bfloat16)
    grad_v_low = grad_v.reshape(seq_count * local_len, features).astype(jnp.bfloat16)
    grad_full_query = outer_sum(token_rows, grad_q_low)
    grad_full_key = outer_sum(token_rows, grad_k_low) + first_only * outer_sum(
        mem_flat, mem_key_low
    )
    grad_full_value = outer_sum(token_rows, grad_v_low) + first_only * outer_sum(
        mem_flat, mem_value_low
    )
    grad_bias_query = jnp.sum(grad_q_low, axis=0, dtype=jnp.float32)
    grad_bias_value = jnp.sum(grad_v_low, axis=0, dtype=jnp.float32) + first_only * jnp.sum(
        mem_value_low, axis=0, dtype=jnp.float32
    )
    input_grad = (
        grad_one
        + back_product(grad_q_low, back_query)
        + back_product(grad_k_low, back_key)
        + back_product(grad_v_low, back_value)
    ).reshape(seq_count, local_len, features)
    memory_grad = (
        back_product(mem_key_low, back_key) + back_product(mem_value_low, back_value)
    ).reshape(seq_count, mem_rows, features)
    owned_parts = (
        lax.psum_scatter(
            grad_full_query.astype(jnp.bfloat16), "shard", scatter_dimension=0, tiled=True
        ).astype(jnp.float32),
        lax.psum_scatter(
            grad_full_key.astype(jnp.bfloat16), "shard", scatter_dimension=0, tiled=True
        ).astype(jnp.float32),
        lax.psum_scatter(
            grad_full_value.astype(jnp.bfloat16), "shard", scatter_dimension=0, tiled=True
        ).astype(jnp.float32),
        lax.psum_scatter(
            grad_full_out.astype(jnp.bfloat16), "shard", scatter_dimension=0, tiled=True
        ).astype(jnp.float32),
        lax.psum_scatter(
            grad_full_up.astype(jnp.bfloat16), "shard", scatter_dimension=0, tiled=True
        ).astype(jnp.float32),
        lax.psum_scatter(
            grad_full_down.astype(jnp.bfloat16), "shard", scatter_dimension=0, tiled=True
        ).astype(jnp.float32),
        lax.psum_scatter(
            grad_bias_query.astype(jnp.bfloat16), "shard", scatter_dimension=0, tiled=True
        ).astype(jnp.float32),
        lax.psum_scatter(
            grad_bias_value.astype(jnp.bfloat16), "shard", scatter_dimension=0, tiled=True
        ).astype(jnp.float32),
        lax.psum_scatter(
            grad_bias_out.astype(jnp.bfloat16), "shard", scatter_dimension=0, tiled=True
        ).astype(jnp.float32),
        lax.psum_scatter(
            grad_bias_up.astype(jnp.bfloat16), "shard", scatter_dimension=0, tiled=True
        ).astype(jnp.float32),
        lax.psum_scatter(
            grad_bias_down.astype(jnp.bfloat16), "shard", scatter_dimension=0, tiled=True
        ).astype(jnp.float32),
        lax.psum_scatter(
            grad_gain_one.astype(jnp.bfloat16), "shard", scatter_dimension=0, tiled=True
        ).astype(jnp.float32),
        lax.psum_scatter(
            grad_offset_one.astype(jnp.bfloat16), "shard", scatter_dimension=0, tiled=True
        ).astype(jnp.float32),
        lax.psum_scatter(
            grad_gain_two.astype(jnp.bfloat16), "shard", scatter_dimension=0, tiled=True
        ).astype(jnp.float32),
        lax.psum_scatter(
            grad_offset_two.astype(jnp.bfloat16), "shard", scatter_dimension=0, tiled=True
        ).astype(jnp.float32),
    )
    (
        part_query,
        part_key,
        part_value,
        part_out,
        part_up,
        part_down,
        part_bias_query,
        part_bias_value,
        part_bias_out,
        part_bias_up,
        part_bias_down,
        part_gain_one,
        part_offset_one,
        part_gain_two,
        part_offset_two,
    ) = owned_parts
    summed_grads = lax.psum(
        (
            part_query,
            part_key,
            part_value,
            part_out,
            part_up,
            part_down,
            part_bias_query,
            part_bias_value,
            part_bias_out,
            part_bias_up,
            part_bias_down,
            part_gain_one,
            part_offset_one,
            part_gain_two,
            part_offset_two,
        ),
        "ctx",
    )
    (
        sum_query,
        sum_key,
        sum_value,
        sum_out,
        sum_up,
        sum_down,
        sum_bias_query,
        sum_bias_value,
        sum_bias_out,
        sum_bias_up,
        sum_bias_down,
        sum_gain_one,
        sum_offset_one,
        sum_gain_two,
        sum_offset_two,
    ) = summed_grads
    return (
        layer_out,
        input_grad,
        memory_grad,
        sum_query,
        sum_key,
        sum_value,
        sum_out,
        sum_up,
        sum_down,
        sum_bias_query,
        sum_bias_value,
        sum_bias_out,
        sum_bias_up,
        sum_bias_down,
        sum_gain_one,
        sum_offset_one,
        sum_gain_two,
        sum_offset_two,
        stream_rms,
    )


MESH_ID = pl.DeviceIdType.MESH
LANES = 128
MEM_PAD = 32
ROW_KINDS = 16
SENDS, ARRIVALS, KEPT = 18, 89, 23
PIECES = ((128, 'xyz'), (128, 'zyx'), (128, 'yxz'), (128, 'yxz'), (256, 'xyz'), (256, 'zyx'), (128, 'yzx'))


def flipped(index, offset, bits):
    total = 0
    for bit in range(bits):
        digit = lax.rem(lax.div(index, 2**bit), 2)
        if offset >> bit & 1:
            digit = 1 - digit
        total = total + digit * 2**bit
    return total


class Copies:
    def __init__(self, send_sems, recv_sems, local_sems, measure):
        self.send_sems, self.recv_sems, self.local_sems = send_sems, recv_sems, local_sems
        self.measure = measure
        self.sent, self.alone, self.received, self.kept = [], [], 0, 0

    def send(self, src, dst, device):
        return self.send_all([(src, dst, device)], dst)

    def send_all(self, items, whole):
        rows = math.prod(whole.shape) * whole.dtype.itemsize // (2 * self.measure.shape[1])
        if rows % 16:
            pool = len(self.sent)
            self.sent.append(None)
            self.alone.append((pool, whole))
        else:
            pool = next(
                (
                    number
                    for number, held in enumerate(self.sent)
                    if held is not None and held + rows <= self.measure.shape[0]
                ),
                len(self.sent),
            )
            if pool == len(self.sent):
                self.sent.append(0)
            self.sent[pool] += rows
        arrival = self.recv_sems.at[self.received]
        self.received += 1
        for src, dst, device in items:
            pltpu.make_async_remote_copy(
                src_ref=src,
                dst_ref=dst,
                send_sem=self.send_sems.at[pool],
                recv_sem=arrival,
                device_id=device,
                device_id_type=MESH_ID,
            ).start()
        return Arrival(whole, arrival)

    def keep(self, items, whole):
        done = self.local_sems.at[self.kept]
        self.kept += 1
        for src, dst in items:
            pltpu.make_async_copy(src, dst, done).start()
        return Arrival(whole, done)

    def finish(self):
        for pool, whole in self.alone:
            Arrival(whole, self.send_sems.at[pool]).wait()
        for pool, rows in enumerate(self.sent):
            if rows is not None:
                Arrival(self.measure.at[pl.ds(0, rows)], self.send_sems.at[pool]).wait()


class Held:
    pass


class Arrival:
    def __init__(self, whole, semaphore):
        self.whole, self.semaphore = whole, semaphore

    def wait(self):
        pltpu.make_async_copy(self.whole, self.whole, self.semaphore).wait()


def layer_kernel(
    x_ref,
    g_ref,
    mem_ref,
    len_ref,
    wq_ref,
    wk_ref,
    wv_ref,
    wo_ref,
    wu_ref,
    wd_ref,
    *refs,
):
    vec_refs, refs = refs[:9], refs[9:]
    (o_layer, o_input, o_mem, o_fin, o_heads, o_rms), refs = refs[:6], refs[6:]
    (
        own_in,
        own_g,
        own_mem,
        mem_in,
        *rest,
    ) = refs
    narrow_in, rest = rest[:8], rest[8:]
    (
        wide_in,
        rms_rows,
        d_branch,
        joined,
        out_rows,
        in_grad,
        tokens,
        tokens_t,
        w_heads,
        w_out,
        w_up,
        w_down,
        vecs,
        q_scaled,
        q_aug,
        k_aug,
        v_mask,
        k_turned,
        v_turned,
        probs,
        d_scores,
        mixed_t,
        inverse_total,
        d_scaled,
        d_scaled_t,
        mixed,
        att,
        hidden,
        act_slope,
        d_pre,
        d_att,
        d_mixed,
        partial,
        got_core,
        got_first,
        got_second,
        got_third,
        got_far,
        final,
        head_part,
        head_core,
        head_x,
        head_far,
        head_all,
        vec_part,
        dx_part,
        dx_got,
        dx_far,
        mem_part,
        mem_far,
        squares,
        send_sems,
        recv_sems,
        local_sems,
    ) = rest
    bf16, f32 = jnp.bfloat16, jnp.float32
    shard, ctx = lax.axis_index("shard"), lax.axis_index("ctx")
    span, width = x_ref.shape[1], x_ref.shape[2]
    spans = 8
    length_all = span * spans
    keys = length_all + MEM_PAD
    x_half, core = lax.div(shard, 2), lax.rem(shard, 2)
    upper, pair = lax.div(ctx, 4), lax.rem(ctx, 4)
    y_side = lax.rem(ctx, 2)
    z_side = lax.rem(lax.div(ctx, 2) + upper, 2)

    def shard_peer(offset):
        return {"shard": flipped(shard, offset, 2), "ctx": ctx}

    def ctx_peer(offset):
        return {"shard": shard, "ctx": flipped(ctx, offset, 3)}

    def span_rows(index):
        return pl.ds(pl.multiple_of(index * span, span), span)

    def pair_lanes(index, size=LANES):
        return pl.ds(pl.multiple_of(index * LANES, LANES), size)

    copies = Copies(send_sems, recv_sems, local_sems, partial.at[0])

    barrier = pltpu.get_barrier_semaphore()
    for offset in (1, 2, 3):
        pl.semaphore_signal(barrier, inc=1, device_id=shard_peer(offset), device_id_type=MESH_ID)
    for offset in range(1, 8):
        pl.semaphore_signal(barrier, inc=1, device_id=ctx_peer(offset), device_id_type=MESH_ID)

    def aligned_rows(index, rows):
        return pl.ds(pl.multiple_of(index * rows, rows), rows)

    def rows_of(ref, index, start=0, rows=None):
        owned = ref.shape[0] // 4
        return ref.at[pl.ds(pl.multiple_of(index * owned + start, LANES), rows or owned)]

    my_rows = pl.ds(pl.multiple_of(shard * LANES, LANES), LANES)
    head_refs = (wq_ref, wk_ref, wv_ref)
    own_blocks = [
        copies.keep(
            [
                (
                    ref.at[:, pair_lanes(pair)],
                    w_heads.at[my_rows, pl.ds(part * LANES, LANES)],
                )
                for part, ref in enumerate(head_refs)
            ],
            w_heads.at[my_rows],
        ),
        copies.keep([(x_ref.at[upper], tokens.at[span_rows(ctx)])], own_in.at[0]),
    ]
    narrow_copies = [
        copies.keep([(ref, copied)], copied)
        for ref, copied in zip(vec_refs, (*narrow_in, wide_in))
    ]
    full_weights = ((wo_ref, w_out), (wd_ref, w_down), (wu_ref, w_up))
    own_weights = [
        copies.keep([(ref, rows_of(full, shard)) for ref, full in full_weights], partial.at[0]),
        copies.keep([(x_ref, own_in)], own_in),
        copies.keep([(g_ref, own_g)], own_g),
        copies.keep([(mem_ref, mem_in)], mem_in),
    ]
    pl.semaphore_wait(barrier, 10)

    partner = flipped(ctx, 6, 3)
    half_span = span // 2

    def half_rows(index, half):
        return pl.ds(pl.multiple_of(index * span + half * half_span, half_span), half_span)

    far_tokens = [
        copies.send(
            x_ref.at[1 - upper, pl.ds(half * half_span, half_span)],
            tokens.at[half_rows(ctx, half)],
            ctx_peer(6),
        )
        for half in range(2)
    ]
    def near_send(offsets):
        return copies.send_all(
            [
                (x_ref.at[upper], tokens.at[span_rows(ctx)], ctx_peer(offset))
                for offset in offsets
            ],
            tokens.at[pl.ds(0, span * len(offsets))],
        )

    near_pair, near_y = near_send((3, 2)), near_send((1,))

    def send_head_rows(offset):
        return copies.send_all(
            [
                (
                    ref.at[:, pair_lanes(pair)],
                    w_heads.at[my_rows, pl.ds(part * LANES, LANES)],
                    shard_peer(offset),
                )
                for part, ref in enumerate(head_refs)
            ],
            w_heads.at[my_rows],
        )

    x_heads = send_head_rows(2)
    core_heads = send_head_rows(1)
    for copy in narrow_copies:
        copy.wait()
    for kind, ref in enumerate((*narrow_in, wide_in)):
        values = ref[...].astype(f32)
        for piece in range(ref.shape[0] // LANES):
            vecs[shard, kind + piece : kind + piece + 1, :] = values[
                piece * LANES : (piece + 1) * LANES
            ].reshape(1, LANES)
    vec_copies = copies.send_all(
        [(vecs.at[shard], vecs.at[shard], shard_peer(offset)) for offset in (2, 3, 1)],
        vecs.at[pl.ds(0, 3)],
    )
    half_down = wd_ref.shape[0] // 2
    x_out = copies.send(wo_ref, rows_of(w_out, shard), shard_peer(2))
    x_down = copies.send(
        wd_ref.at[pl.ds(pl.multiple_of(y_side * half_down, LANES), half_down)],
        rows_of(w_down, shard, y_side * half_down, half_down),
        shard_peer(2),
    )
    half_up = wu_ref.shape[0] // 2
    x_up = [
        copies.send(
            wu_ref.at[pl.ds(half * half_up, half_up)],
            w_up.at[aligned_rows(shard * 2 + half, half_up)],
            shard_peer(2),
        )
        for half in range(2)
    ]
    core_weights = copies.send_all(
        [(ref, rows_of(full, shard), shard_peer(1)) for ref, full in full_weights], partial.at[0]
    )

    for copy in own_weights:
        copy.wait()
    own_mem[...] = jnp.zeros_like(own_mem)
    for seq in range(own_mem.shape[0]):
        own_mem[seq, :MEM_ROWS, :] = mem_in[:, seq, :]

    passed_pair, passed_y = [], []
    for half, copy in enumerate(far_tokens):
        copy.wait()
        place = tokens.at[half_rows(partner, half)]
        passed_pair.append(
            copies.send_all(
                [(place, place, ctx_peer(3)), (place, place, ctx_peer(2))], tokens.at[pl.ds(0, span)]
            )
        )
        passed_y.append(copies.send(place, place, ctx_peer(1)))
    x_heads.wait()
    x_owner = flipped(shard, 2, 2)
    place = rows_of(w_heads, x_owner)
    passed_heads = copies.send(place, place, shard_peer(1))
    x_out.wait()
    x_down.wait()
    place = rows_of(w_down, x_owner, y_side * half_down, half_down)
    y_down = copies.send(place, place, ctx_peer(1))
    passed_early = copies.send_all(
        [(part, part, shard_peer(1)) for part in (rows_of(w_out, x_owner), place)],
        partial.at[0, pl.ds(0, LANES + half_down)],
    )

    for copy in own_blocks:
        copy.wait()
    for copy in (core_heads, passed_heads, vec_copies):
        copy.wait()

    def full_vec(kind):
        return jnp.concatenate([vecs[owner, kind : kind + 1, :] for owner in range(4)], axis=1)

    length = len_ref[upper]
    lane = lax.broadcasted_iota(jnp.int32, (span * 2, LANES), 1)

    def put_query(rows, projected):
        scaled = (projected + vecs[pair, 0:1, :]).astype(bf16).astype(f32) * (HEAD_DIM**-0.5)
        q_scaled[rows, :] = scaled.astype(bf16)
        q_aug[0, rows, :] = jnp.where(
            lane < HEAD_DIM, scaled, jnp.where(lane == HEAD_DIM, 1.0, 0.0)
        ).astype(bf16)
        q_aug[1, rows, :] = jnp.where(
            lane >= HEAD_DIM, scaled, jnp.where(lane == 0, 1.0, 0.0)
        ).astype(bf16)

    def put_key_value(rows, key, value, left_out):
        lanes = lax.broadcasted_iota(jnp.int32, key.shape, 1)
        key = key.astype(bf16).astype(f32)
        value = (value + vecs[pair, 1:2, :]).astype(bf16).astype(f32)
        k_aug[0, rows, :] = jnp.where(
            lanes < HEAD_DIM, key, jnp.where(lanes == HEAD_DIM, left_out, 0.0)
        ).astype(bf16)
        k_aug[1, rows, :] = jnp.where(
            lanes >= HEAD_DIM, key, jnp.where(lanes == 0, left_out, 0.0)
        ).astype(bf16)
        v_mask[0, rows, :] = jnp.where(lanes < HEAD_DIM, value, 0.0).astype(bf16)
        v_mask[1, rows, :] = jnp.where(lanes >= HEAD_DIM, value, 0.0).astype(bf16)
        k_turned[:, rows] = key.T.astype(bf16)
        v_turned[:, rows] = value.T.astype(bf16)

    def block_rows(high):
        block = lax.div(flipped(ctx, 2 * high, 3), 2)
        return block, pl.ds(pl.multiple_of(block * span * 2, span * 2), span * 2)

    arrivals = ([near_y], [near_pair], passed_pair, passed_y)
    for high in (0, 1, 3, 2):
        for copy in arrivals[high]:
            copy.wait()
        block, rows = block_rows(high)
        projected = matmul(tokens[rows, :], w_heads[...])
        put_query(rows, projected[:, :LANES])
        position = block * span * 2 + lax.broadcasted_iota(jnp.int32, (span * 2, LANES), 0)
        put_key_value(
            rows,
            projected[:, LANES : 2 * LANES],
            projected[:, 2 * LANES :],
            jnp.where(position < length, 0.0, -1e30),
        )
    projected = matmul(own_mem[upper], w_heads[:, LANES:])
    position = lax.broadcasted_iota(jnp.int32, (MEM_PAD, LANES), 0)
    put_key_value(
        pl.ds(length_all, MEM_PAD),
        projected[:, :LANES],
        projected[:, LANES:],
        jnp.where(position < MEM_ROWS, 0.0, -1e30),
    )

    att_copies = []
    for high in (3, 2, 1, 0):
        if high == 1:
            x_up[0].wait()
            place = w_up.at[aligned_rows(x_owner * 2, half_up)]
            passed_up = copies.send(place, place, shard_peer(1))
        _, rows = block_rows(high)
        for head in range(2):
            scores = back_product(k_aug[head], q_aug[head, rows, :])
            exponent = jnp.exp(scores - jnp.max(scores, axis=0, keepdims=True))
            total = jnp.sum(exponent, axis=0, keepdims=True)
            inverse = 1.0 / total
            inverse_total[head : head + 1, rows] = inverse
            weights = exponent.astype(bf16)
            probs[head, :, rows] = weights
            half = pl.ds(head * HEAD_DIM, HEAD_DIM)
            mixed_t[half, rows] = matmul(v_turned[half, :], weights) * inverse
        mixed[rows, :] = mixed_t[:, rows].T.astype(bf16)
        att_items = []
        for low in (0, 1):
            offset = 2 * high + low
            source = mixed.at[span_rows(flipped(ctx, offset, 3))]
            target = att.at[span_rows(upper), pair_lanes(pair)]
            if offset:
                att_items.append((source, target, ctx_peer(offset)))
            else:
                own_att = copies.keep([(source, target)], source)

        att_copies.append(copies.send_all(att_items, mixed.at[pl.ds(0, span * len(att_items))]))

    y_down.wait()
    x_up[1].wait()
    places = (
        w_up.at[aligned_rows(x_owner * 2 + 1, half_up)],
        rows_of(w_down, x_owner, (1 - y_side) * half_down, half_down),
    )
    passed_weights = copies.send_all(
        [(place, place, shard_peer(1)) for place in places],
        partial.at[0, pl.ds(0, half_down + 4 * half_up)],
    )
    for block in range(4):
        rows = pl.ds(block * span * 2, span * 2)
        tokens_t[:, rows] = tokens[rows, :].astype(f32).T.astype(bf16)
    core_weights.wait()
    passed_early.wait()
    own_att.wait()
    for copy in att_copies:
        copy.wait()

    seqs = own_in.shape[0]
    local_rows = seqs * span
    own_x = own_in[...].reshape(local_rows, width).astype(f32)
    branch = matmul(att[...], w_out[...]) + full_vec(2)
    normed, unit_one, inverse_one = norm_forward(own_x + branch, full_vec(4), full_vec(5))
    normed_low = normed.astype(bf16)
    passed_up.wait()
    passed_weights.wait()
    ffn_out = jnp.zeros((local_rows, width), f32)
    for chunk in range(4):
        columns = pl.ds(chunk * width, width)
        bias = jnp.concatenate([vecs[chunk, 8 + i : 9 + i, :] for i in range(4)], axis=1)
        pre_act = matmul(normed_low, w_up[:, columns]) + bias
        square = pre_act * pre_act
        bent = jnp.tanh(GELU_SCALE * pre_act * (1.0 + 0.044715 * square))
        hidden[:, columns] = (0.5 * pre_act * (1.0 + bent)).astype(bf16)
        act_slope[:, columns] = 0.5 * (1.0 + bent) + 0.5 * pre_act * (1.0 - bent * bent) * (
            GELU_SCALE * (1.0 + 3 * 0.044715 * square)
        )
        ffn_out = ffn_out + matmul(hidden[:, columns], w_down[columns, :])
    ffn_out = ffn_out + full_vec(3)
    output, unit_two, inverse_two = norm_forward(normed + ffn_out, full_vec(6), full_vec(7))
    out_rows[...] = output.astype(bf16)

    chunks = []
    first_row = 0
    for rows, order in PIECES:
        chunks.append((first_row, rows, order))
        first_row += rows
    sides = {"x": x_half, "y": y_side, "z": z_side}
    peers = {"x": shard_peer(2), "y": ctx_peer(1), "z": ctx_peer(2)}
    waits = {}
    out_copies = [copies.keep([(out_rows, o_layer)], out_rows)]
    final_items, input_items = [], []

    def arrived(key):
        waits.pop(key).wait()

    def add_rows(target, first):
        target[...] = (target[...].astype(f32) + first[...].astype(f32)).astype(bf16)

    def aligned(start, rows):
        return pl.ds(pl.multiple_of(start, rows), rows)

    def core_send(number):
        start, rows, _ = chunks[number]
        waits["core", number] = copies.send_all(
            [
                (
                    partial.at[2 * side + 1 - core, pl.ds(start, rows)],
                    got_core.at[side, pl.ds(start, rows)],
                    shard_peer(1),
                )
                for side in range(2)
            ],
            partial.at[0, pl.ds(0, 2 * rows)],
        )

    def slabs(number, step):
        start, rows, order = chunks[number]
        if step == 0:
            return [got_core.at[side, pl.ds(start, rows)] for side in range(2)]
        buffer = (got_first, got_second, got_third)[step - 1]
        size = rows >> (step - 1)
        first = start >> (step - 1)
        if "x" in order[:step]:
            return [buffer.at[pl.ds(first, size)]]
        return [buffer.at[pl.ds(first + side * (size // 2), size // 2)] for side in range(2)]

    def split(number, step):
        whole = slabs(number, step)
        axis = chunks[number][2][step]
        side = sides[axis]
        if axis == "x":
            start, rows, _ = chunks[number]
            if step == 0:
                return (
                    [got_core.at[side, pl.ds(start, rows)]],
                    [got_core.at[1 - side, pl.ds(start, rows)]],
                )
            buffer = (got_first, got_second, got_third)[step - 1]
            size, first = rows >> step, start >> (step - 1)
            return (
                [buffer.at[aligned(first + side * size, size)]],
                [buffer.at[aligned(first + (1 - side) * size, size)]],
            )
        half = whole[0].shape[0] // 2
        return (
            [slab.at[aligned(side * half, half)] for slab in whole],
            [slab.at[aligned((1 - side) * half, half)] for slab in whole],
        )

    def halve(number, step):
        if step == 0:
            arrived(("core", number))
            for side, slab in enumerate(slabs(number, 0)):
                start, rows, _ = chunks[number]
                add_rows(slab, partial.at[2 * side + core, pl.ds(start, rows)])
        else:
            join(number, step)
        axis = chunks[number][2][step]
        _, gone = split(number, step)
        start, rows, _ = chunks[number]
        waits[step, number] = copies.send_all(
            [(slab, target, peers[axis]) for slab, target in zip(gone, slabs(number, step + 1))],
            (got_first, got_second, got_third)[step].at[pl.ds(start >> step, rows >> step)],
        )

    def join(number, step):
        arrived((step - 1, number))
        kept, _ = split(number, step - 1)
        for target, slab in zip(slabs(number, step), kept):
            add_rows(target, slab)

    def cross(number):
        join(number, 3)
        start, rows, _ = chunks[number]
        here = pl.ds(start // 4, rows // 4)
        waits["cross", number] = copies.send(got_third.at[here], got_far.at[here], ctx_peer(6))

    def place_of(number, count):
        start, rows, order = chunks[number]
        for axis in order.replace("x", "")[: 2 - count]:
            rows = rows // 2
            start = start + sides[axis] * rows
        return aligned(start, rows)

    def gather(number, count):
        start, rows, order = chunks[number]
        if count == 0:
            arrived(("cross", number))
            here = pl.ds(start // 4, rows // 4)
            final[place_of(number, 0), :] = (
                got_third[here, :].astype(f32) + got_far[here, :].astype(f32)
            ).astype(bf16)
        else:
            arrived(("gather", number))
        place = final.at[place_of(number, count)]
        waits["gather", number] = copies.send(
            place, place, peers[order.replace("x", "")[1 - count]]
        )

    def write_out(number):
        start, rows, _ = chunks[number]
        arrived(("gather", number))
        place = pl.ds(start, rows)
        final_items.append((final.at[place], o_fin.at[place]))
        if len(final_items) == len(chunks):
            out_copies.append(copies.keep(final_items, final))

    def outer_part(number):
        start, rows, _ = chunks[number]
        done = 0
        while done < rows:
            row = start + done
            if row < width:
                size = min(rows - done, width - row)
                for owner in range(4):
                    columns = slice(owner * width + row, owner * width + row + size)
                    partial[owner, row : row + size, :] = outer_sum(
                        hidden[:, columns], held.d_ffn
                    ).astype(bf16)
            else:
                size = LANES
                if row < 2 * width:
                    chunk = (row - width) // LANES
                    grad = outer_sum(
                        held.normed, d_pre[:, chunk * width : (chunk + 1) * width]
                    ).astype(bf16)
                else:
                    grad = outer_sum(att[...], d_branch[...]).astype(bf16)
                for owner in range(4):
                    partial[owner, row : row + size, :] = grad[owner * LANES : (owner + 1) * LANES]
            done += size
        core_send(number)

    held = Held()
    held.normed = normed_low


    def second_norm():
        cotangent = own_g[...].reshape(local_rows, width).astype(f32)
        held.two, held.second_gain, held.second_bias = norm_backward(
            cotangent, unit_two, inverse_two, full_vec(6)
        )
        held.d_ffn = held.two.astype(bf16)

    def first_norm():
        d_normed = held.two
        for chunk in range(4):
            columns = pl.ds(chunk * width, width)
            d_hidden = back_product(held.d_ffn, w_down[columns, :])
            d_chunk = (d_hidden * act_slope[:, columns]).astype(bf16)
            d_pre[:, columns] = d_chunk
            d_normed = d_normed + back_product(d_chunk, w_up[:, columns])
        d_one, held.first_gain, held.first_bias = norm_backward(
            d_normed, unit_one, inverse_one, full_vec(4)
        )
        in_grad[...] = d_one
        d_branch[...] = d_one.astype(bf16)

    def attended_grad():
        held.d_att = []
        for rows_of_seq, offsets in ((1 - upper, (6, 7, 4, 5)), (upper, (2, 3, 1, 0))):
            rows = span_rows(rows_of_seq)
            d_att[rows, :] = back_product(d_branch[rows, :], w_out[...]).astype(bf16)
            items = []
            for offset in offsets:
                peer = flipped(ctx, offset, 3)
                source = d_att.at[rows, pair_lanes(lax.rem(peer, 4))]
                target = d_mixed.at[span_rows(ctx)]
                if offset:
                    items.append((source, target, ctx_peer(offset)))
                else:
                    held.own_d_att = copies.keep([(source, target)], target)
            held.d_att.append(copies.send_all(items, d_mixed.at[pl.ds(0, span * len(items))]))

    def square_sums():
        row_id = lax.broadcasted_iota(jnp.int32, (8, LANES), 0)
        tile = jnp.zeros((8, LANES), f32)
        for seq in range(seqs):
            position = ctx * span + lax.broadcasted_iota(jnp.int32, (span, 1), 0)
            valid = jnp.where(position < len_ref[seq], 1.0, 0.0)
            for kind, values in enumerate((own_x, branch, ffn_out)):
                piece = values[seq * span : (seq + 1) * span]
                row_sum = jnp.sum(piece * piece, axis=1, keepdims=True) * valid
                tile = tile + jnp.where(
                    row_id == seq * 3 + kind, jnp.sum(row_sum, axis=0, keepdims=True), 0.0
                )
        squares[ctx] = tile
        held.squares = copies.send_all(
            [
                (squares.at[ctx], squares.at[ctx], ctx_peer(offset))
                for offset in (6, 7, 4, 5, 2, 3, 1)
            ],
            squares.at[pl.ds(0, 7)],
        )

    def narrow_grads():
        vec_part[...] = jnp.zeros_like(vec_part)
        wide_grads = (
            jnp.sum(d_branch[...].astype(f32), axis=0, keepdims=True),
            jnp.sum(held.d_ffn.astype(f32), axis=0, keepdims=True),
            held.first_gain,
            held.first_bias,
            held.second_gain,
            held.second_bias,
        )
        for owner in range(4):
            for kind, values in enumerate(wide_grads):
                vec_part[owner, 2 + kind : 3 + kind, :] = values.reshape(1, width)[
                    :, owner * LANES : (owner + 1) * LANES
                ]
            columns = pl.ds(owner * width, width)
            bias = jnp.sum(d_pre[:, columns].astype(f32), axis=0, keepdims=True)
            for part in range(4):
                vec_part[owner, 8 + part : 9 + part, :] = bias[
                    :, part * LANES : (part + 1) * LANES
                ]

    def deltas():
        held.own_d_att.wait()
        for copy in held.d_att:
            copy.wait()
        turned = d_mixed[...].astype(f32).T
        products = turned * mixed_t[...]
        held.deltas = []
        for head in range(2):
            half = slice(head * HEAD_DIM, (head + 1) * HEAD_DIM)
            inverse = inverse_total[head : head + 1, :]
            held.deltas.append(jnp.sum(products[half], axis=0, keepdims=True) * inverse)
            d_scaled_t[half, :] = (turned[half] * inverse).astype(bf16)
        d_scaled[...] = d_scaled_t[...].astype(f32).T.astype(bf16)

    def score_grads(head):
        delta = held.deltas[head]
        for block in range(4):
            rows = slice(block * span * 2, (block + 1) * span * 2)
            dots = matmul(v_mask[head], d_scaled_t[:, rows])
            weights = probs[head, :, rows].astype(f32)
            d_scores[head, :, rows] = (weights * (dots - delta[:, rows])).astype(bf16)

    def scores_0():
        score_grads(0)

    def scores_1():
        score_grads(1)

    def key_value_grads():
        key_lane = lax.broadcasted_iota(jnp.int32, (keys, LANES), 1)
        grad_value = jnp.where(
            key_lane < HEAD_DIM, matmul(probs[0], d_scaled[...]), matmul(probs[1], d_scaled[...])
        ).astype(bf16)
        grad_key = jnp.where(
            key_lane < HEAD_DIM,
            matmul(d_scores[0], q_scaled[...]),
            matmul(d_scores[1], q_scaled[...]),
        ).astype(bf16)
        joined[:, LANES : 2 * LANES] = grad_key[:length_all]
        joined[:, 2 * LANES :] = grad_value[:length_all]
        held.memory = jnp.concatenate([grad_key[length_all:], grad_value[length_all:]], axis=1)
        held.value = jnp.sum(grad_value.astype(f32), axis=0, keepdims=True)

    def query_grads():
        grad_query = jnp.concatenate(
            [
                matmul(k_turned[:HEAD_DIM, :], d_scores[0]),
                matmul(k_turned[HEAD_DIM:, :], d_scores[1]),
            ],
            axis=0,
        ) * (HEAD_DIM**-0.5)
        grad_query = grad_query.T.astype(bf16)
        joined[:, :LANES] = grad_query
        held.query = jnp.sum(grad_query.astype(f32), axis=0, keepdims=True)

    def input_part(mirror, order):
        for place, offset in enumerate(order):
            rows = span_rows(flipped(ctx, offset ^ mirror, 3))
            dx_part[
                4 * (mirror == 0) + place
            ] = back_product(joined[rows, :], w_heads[...]).astype(bf16)

    def two(ref, first):
        return ref.at[pl.ds(first, 2)]

    def input_far():
        input_part(6, (0, 2, 1, 3))
        held.far_y = copies.send(two(dx_part, 2), two(dx_got, 0), ctx_peer(1))

    def input_near():
        input_part(0, (0, 2, 1, 3))
        held.near_y = copies.send(two(dx_part, 6), two(dx_got, 2), ctx_peer(1))

    def input_far_z():
        held.far_y.wait()
        add_rows(two(dx_part, 0), two(dx_got, 0))
        held.far_z = copies.send(dx_part.at[1], dx_got.at[4], ctx_peer(2))

    def input_near_z():
        held.near_y.wait()
        add_rows(two(dx_part, 4), two(dx_got, 2))
        held.near_z = copies.send(dx_part.at[5], dx_got.at[5], ctx_peer(2))

    def input_cross():
        held.far_z.wait()
        add_rows(dx_got.at[4], dx_part.at[0])
        held.cross = copies.send(dx_got.at[4], dx_far, ctx_peer(6))

    def write_input_rows(index, parts):
        rows = span_rows(index)
        total = in_grad[rows, :]
        for part in parts:
            total = total + part.astype(f32)
        in_grad[rows, :] = total
        input_items.append((in_grad.at[rows], o_input.at[rows]))
        if len(input_items) == 2:
            out_copies.append(copies.keep(input_items, in_grad))

    def input_near_out():
        held.near_z.wait()
        write_input_rows(upper, (dx_part[4], dx_got[5]))

    def input_far_out():
        held.cross.wait()
        write_input_rows(1 - upper, (dx_far[...],))

    def memory_part():
        mem_part[pair] = back_product(held.memory, w_heads[:, LANES:]).astype(bf16)
        held.mem = copies.send_all(
            [(mem_part.at[pair], mem_part.at[pair], ctx_peer(offset)) for offset in (3, 2, 1)],
            mem_part.at[pl.ds(0, 3)],
        )

    def memory_cross():
        held.mem.wait()
        mem_far[upper] = (
            mem_part[0].astype(f32)
            + mem_part[1].astype(f32)
            + mem_part[2].astype(f32)
            + mem_part[3].astype(f32)
        ).astype(bf16)
        held.mem_far = copies.send(mem_far.at[upper], mem_far.at[upper], ctx_peer(6))

    def memory_out():
        held.mem_far.wait()
        out_copies.append(copies.keep([(mem_far, o_mem)], mem_far))

    def head_grads():
        grad_heads = matmul(tokens_t[...], joined[...])
        mem_grad = outer_sum(own_mem[upper], held.memory)
        for owner in range(4):
            rows = slice(owner * LANES, (owner + 1) * LANES)
            head_part[owner, :LANES, :LANES] = grad_heads[rows, :LANES].astype(bf16)
            head_part[owner, :LANES, LANES:] = (grad_heads[rows, LANES:] + mem_grad[rows]).astype(
                bf16
            )
            mine = pair == owner
            vec_part[owner, 0:1, :] = jnp.where(mine, held.query, 0.0)
            vec_part[owner, 1:2, :] = jnp.where(mine, held.value, 0.0)
            head_part[owner, LANES:, :] = jnp.zeros((ROW_KINDS, 3 * LANES), bf16)
            head_part[owner, LANES:, :LANES] = vec_part[owner].astype(bf16)
        held.head_core = copies.send_all(
            [
                (head_part.at[2 * side + 1 - core], head_core.at[side], shard_peer(1))
                for side in range(2)
            ],
            head_core,
        )

    def head_x_send():
        held.head_core.wait()
        for side in range(2):
            add_rows(head_core.at[side], head_part.at[2 * side + core])
        held.head_x = copies.send(head_core.at[1 - x_half], head_x, shard_peer(2))

    def head_far_send():
        held.head_x.wait()
        add_rows(head_x, head_core.at[x_half])
        held.head_far = copies.send(head_x, head_far, ctx_peer(4))

    def head_gather():
        held.head_far.wait()
        head_all[pair] = (head_x[...].astype(f32) + head_far[...].astype(f32)).astype(bf16)
        held.heads = copies.send(head_all.at[pair], head_all.at[pair], ctx_peer(2))

    def head_spread():
        held.heads.wait()
        places = [head_all.at[index] for index in (pair, flipped(pair, 2, 2))]
        held.heads = copies.send_all(
            [(place, place, ctx_peer(1)) for place in places], head_all.at[pl.ds(0, 2)]
        )

    def head_out():
        held.heads.wait()
        out_copies.append(copies.keep([(head_all, o_heads)], head_all))

    def rms_out():
        held.squares.wait()
        row_id = lax.broadcasted_iota(jnp.int32, (8, LANES), 0)
        total = squares[0]
        for other in range(1, spans):
            total = total + squares[other]
        valid_tokens = jnp.where(row_id < 3, len_ref[0], len_ref[1]).astype(f32)
        rms_rows[...] = jnp.sqrt(total / (valid_tokens * width))
        out_copies.append(copies.keep([(rms_rows, o_rms)], rms_rows))

    second_norm()
    outer_part(0)
    outer_part(1)
    outer_part(2)
    outer_part(3)
    first_norm()
    attended_grad()
    outer_part(4)
    outer_part(5)
    outer_part(6)
    square_sums()
    narrow_grads()
    halve(0, 0)
    halve(1, 0)
    halve(2, 0)
    halve(3, 0)
    halve(4, 0)
    halve(5, 0)
    halve(0, 1)
    halve(6, 0)
    halve(2, 1)
    deltas()
    scores_0()
    halve(1, 1)
    scores_1()
    halve(3, 1)
    key_value_grads()
    halve(0, 2)
    halve(4, 1)
    query_grads()
    halve(2, 2)
    input_far()
    halve(3, 2)
    halve(5, 1)
    halve(6, 1)
    input_near()
    memory_part()
    cross(0)
    head_grads()
    halve(1, 2)
    cross(2)
    cross(3)
    halve(6, 2)
    halve(4, 2)
    gather(0, 0)
    head_x_send()
    cross(1)
    cross(6)
    gather(2, 0)
    gather(3, 0)
    cross(4)
    gather(0, 1)
    gather(1, 0)
    head_far_send()
    input_far_z()
    gather(6, 0)
    gather(2, 1)
    gather(3, 1)
    halve(5, 2)
    gather(4, 0)
    cross(5)
    input_cross()
    head_gather()
    input_near_z()
    gather(6, 1)
    memory_cross()
    gather(4, 1)
    write_out(0)
    gather(1, 1)
    gather(5, 0)
    write_out(2)
    write_out(3)
    write_out(6)
    input_far_out()
    head_spread()
    write_out(4)
    gather(5, 1)
    input_near_out()
    memory_out()
    rms_out()
    write_out(1)
    head_out()
    write_out(5)
    for copy in out_copies:
        copy.wait()
    copies.finish()
    assert (len(copies.sent), copies.received, copies.kept) == (SENDS, ARRIVALS, KEPT)


def outputs_kernel(layer, input_grad, mem_grad, weights, heads, rms, *outs):
    f32 = jnp.float32
    (
        o_layer,
        o_input,
        o_mem,
        o_query,
        o_key,
        o_value,
        o_out,
        o_up,
        o_down,
        o_b_query,
        o_b_value,
        o_b_out,
        o_b_up,
        o_b_down,
        o_first_gain,
        o_first_bias,
        o_second_gain,
        o_second_bias,
        o_rms,
    ) = outs
    width = weights.shape[1]
    o_layer[...] = layer[...].reshape(o_layer.shape)
    o_input[...] = input_grad[...].reshape(o_input.shape)
    for seq in range(o_mem.shape[1]):
        o_mem[:, seq, :] = mem_grad[seq].astype(f32)[:MEM_ROWS]
    o_down[...] = weights[:width, :].astype(f32)
    for chunk in range(4):
        o_up[:, chunk * width : (chunk + 1) * width] = weights[
            width + chunk * LANES : width + (chunk + 1) * LANES, :
        ].astype(f32)
    o_out[...] = weights[2 * width :, :].astype(f32)
    for owner in range(4):
        for part, ref in enumerate((o_query, o_key, o_value)):
            ref[:, owner * LANES : (owner + 1) * LANES] = heads[
                owner, :LANES, part * LANES : (part + 1) * LANES
            ].astype(f32)
    vec = (
        heads[0, LANES:, :LANES].astype(f32)
        + heads[1, LANES:, :LANES].astype(f32)
        + heads[2, LANES:, :LANES].astype(f32)
        + heads[3, LANES:, :LANES].astype(f32)
    )
    narrow = (
        o_b_query,
        o_b_value,
        o_b_out,
        o_b_down,
        o_first_gain,
        o_first_bias,
        o_second_gain,
        o_second_bias,
    )
    for kind, ref in enumerate(narrow):
        ref[...] = vec[kind]
    for piece in range(4):
        o_b_up[piece * LANES : (piece + 1) * LANES] = vec[8 + piece]
    for seq in range(o_rms.shape[0]):
        for kind in range(3):
            o_rms[seq : seq + 1, kind : kind + 1] = rms[seq * 3 + kind : seq * 3 + kind + 1, :1]


def fast_layer(
    inputs,
    memory,
    lengths,
    w_query,
    w_key,
    w_value,
    w_out,
    w_up,
    w_down,
    b_query,
    b_value,
    b_out,
    b_up,
    b_down,
    first_gain,
    first_bias,
    second_gain,
    second_bias,
    out_grad,
):
    bf16, f32 = jnp.bfloat16, jnp.float32
    seqs, span, width = inputs.shape
    length_all, keys = 8 * span, 8 * span + MEM_PAD
    hidden_width = w_up.shape[1]
    narrow = (b_query, b_value, b_out, b_down, first_gain, first_bias, second_gain, second_bias)
    vmem, anywhere = pl.BlockSpec(memory_space=pltpu.VMEM), pl.BlockSpec(memory_space=pl.ANY)
    smem = pl.BlockSpec(memory_space=pltpu.SMEM)
    stacked = 2 * width + LANES
    scratch = [
        ((seqs, span, width), bf16),
        ((seqs, span, width), bf16),
        ((seqs, MEM_PAD, width), bf16),
        ((memory.shape[1], seqs, width), bf16),
        *[(ref.shape, bf16) for ref in (*narrow, b_up)],
        ((8, LANES), f32),
        ((seqs * span, width), bf16),
        ((length_all, 3 * LANES), bf16),
        ((seqs * span, width), bf16),
        ((seqs * span, width), f32),
        ((length_all, width), bf16),
        ((width, length_all), bf16),
        ((width, 3 * LANES), bf16),
        ((width, width), bf16),
        ((width, hidden_width), bf16),
        ((hidden_width, width), bf16),
        ((4, ROW_KINDS, LANES), f32),
        ((length_all, LANES), bf16),
        ((2, length_all, LANES), bf16),
        ((2, keys, LANES), bf16),
        ((2, keys, LANES), bf16),
        ((LANES, keys), bf16),
        ((LANES, keys), bf16),
        ((2, keys, length_all), bf16),
        ((2, keys, length_all), bf16),
        ((LANES, length_all), f32),
        ((8, length_all), f32),
        ((length_all, LANES), bf16),
        ((LANES, length_all), bf16),
        ((length_all, LANES), bf16),
        ((seqs * span, width), bf16),
        ((seqs * span, hidden_width), bf16),
        ((seqs * span, hidden_width), f32),
        ((seqs * span, hidden_width), bf16),
        ((seqs * span, width), bf16),
        ((length_all, LANES), bf16),
        ((4, stacked, width), bf16),
        ((2, stacked, width), bf16),
        ((stacked, width), bf16),
        ((stacked // 2, width), bf16),
        ((stacked // 4, width), bf16),
        ((stacked // 4, width), bf16),
        ((stacked, width), bf16),
        ((4, LANES + ROW_KINDS, 3 * LANES), bf16),
        ((2, LANES + ROW_KINDS, 3 * LANES), bf16),
        ((LANES + ROW_KINDS, 3 * LANES), bf16),
        ((LANES + ROW_KINDS, 3 * LANES), bf16),
        ((4, LANES + ROW_KINDS, 3 * LANES), bf16),
        ((4, ROW_KINDS, LANES), f32),
        ((8, span, width), bf16),
        ((6, span, width), bf16),
        ((span, width), bf16),
        ((4, MEM_PAD, width), bf16),
        ((2, MEM_PAD, width), bf16),
        ((8, 8, LANES), f32),
    ]
    made = pl.pallas_call(
        layer_kernel,
        out_shape=[
            jax.ShapeDtypeStruct((seqs * span, width), bf16),
            jax.ShapeDtypeStruct((seqs * span, width), f32),
            jax.ShapeDtypeStruct((seqs, MEM_PAD, width), bf16),
            jax.ShapeDtypeStruct((stacked, width), bf16),
            jax.ShapeDtypeStruct((4, LANES + ROW_KINDS, 3 * LANES), bf16),
            jax.ShapeDtypeStruct((8, LANES), f32),
        ],
        in_specs=[anywhere] * 3 + [smem] + [anywhere] * 15,
        out_specs=[anywhere] * 6,
        scratch_shapes=[pltpu.VMEM(shape, kind) for shape, kind in scratch]
        + [pltpu.SemaphoreType.DMA((count,)) for count in (SENDS, ARRIVALS, KEPT)],
        compiler_params=pltpu.CompilerParams(
            collective_id=0, has_side_effects=True, vmem_limit_bytes=60 * 2**20
        ),
        name="layer",
    )(
        inputs,
        out_grad,
        memory.transpose(1, 0, 2),
        lengths,
        w_query,
        w_key,
        w_value,
        w_out,
        w_up,
        w_down,
        *narrow,
        b_up,
    )
    mem_rows = memory.shape[1]
    shapes = (
        ((seqs, span, width), bf16),
        ((seqs, span, width), f32),
        ((mem_rows, seqs, width), f32),
        (w_query.shape, f32),
        (w_key.shape, f32),
        (w_value.shape, f32),
        (w_out.shape, f32),
        (w_up.shape, f32),
        (w_down.shape, f32),
        (b_query.shape, f32),
        (b_value.shape, f32),
        (b_out.shape, f32),
        (b_up.shape, f32),
        (b_down.shape, f32),
        (first_gain.shape, f32),
        (first_bias.shape, f32),
        (second_gain.shape, f32),
        (second_bias.shape, f32),
        ((seqs, 3), f32),
    )
    outs = pl.pallas_call(
        outputs_kernel,
        out_shape=[jax.ShapeDtypeStruct(shape, kind) for shape, kind in shapes],
        in_specs=[vmem] * 6,
        out_specs=[vmem] * len(shapes),
        compiler_params=pltpu.CompilerParams(vmem_limit_bytes=60 * 2**20),
        name="outputs",
    )(*made)
    return (*outs[:2], outs[2].transpose(1, 0, 2), *outs[3:])


def takes_fast_plan(mesh, inputs, memory, w_up):
    return (
        mesh.shape["shard"] == 4
        and mesh.shape["ctx"] == 8
        and inputs.shape == (2, LANES, HEADS * HEAD_DIM)
        and memory.shape[1] == MEM_ROWS
        and w_up.shape == (LANES, 4 * HEADS * HEAD_DIM)
    )


def solution(mesh):
    in_specs = (
        P("shard", "ctx", None),
        P("shard", None, None),
        P("shard"),
        P("shard", None),
        P("shard", None),
        P("shard", None),
        P("shard", None),
        P("shard", None),
        P("shard", None),
        P("shard"),
        P("shard"),
        P("shard"),
        P("shard"),
        P("shard"),
        P("shard"),
        P("shard"),
        P("shard"),
        P("shard"),
        P("shard", "ctx", None),
    )
    out_specs = (
        P("shard", "ctx", None),
        P("shard", "ctx", None),
        P("shard", None, None),
        P("shard", None),
        P("shard", None),
        P("shard", None),
        P("shard", None),
        P("shard", None),
        P("shard", None),
        P("shard"),
        P("shard"),
        P("shard"),
        P("shard"),
        P("shard"),
        P("shard"),
        P("shard"),
        P("shard"),
        P("shard"),
        P("shard", None),
    )

    def layer(*arrays):
        if takes_fast_plan(mesh, arrays[0], arrays[1], arrays[7]):
            return fast_layer(*arrays)
        return local(*arrays)

    return jax.shard_map(layer, mesh=mesh, in_specs=in_specs, out_specs=out_specs, check_vma=False)
```

```python
import math

import jax
import jax.numpy as jnp
from jax import lax
from jax.experimental import pallas as pl
from jax.experimental.pallas import tpu as pltpu
from jax.sharding import PartitionSpec as P

HEADS = 8
HEAD_DIM = 64
MEM_ROWS = 20
GELU_SCALE = math.sqrt(2 / math.pi)


eps = 1e-05


def matmul(operand, second):
    return jnp.dot(operand, second, preferred_element_type=jnp.float32)


def outer_sum(operand, second):
    return lax.dot_general(
        operand, second, (((0,), (0,)), ((), ())), preferred_element_type=jnp.float32
    )


def back_product(operand, second):
    return lax.dot_general(
        operand, second, (((1,), (1,)), ((), ())), preferred_element_type=jnp.float32
    )


def to_float(tensor):
    return tensor.astype(jnp.float32)


def smooth_act(values):
    return jax.nn.gelu(values, approximate=True)


def split_heads(tensor):
    return tensor.reshape(tensor.shape[0], tensor.shape[1], HEADS, HEAD_DIM)


def head_scores(queries, key_heads):
    return jnp.einsum(
        "sqhd,skhd->sqhk", queries, key_heads, preferred_element_type=jnp.float32
    ) * HEAD_DIM ** (-0.5)


def norm_forward(matrix, gain, offset):
    row_mean = jnp.mean(matrix, axis=-1, keepdims=True)
    centered = matrix - row_mean
    inverse = lax.rsqrt(jnp.mean(centered * centered, axis=-1, keepdims=True) + eps)
    unit_rows = centered * inverse
    return (unit_rows * gain + offset, unit_rows, inverse)


def norm_backward(cotangent, unit_rows, inverse, gain):
    scaled = cotangent * gain
    centered_grad = (
        scaled
        - jnp.mean(scaled, axis=-1, keepdims=True)
        - unit_rows * jnp.mean(scaled * unit_rows, axis=-1, keepdims=True)
    )
    return (
        inverse * centered_grad,
        jnp.sum(cotangent * unit_rows, axis=0),
        jnp.sum(cotangent, axis=0),
    )


def in_blocks(update, carried, arrays, first_row, slice_dim):
    piece_rows = arrays[0].shape[slice_dim]
    block_len = math.gcd(piece_rows, 1024)
    if block_len == piece_rows:
        return update(carried, arrays, first_row)

    def one_block(current, number):
        block_start = number * block_len
        sliced = tuple(
            (
                lax.dynamic_slice_in_dim(tensor, block_start, block_len, slice_dim)
                for tensor in arrays
            )
        )
        return (update(current, sliced, first_row + block_start), None)

    carried, unused = lax.scan(
        one_block, carried, jnp.arange(piece_rows // block_len, dtype=jnp.int32)
    )
    return carried


def softmax_update(carried, pieces, first_row, queries, lengths):
    row_max, row_total, weighted = carried
    key_piece, value_piece = pieces
    piece_rows = key_piece.shape[1]
    scores = head_scores(queries, split_heads(key_piece))
    key_mask = (first_row + jnp.arange(piece_rows, dtype=jnp.int32))[None, :] < lengths[:, None]
    scores = jnp.where(key_mask[:, None, None, :], scores, -1e30)
    new_max = jnp.maximum(row_max, jnp.max(scores, axis=-1))
    factor = jnp.exp(row_max - new_max)
    exponent = jnp.exp(scores - new_max[..., None])
    row_total = row_total * factor + jnp.sum(exponent, axis=-1)
    weighted = weighted * factor[..., None] + jnp.einsum(
        "sqhk,skhd->sqhd",
        exponent.astype(jnp.bfloat16),
        split_heads(value_piece),
        preferred_element_type=jnp.float32,
    )
    return (new_max, row_total, weighted)


def query_update(grad_q, pieces, first_row, queries, grad_heads, log_total, row_delta, lengths):
    key_piece, value_piece = pieces
    piece_rows = key_piece.shape[1]
    key_heads = split_heads(key_piece)
    scores = head_scores(queries, key_heads)
    key_mask = (first_row + jnp.arange(piece_rows, dtype=jnp.int32))[None, :] < lengths[:, None]
    scores = jnp.where(key_mask[:, None, None, :], scores, -1e30)
    attn_probs = jnp.exp(scores - log_total[..., None])
    value_dots = jnp.einsum(
        "sqhd,skhd->sqhk", grad_heads, split_heads(value_piece), preferred_element_type=jnp.float32
    )
    d_scores = (attn_probs * (value_dots - row_delta[..., None])).astype(jnp.bfloat16)
    return grad_q + jnp.einsum(
        "sqhk,skhd->sqhd", d_scores, key_heads, preferred_element_type=jnp.float32
    ) * HEAD_DIM ** (-0.5)


def key_update(carried, pieces, first_row, key_heads, value_heads, log_all, delta_all, key_mask):
    grad_k, grad_v = carried
    query_piece, grad_piece = pieces
    piece_rows = query_piece.shape[1]
    log_total = lax.dynamic_slice_in_dim(log_all, first_row, piece_rows, 1)
    row_delta = lax.dynamic_slice_in_dim(delta_all, first_row, piece_rows, 1)
    queries = split_heads(query_piece)
    grad_heads = split_heads(grad_piece)
    scores = head_scores(queries, key_heads)
    scores = jnp.where(key_mask[:, None, None, :], scores, -1e30)
    attn_probs = jnp.exp(scores - log_total[..., None])
    grad_v = grad_v + jnp.einsum(
        "sqhk,sqhd->skhd",
        attn_probs.astype(jnp.bfloat16),
        grad_heads,
        preferred_element_type=jnp.float32,
    )
    value_dots = jnp.einsum(
        "sqhd,skhd->sqhk", grad_heads, value_heads, preferred_element_type=jnp.float32
    )
    d_scores = (attn_probs * (value_dots - row_delta[..., None])).astype(jnp.bfloat16)
    grad_k = grad_k + jnp.einsum(
        "sqhk,sqhd->skhd", d_scores, queries, preferred_element_type=jnp.float32
    ) * HEAD_DIM ** (-0.5)
    return (grad_k, grad_v)


def local(
    inputs,
    memory,
    lengths,
    w_query,
    w_key,
    w_value,
    w_out,
    w_up,
    w_down,
    b_query,
    b_value,
    b_out,
    b_up,
    b_down,
    first_gain,
    first_bias,
    second_gain,
    second_bias,
    out_grad,
):
    gathered = (
        lax.all_gather(w_query, "shard", axis=0, tiled=True),
        lax.all_gather(w_key, "shard", axis=0, tiled=True),
        lax.all_gather(w_value, "shard", axis=0, tiled=True),
        lax.all_gather(w_out, "shard", axis=0, tiled=True),
        lax.all_gather(w_up, "shard", axis=0, tiled=True),
        lax.all_gather(w_down, "shard", axis=0, tiled=True),
        lax.all_gather(b_query, "shard", axis=0, tiled=True),
        lax.all_gather(b_value, "shard", axis=0, tiled=True),
        lax.all_gather(b_out, "shard", axis=0, tiled=True),
        lax.all_gather(b_up, "shard", axis=0, tiled=True),
        lax.all_gather(b_down, "shard", axis=0, tiled=True),
        lax.all_gather(first_gain, "shard", axis=0, tiled=True),
        lax.all_gather(first_bias, "shard", axis=0, tiled=True),
        lax.all_gather(second_gain, "shard", axis=0, tiled=True),
        lax.all_gather(second_bias, "shard", axis=0, tiled=True),
    )
    (
        full_query,
        full_key,
        full_value,
        full_out,
        full_up,
        full_down,
        bias_query,
        bias_value,
        bias_out,
        bias_up,
        bias_down,
        gain_one,
        offset_one,
        gain_two,
        offset_two,
    ) = gathered
    seq_count, local_len, features = inputs.shape
    mem_rows = memory.shape[1]
    token_rows = inputs.reshape(seq_count * local_len, features)
    mem_flat = memory.reshape(seq_count * mem_rows, features)
    query = (
        (matmul(token_rows, full_query) + to_float(bias_query))
        .astype(jnp.bfloat16)
        .reshape(seq_count, local_len, features)
    )
    key = matmul(token_rows, full_key).astype(jnp.bfloat16).reshape(seq_count, local_len, features)
    value = (
        (matmul(token_rows, full_value) + to_float(bias_value))
        .astype(jnp.bfloat16)
        .reshape(seq_count, local_len, features)
    )
    mem_key = matmul(mem_flat, full_key).astype(jnp.bfloat16).reshape(seq_count, mem_rows, features)
    mem_value = (
        (matmul(mem_flat, full_value) + to_float(bias_value))
        .astype(jnp.bfloat16)
        .reshape(seq_count, mem_rows, features)
    )
    query_heads = split_heads(query)
    mem_key_heads = split_heads(mem_key)
    mem_value_heads = split_heads(mem_value)
    position_zero = lax.axis_index("ctx") * local_len
    key_mask = (position_zero + jnp.arange(local_len, dtype=jnp.int32))[None, :] < lengths[:, None]
    mem_scores = head_scores(query_heads, mem_key_heads)
    mem_max = jnp.max(mem_scores, axis=-1)
    mem_exponent = jnp.exp(mem_scores - mem_max[..., None])
    start_state = (
        mem_max,
        jnp.sum(mem_exponent, axis=-1),
        jnp.einsum(
            "sqhk,skhd->sqhd",
            mem_exponent.astype(jnp.bfloat16),
            mem_value_heads,
            preferred_element_type=jnp.float32,
        ),
    )

    def forward_step(carried, pieces, first_row):
        return softmax_update(carried, pieces, first_row, query_heads, lengths)

    row_max, row_total, weighted = in_blocks(
        forward_step,
        start_state,
        (
            lax.all_gather(key, "ctx", axis=1, tiled=True),
            lax.all_gather(value, "ctx", axis=1, tiled=True),
        ),
        jnp.int32(0),
        1,
    )
    log_total = row_max + jnp.log(row_total)
    attended_full = (weighted / row_total[..., None]).reshape(seq_count, local_len, features)
    attended = attended_full.astype(jnp.bfloat16).reshape(seq_count * local_len, features)
    branch = matmul(attended, full_out) + to_float(bias_out)
    normed, unit_one, inverse_one = norm_forward(
        to_float(token_rows) + branch, to_float(gain_one), to_float(offset_one)
    )
    normed_low = normed.astype(jnp.bfloat16)
    pre_act = matmul(normed_low, full_up) + to_float(bias_up)
    activated, act_pullback = jax.vjp(smooth_act, pre_act)
    hidden = activated.astype(jnp.bfloat16)
    ffn_out = matmul(hidden, full_down) + to_float(bias_down)
    output_rows, unit_two, inverse_two = norm_forward(
        normed + ffn_out, to_float(gain_two), to_float(offset_two)
    )
    layer_out = output_rows.astype(jnp.bfloat16).reshape(seq_count, local_len, features)
    valid_rows = key_mask.astype(jnp.float32)
    input_squares = jnp.sum(jnp.square(to_float(inputs)), axis=2)
    branch_squares = jnp.sum(jnp.square(branch), axis=1).reshape(seq_count, local_len)
    ffn_squares = jnp.sum(jnp.square(ffn_out), axis=1).reshape(seq_count, local_len)
    squares = jnp.stack(
        [
            jnp.sum(valid_rows * input_squares, axis=1),
            jnp.sum(valid_rows * branch_squares, axis=1),
            jnp.sum(valid_rows * ffn_squares, axis=1),
        ],
        axis=1,
    )
    squares = lax.psum(squares, "ctx")
    stream_rms = jnp.sqrt(squares / (lengths.astype(jnp.float32)[:, None] * features))
    back_query, back_key, back_value, back_out, back_up, back_down, back_gain_one, back_gain_two = (
        lax.all_gather(w_query, "shard", axis=0, tiled=True),
        lax.all_gather(w_key, "shard", axis=0, tiled=True),
        lax.all_gather(w_value, "shard", axis=0, tiled=True),
        lax.all_gather(w_out, "shard", axis=0, tiled=True),
        lax.all_gather(w_up, "shard", axis=0, tiled=True),
        lax.all_gather(w_down, "shard", axis=0, tiled=True),
        lax.all_gather(first_gain, "shard", axis=0, tiled=True),
        lax.all_gather(second_gain, "shard", axis=0, tiled=True),
    )
    cotangent = to_float(out_grad).reshape(seq_count * local_len, features)
    grad_two, grad_gain_two, grad_offset_two = norm_backward(
        cotangent, unit_two, inverse_two, to_float(back_gain_two)
    )
    grad_ffn = grad_two.astype(jnp.bfloat16)
    grad_bias_down = jnp.sum(grad_ffn, axis=0, dtype=jnp.float32)
    grad_full_down = outer_sum(hidden, grad_ffn)
    grad_hidden = back_product(grad_ffn, back_down)
    grad_pre = act_pullback(grad_hidden)[0].astype(jnp.bfloat16)
    grad_bias_up = jnp.sum(grad_pre, axis=0, dtype=jnp.float32)
    grad_full_up = outer_sum(normed_low, grad_pre)
    grad_normed = grad_two + back_product(grad_pre, back_up)
    grad_one, grad_gain_one, grad_offset_one = norm_backward(
        grad_normed, unit_one, inverse_one, to_float(back_gain_one)
    )
    grad_branch = grad_one.astype(jnp.bfloat16)
    grad_bias_out = jnp.sum(grad_branch, axis=0, dtype=jnp.float32)
    grad_full_out = outer_sum(attended, grad_branch)
    grad_att = (
        back_product(grad_branch, back_out)
        .astype(jnp.bfloat16)
        .reshape(seq_count, local_len, features)
    )
    row_delta = jnp.sum(
        (to_float(grad_att) * attended_full).reshape(seq_count, local_len, HEADS, HEAD_DIM), axis=-1
    )
    log_all, delta_all = (
        lax.all_gather(log_total, "ctx", axis=1, tiled=True),
        lax.all_gather(row_delta, "ctx", axis=1, tiled=True),
    )
    grad_heads = split_heads(grad_att)
    mem_probs = jnp.exp(head_scores(query_heads, mem_key_heads) - log_total[..., None])
    mem_dots = jnp.einsum(
        "sqhd,skhd->sqhk", grad_heads, mem_value_heads, preferred_element_type=jnp.float32
    )
    mem_dscores = (mem_probs * (mem_dots - row_delta[..., None])).astype(jnp.bfloat16)
    start_query = jnp.einsum(
        "sqhk,skhd->sqhd", mem_dscores, mem_key_heads, preferred_element_type=jnp.float32
    ) * HEAD_DIM ** (-0.5)
    mem_grad_key = jnp.einsum(
        "sqhk,sqhd->skhd", mem_dscores, query_heads, preferred_element_type=jnp.float32
    ) * HEAD_DIM ** (-0.5)
    mem_grad_value = jnp.einsum(
        "sqhk,sqhd->skhd",
        mem_probs.astype(jnp.bfloat16),
        grad_heads,
        preferred_element_type=jnp.float32,
    )
    key_heads = split_heads(key)
    value_heads = split_heads(value)
    empty_grads = jnp.zeros(key_heads.shape, jnp.float32)

    def query_step(carried, pieces, first_row):
        return query_update(
            carried, pieces, first_row, query_heads, grad_heads, log_total, row_delta, lengths
        )

    def key_step(carried, pieces, first_row):
        return key_update(
            carried, pieces, first_row, key_heads, value_heads, log_all, delta_all, key_mask
        )

    grad_q = in_blocks(
        query_step,
        start_query,
        (
            lax.all_gather(key, "ctx", axis=1, tiled=True),
            lax.all_gather(value, "ctx", axis=1, tiled=True),
        ),
        jnp.int32(0),
        1,
    )
    grad_k, grad_v = in_blocks(
        key_step,
        (empty_grads, empty_grads),
        (
            lax.all_gather(query, "ctx", axis=1, tiled=True),
            lax.all_gather(grad_att, "ctx", axis=1, tiled=True),
        ),
        jnp.int32(0),
        1,
    )
    mem_key_sum, mem_value_sum = lax.psum((mem_grad_key, mem_grad_value), "ctx")
    mem_key_low = mem_key_sum.reshape(seq_count * mem_rows, features).astype(jnp.bfloat16)
    mem_value_low = mem_value_sum.reshape(seq_count * mem_rows, features).astype(jnp.bfloat16)
    first_only = (lax.axis_index("ctx") == 0).astype(jnp.float32)
    grad_q_low = grad_q.reshape(seq_count * local_len, features).astype(jnp.bfloat16)
    grad_k_low = grad_k.reshape(seq_count * local_len, features).astype(jnp.bfloat16)
    grad_v_low = grad_v.reshape(seq_count * local_len, features).astype(jnp.bfloat16)
    grad_full_query = outer_sum(token_rows, grad_q_low)
    grad_full_key = outer_sum(token_rows, grad_k_low) + first_only * outer_sum(
        mem_flat, mem_key_low
    )
    grad_full_value = outer_sum(token_rows, grad_v_low) + first_only * outer_sum(
        mem_flat, mem_value_low
    )
    grad_bias_query = jnp.sum(grad_q_low, axis=0, dtype=jnp.float32)
    grad_bias_value = jnp.sum(grad_v_low, axis=0, dtype=jnp.float32) + first_only * jnp.sum(
        mem_value_low, axis=0, dtype=jnp.float32
    )
    input_grad = (
        grad_one
        + back_product(grad_q_low, back_query)
        + back_product(grad_k_low, back_key)
        + back_product(grad_v_low, back_value)
    ).reshape(seq_count, local_len, features)
    memory_grad = (
        back_product(mem_key_low, back_key) + back_product(mem_value_low, back_value)
    ).reshape(seq_count, mem_rows, features)
    owned_parts = (
        lax.psum_scatter(
            grad_full_query.astype(jnp.bfloat16), "shard", scatter_dimension=0, tiled=True
        ).astype(jnp.float32),
        lax.psum_scatter(
            grad_full_key.astype(jnp.bfloat16), "shard", scatter_dimension=0, tiled=True
        ).astype(jnp.float32),
        lax.psum_scatter(
            grad_full_value.astype(jnp.bfloat16), "shard", scatter_dimension=0, tiled=True
        ).astype(jnp.float32),
        lax.psum_scatter(
            grad_full_out.astype(jnp.bfloat16), "shard", scatter_dimension=0, tiled=True
        ).astype(jnp.float32),
        lax.psum_scatter(
            grad_full_up.astype(jnp.bfloat16), "shard", scatter_dimension=0, tiled=True
        ).astype(jnp.float32),
        lax.psum_scatter(
            grad_full_down.astype(jnp.bfloat16), "shard", scatter_dimension=0, tiled=True
        ).astype(jnp.float32),
        lax.psum_scatter(
            grad_bias_query.astype(jnp.bfloat16), "shard", scatter_dimension=0, tiled=True
        ).astype(jnp.float32),
        lax.psum_scatter(
            grad_bias_value.astype(jnp.bfloat16), "shard", scatter_dimension=0, tiled=True
        ).astype(jnp.float32),
        lax.psum_scatter(
            grad_bias_out.astype(jnp.bfloat16), "shard", scatter_dimension=0, tiled=True
        ).astype(jnp.float32),
        lax.psum_scatter(
            grad_bias_up.astype(jnp.bfloat16), "shard", scatter_dimension=0, tiled=True
        ).astype(jnp.float32),
        lax.psum_scatter(
            grad_bias_down.astype(jnp.bfloat16), "shard", scatter_dimension=0, tiled=True
        ).astype(jnp.float32),
        lax.psum_scatter(
            grad_gain_one.astype(jnp.bfloat16), "shard", scatter_dimension=0, tiled=True
        ).astype(jnp.float32),
        lax.psum_scatter(
            grad_offset_one.astype(jnp.bfloat16), "shard", scatter_dimension=0, tiled=True
        ).astype(jnp.float32),
        lax.psum_scatter(
            grad_gain_two.astype(jnp.bfloat16), "shard", scatter_dimension=0, tiled=True
        ).astype(jnp.float32),
        lax.psum_scatter(
            grad_offset_two.astype(jnp.bfloat16), "shard", scatter_dimension=0, tiled=True
        ).astype(jnp.float32),
    )
    (
        part_query,
        part_key,
        part_value,
        part_out,
        part_up,
        part_down,
        part_bias_query,
        part_bias_value,
        part_bias_out,
        part_bias_up,
        part_bias_down,
        part_gain_one,
        part_offset_one,
        part_gain_two,
        part_offset_two,
    ) = owned_parts
    summed_grads = lax.psum(
        (
            part_query,
            part_key,
            part_value,
            part_out,
            part_up,
            part_down,
            part_bias_query,
            part_bias_value,
            part_bias_out,
            part_bias_up,
            part_bias_down,
            part_gain_one,
            part_offset_one,
            part_gain_two,
            part_offset_two,
        ),
        "ctx",
    )
    (
        sum_query,
        sum_key,
        sum_value,
        sum_out,
        sum_up,
        sum_down,
        sum_bias_query,
        sum_bias_value,
        sum_bias_out,
        sum_bias_up,
        sum_bias_down,
        sum_gain_one,
        sum_offset_one,
        sum_gain_two,
        sum_offset_two,
    ) = summed_grads
    return (
        layer_out,
        input_grad,
        memory_grad,
        sum_query,
        sum_key,
        sum_value,
        sum_out,
        sum_up,
        sum_down,
        sum_bias_query,
        sum_bias_value,
        sum_bias_out,
        sum_bias_up,
        sum_bias_down,
        sum_gain_one,
        sum_offset_one,
        sum_gain_two,
        sum_offset_two,
        stream_rms,
    )


MESH_ID = pl.DeviceIdType.MESH
LANES = 128
MEM_PAD = 32
ROW_KINDS = 16
SENDS, ARRIVALS, KEPT = 18, 89, 23
PIECES = ((128, 'xyz'), (128, 'zyx'), (128, 'yxz'), (128, 'yxz'), (256, 'xyz'), (256, 'zyx'), (128, 'yzx'))


def flipped(index, offset, bits):
    total = 0
    for bit in range(bits):
        digit = lax.rem(lax.div(index, 2**bit), 2)
        if offset >> bit & 1:
            digit = 1 - digit
        total = total + digit * 2**bit
    return total


class Copies:
    def __init__(self, send_sems, recv_sems, local_sems, measure):
        self.send_sems, self.recv_sems, self.local_sems = send_sems, recv_sems, local_sems
        self.measure = measure
        self.sent, self.alone, self.received, self.kept = [], [], 0, 0

    def send(self, src, dst, device):
        return self.send_all([(src, dst, device)], dst)

    def send_all(self, items, whole):
        rows = math.prod(whole.shape) * whole.dtype.itemsize // (2 * self.measure.shape[1])
        if rows % 16:
            pool = len(self.sent)
            self.sent.append(None)
            self.alone.append((pool, whole))
        else:
            pool = next(
                (
                    number
                    for number, held in enumerate(self.sent)
                    if held is not None and held + rows <= self.measure.shape[0]
                ),
                len(self.sent),
            )
            if pool == len(self.sent):
                self.sent.append(0)
            self.sent[pool] += rows
        arrival = self.recv_sems.at[self.received]
        self.received += 1
        for src, dst, device in items:
            pltpu.make_async_remote_copy(
                src_ref=src,
                dst_ref=dst,
                send_sem=self.send_sems.at[pool],
                recv_sem=arrival,
                device_id=device,
                device_id_type=MESH_ID,
            ).start()
        return Arrival(whole, arrival)

    def keep(self, items, whole):
        done = self.local_sems.at[self.kept]
        self.kept += 1
        for src, dst in items:
            pltpu.make_async_copy(src, dst, done).start()
        return Arrival(whole, done)

    def finish(self):
        for pool, whole in self.alone:
            Arrival(whole, self.send_sems.at[pool]).wait()
        for pool, rows in enumerate(self.sent):
            if rows is not None:
                Arrival(self.measure.at[pl.ds(0, rows)], self.send_sems.at[pool]).wait()


class Held:
    pass


class Arrival:
    def __init__(self, whole, semaphore):
        self.whole, self.semaphore = whole, semaphore

    def wait(self):
        pltpu.make_async_copy(self.whole, self.whole, self.semaphore).wait()


def layer_kernel(
    x_ref,
    g_ref,
    mem_ref,
    len_ref,
    wq_ref,
    wk_ref,
    wv_ref,
    wo_ref,
    wu_ref,
    wd_ref,
    *refs,
):
    vec_refs, refs = refs[:9], refs[9:]
    (o_layer, o_input, o_mem, o_fin, o_heads, o_rms), refs = refs[:6], refs[6:]
    (
        own_in,
        own_g,
        own_mem,
        mem_in,
        *rest,
    ) = refs
    narrow_in, rest = rest[:8], rest[8:]
    (
        wide_in,
        rms_rows,
        d_branch,
        joined,
        out_rows,
        in_grad,
        tokens,
        tokens_t,
        w_heads,
        w_out,
        w_up,
        w_down,
        vecs,
        q_scaled,
        q_aug,
        k_aug,
        v_mask,
        k_turned,
        v_turned,
        probs,
        d_scores,
        mixed_t,
        inverse_total,
        d_scaled,
        d_scaled_t,
        mixed,
        att,
        hidden,
        act_slope,
        d_pre,
        d_att,
        d_mixed,
        partial,
        got_core,
        got_first,
        got_second,
        got_third,
        got_far,
        final,
        head_part,
        head_core,
        head_x,
        head_far,
        head_all,
        vec_part,
        dx_part,
        dx_got,
        dx_far,
        mem_part,
        mem_far,
        squares,
        send_sems,
        recv_sems,
        local_sems,
    ) = rest
    bf16, f32 = jnp.bfloat16, jnp.float32
    shard, ctx = lax.axis_index("shard"), lax.axis_index("ctx")
    span, width = x_ref.shape[1], x_ref.shape[2]
    spans = 8
    length_all = span * spans
    keys = length_all + MEM_PAD
    x_half, core = lax.div(shard, 2), lax.rem(shard, 2)
    upper, pair = lax.div(ctx, 4), lax.rem(ctx, 4)
    y_side = lax.rem(ctx, 2)
    z_side = lax.rem(lax.div(ctx, 2) + upper, 2)

    def shard_peer(offset):
        return {"shard": flipped(shard, offset, 2), "ctx": ctx}

    def ctx_peer(offset):
        return {"shard": shard, "ctx": flipped(ctx, offset, 3)}

    def span_rows(index):
        return pl.ds(pl.multiple_of(index * span, span), span)

    def pair_lanes(index, size=LANES):
        return pl.ds(pl.multiple_of(index * LANES, LANES), size)

    copies = Copies(send_sems, recv_sems, local_sems, partial.at[0])

    barrier = pltpu.get_barrier_semaphore()
    for offset in (1, 2, 3):
        pl.semaphore_signal(barrier, inc=1, device_id=shard_peer(offset), device_id_type=MESH_ID)
    for offset in range(1, 8):
        pl.semaphore_signal(barrier, inc=1, device_id=ctx_peer(offset), device_id_type=MESH_ID)

    def aligned_rows(index, rows):
        return pl.ds(pl.multiple_of(index * rows, rows), rows)

    def rows_of(ref, index, start=0, rows=None):
        owned = ref.shape[0] // 4
        return ref.at[pl.ds(pl.multiple_of(index * owned + start, LANES), rows or owned)]

    my_rows = pl.ds(pl.multiple_of(shard * LANES, LANES), LANES)
    head_refs = (wq_ref, wk_ref, wv_ref)
    own_blocks = [
        copies.keep(
            [
                (
                    ref.at[:, pair_lanes(pair)],
                    w_heads.at[my_rows, pl.ds(part * LANES, LANES)],
                )
                for part, ref in enumerate(head_refs)
            ],
            w_heads.at[my_rows],
        ),
        copies.keep([(x_ref.at[upper], tokens.at[span_rows(ctx)])], own_in.at[0]),
    ]
    narrow_copies = [
        copies.keep([(ref, copied)], copied)
        for ref, copied in zip(vec_refs, (*narrow_in, wide_in))
    ]
    full_weights = ((wo_ref, w_out), (wd_ref, w_down), (wu_ref, w_up))
    own_weights = [
        copies.keep([(ref, rows_of(full, shard)) for ref, full in full_weights], partial.at[0]),
        copies.keep([(x_ref, own_in)], own_in),
        copies.keep([(g_ref, own_g)], own_g),
        copies.keep([(mem_ref, mem_in)], mem_in),
    ]
    pl.semaphore_wait(barrier, 10)

    partner = flipped(ctx, 6, 3)
    half_span = span // 2

    def half_rows(index, half):
        return pl.ds(pl.multiple_of(index * span + half * half_span, half_span), half_span)

    far_tokens = [
        copies.send(
            x_ref.at[1 - upper, pl.ds(half * half_span, half_span)],
            tokens.at[half_rows(ctx, half)],
            ctx_peer(6),
        )
        for half in range(2)
    ]
    def near_send(offsets):
        return copies.send_all(
            [
                (x_ref.at[upper], tokens.at[span_rows(ctx)], ctx_peer(offset))
                for offset in offsets
            ],
            tokens.at[pl.ds(0, span * len(offsets))],
        )

    near_pair, near_y = near_send((3, 2)), near_send((1,))

    def send_head_rows(offset):
        return copies.send_all(
            [
                (
                    ref.at[:, pair_lanes(pair)],
                    w_heads.at[my_rows, pl.ds(part * LANES, LANES)],
                    shard_peer(offset),
                )
                for part, ref in enumerate(head_refs)
            ],
            w_heads.at[my_rows],
        )

    x_heads = send_head_rows(2)
    core_heads = send_head_rows(1)
    for copy in narrow_copies:
        copy.wait()
    for kind, ref in enumerate((*narrow_in, wide_in)):
        values = ref[...].astype(f32)
        for piece in range(ref.shape[0] // LANES):
            vecs[shard, kind + piece : kind + piece + 1, :] = values[
                piece * LANES : (piece + 1) * LANES
            ].reshape(1, LANES)
    vec_copies = copies.send_all(
        [(vecs.at[shard], vecs.at[shard], shard_peer(offset)) for offset in (2, 3, 1)],
        vecs.at[pl.ds(0, 3)],
    )
    half_down = wd_ref.shape[0] // 2
    x_out = copies.send(wo_ref, rows_of(w_out, shard), shard_peer(2))
    x_down = copies.send(
        wd_ref.at[pl.ds(pl.multiple_of(y_side * half_down, LANES), half_down)],
        rows_of(w_down, shard, y_side * half_down, half_down),
        shard_peer(2),
    )
    half_up = wu_ref.shape[0] // 2
    x_up = [
        copies.send(
            wu_ref.at[pl.ds(half * half_up, half_up)],
            w_up.at[aligned_rows(shard * 2 + half, half_up)],
            shard_peer(2),
        )
        for half in range(2)
    ]
    core_weights = copies.send_all(
        [(ref, rows_of(full, shard), shard_peer(1)) for ref, full in full_weights], partial.at[0]
    )

    for copy in own_weights:
        copy.wait()
    own_mem[...] = jnp.zeros_like(own_mem)
    for seq in range(own_mem.shape[0]):
        own_mem[seq, :MEM_ROWS, :] = mem_in[:, seq, :]

    passed_pair, passed_y = [], []
    for half, copy in enumerate(far_tokens):
        copy.wait()
        place = tokens.at[half_rows(partner, half)]
        passed_pair.append(
            copies.send_all(
                [(place, place, ctx_peer(3)), (place, place, ctx_peer(2))], tokens.at[pl.ds(0, span)]
            )
        )
        passed_y.append(copies.send(place, place, ctx_peer(1)))
    x_heads.wait()
    x_owner = flipped(shard, 2, 2)
    place = rows_of(w_heads, x_owner)
    passed_heads = copies.send(place, place, shard_peer(1))
    x_out.wait()
    x_down.wait()
    place = rows_of(w_down, x_owner, y_side * half_down, half_down)
    y_down = copies.send(place, place, ctx_peer(1))
    passed_early = copies.send_all(
        [(part, part, shard_peer(1)) for part in (rows_of(w_out, x_owner), place)],
        partial.at[0, pl.ds(0, LANES + half_down)],
    )

    for copy in own_blocks:
        copy.wait()
    for copy in (core_heads, passed_heads, vec_copies):
        copy.wait()

    def full_vec(kind):
        return jnp.concatenate([vecs[owner, kind : kind + 1, :] for owner in range(4)], axis=1)

    length = len_ref[upper]
    lane = lax.broadcasted_iota(jnp.int32, (span * 2, LANES), 1)

    def put_query(rows, projected):
        scaled = (projected + vecs[pair, 0:1, :]).astype(bf16).astype(f32) * (HEAD_DIM**-0.5)
        q_scaled[rows, :] = scaled.astype(bf16)
        q_aug[0, rows, :] = jnp.where(
            lane < HEAD_DIM, scaled, jnp.where(lane == HEAD_DIM, 1.0, 0.0)
        ).astype(bf16)
        q_aug[1, rows, :] = jnp.where(
            lane >= HEAD_DIM, scaled, jnp.where(lane == 0, 1.0, 0.0)
        ).astype(bf16)

    def put_key_value(rows, key, value, left_out):
        lanes = lax.broadcasted_iota(jnp.int32, key.shape, 1)
        key = key.astype(bf16).astype(f32)
        value = (value + vecs[pair, 1:2, :]).astype(bf16).astype(f32)
        k_aug[0, rows, :] = jnp.where(
            lanes < HEAD_DIM, key, jnp.where(lanes == HEAD_DIM, left_out, 0.0)
        ).astype(bf16)
        k_aug[1, rows, :] = jnp.where(
            lanes >= HEAD_DIM, key, jnp.where(lanes == 0, left_out, 0.0)
        ).astype(bf16)
        v_mask[0, rows, :] = jnp.where(lanes < HEAD_DIM, value, 0.0).astype(bf16)
        v_mask[1, rows, :] = jnp.where(lanes >= HEAD_DIM, value, 0.0).astype(bf16)
        k_turned[:, rows] = key.T.astype(bf16)
        v_turned[:, rows] = value.T.astype(bf16)

    def block_rows(high):
        block = lax.div(flipped(ctx, 2 * high, 3), 2)
        return block, pl.ds(pl.multiple_of(block * span * 2, span * 2), span * 2)

    arrivals = ([near_y], [near_pair], passed_pair, passed_y)
    for high in (0, 1, 3, 2):
        for copy in arrivals[high]:
            copy.wait()
        block, rows = block_rows(high)
        projected = matmul(tokens[rows, :], w_heads[...])
        put_query(rows, projected[:, :LANES])
        position = block * span * 2 + lax.broadcasted_iota(jnp.int32, (span * 2, LANES), 0)
        put_key_value(
            rows,
            projected[:, LANES : 2 * LANES],
            projected[:, 2 * LANES :],
            jnp.where(position < length, 0.0, -1e30),
        )
    projected = matmul(own_mem[upper], w_heads[:, LANES:])
    position = lax.broadcasted_iota(jnp.int32, (MEM_PAD, LANES), 0)
    put_key_value(
        pl.ds(length_all, MEM_PAD),
        projected[:, :LANES],
        projected[:, LANES:],
        jnp.where(position < MEM_ROWS, 0.0, -1e30),
    )

    att_copies = []
    for high in (3, 2, 1, 0):
        if high == 1:
            x_up[0].wait()
            place = w_up.at[aligned_rows(x_owner * 2, half_up)]
            passed_up = copies.send(place, place, shard_peer(1))
        _, rows = block_rows(high)
        for head in range(2):
            scores = back_product(k_aug[head], q_aug[head, rows, :])
            exponent = jnp.exp(scores - jnp.max(scores, axis=0, keepdims=True))
            total = jnp.sum(exponent, axis=0, keepdims=True)
            inverse = 1.0 / total
            inverse_total[head : head + 1, rows] = inverse
            weights = exponent.astype(bf16)
            probs[head, :, rows] = weights
            half = pl.ds(head * HEAD_DIM, HEAD_DIM)
            mixed_t[half, rows] = matmul(v_turned[half, :], weights) * inverse
        mixed[rows, :] = mixed_t[:, rows].T.astype(bf16)
        att_items = []
        for low in (0, 1):
            offset = 2 * high + low
            source = mixed.at[span_rows(flipped(ctx, offset, 3))]
            target = att.at[span_rows(upper), pair_lanes(pair)]
            if offset:
                att_items.append((source, target, ctx_peer(offset)))
            else:
                own_att = copies.keep([(source, target)], source)

        att_copies.append(copies.send_all(att_items, mixed.at[pl.ds(0, span * len(att_items))]))

    y_down.wait()
    x_up[1].wait()
    places = (
        w_up.at[aligned_rows(x_owner * 2 + 1, half_up)],
        rows_of(w_down, x_owner, (1 - y_side) * half_down, half_down),
    )
    passed_weights = copies.send_all(
        [(place, place, shard_peer(1)) for place in places],
        partial.at[0, pl.ds(0, half_down + 4 * half_up)],
    )
    for block in range(4):
        rows = pl.ds(block * span * 2, span * 2)
        tokens_t[:, rows] = tokens[rows, :].astype(f32).T.astype(bf16)
    core_weights.wait()
    passed_early.wait()
    own_att.wait()
    for copy in att_copies:
        copy.wait()

    seqs = own_in.shape[0]
    local_rows = seqs * span
    own_x = own_in[...].reshape(local_rows, width).astype(f32)
    branch = matmul(att[...], w_out[...]) + full_vec(2)
    normed, unit_one, inverse_one = norm_forward(own_x + branch, full_vec(4), full_vec(5))
    normed_low = normed.astype(bf16)
    passed_up.wait()
    passed_weights.wait()
    ffn_out = jnp.zeros((local_rows, width), f32)
    for chunk in range(4):
        columns = pl.ds(chunk * width, width)
        bias = jnp.concatenate([vecs[chunk, 8 + i : 9 + i, :] for i in range(4)], axis=1)
        pre_act = matmul(normed_low, w_up[:, columns]) + bias
        square = pre_act * pre_act
        bent = jnp.tanh(GELU_SCALE * pre_act * (1.0 + 0.044715 * square))
        hidden[:, columns] = (0.5 * pre_act * (1.0 + bent)).astype(bf16)
        act_slope[:, columns] = 0.5 * (1.0 + bent) + 0.5 * pre_act * (1.0 - bent * bent) * (
            GELU_SCALE * (1.0 + 3 * 0.044715 * square)
        )
        ffn_out = ffn_out + matmul(hidden[:, columns], w_down[columns, :])
    ffn_out = ffn_out + full_vec(3)
    output, unit_two, inverse_two = norm_forward(normed + ffn_out, full_vec(6), full_vec(7))
    out_rows[...] = output.astype(bf16)

    chunks = []
    first_row = 0
    for rows, order in PIECES:
        chunks.append((first_row, rows, order))
        first_row += rows
    sides = {"x": x_half, "y": y_side, "z": z_side}
    peers = {"x": shard_peer(2), "y": ctx_peer(1), "z": ctx_peer(2)}
    waits = {}
    out_copies = [copies.keep([(out_rows, o_layer)], out_rows)]
    final_out, input_out = copies.keep([], final), copies.keep([], in_grad)
    out_copies += [final_out, input_out]

    def arrived(key):
        waits.pop(key).wait()

    def add_rows(target, first):
        target[...] = (target[...].astype(f32) + first[...].astype(f32)).astype(bf16)

    def aligned(start, rows):
        return pl.ds(pl.multiple_of(start, rows), rows)

    def core_send(number):
        start, rows, _ = chunks[number]
        waits["core", number] = copies.send_all(
            [
                (
                    partial.at[2 * side + 1 - core, pl.ds(start, rows)],
                    got_core.at[side, pl.ds(start, rows)],
                    shard_peer(1),
                )
                for side in range(2)
            ],
            partial.at[0, pl.ds(0, 2 * rows)],
        )

    def slabs(number, step):
        start, rows, order = chunks[number]
        if step == 0:
            return [got_core.at[side, pl.ds(start, rows)] for side in range(2)]
        buffer = (got_first, got_second, got_third)[step - 1]
        size = rows >> (step - 1)
        first = start >> (step - 1)
        if "x" in order[:step]:
            return [buffer.at[pl.ds(first, size)]]
        return [buffer.at[pl.ds(first + side * (size // 2), size // 2)] for side in range(2)]

    def split(number, step):
        whole = slabs(number, step)
        axis = chunks[number][2][step]
        side = sides[axis]
        if axis == "x":
            start, rows, _ = chunks[number]
            if step == 0:
                return (
                    [got_core.at[side, pl.ds(start, rows)]],
                    [got_core.at[1 - side, pl.ds(start, rows)]],
                )
            buffer = (got_first, got_second, got_third)[step - 1]
            size, first = rows >> step, start >> (step - 1)
            return (
                [buffer.at[aligned(first + side * size, size)]],
                [buffer.at[aligned(first + (1 - side) * size, size)]],
            )
        half = whole[0].shape[0] // 2
        return (
            [slab.at[aligned(side * half, half)] for slab in whole],
            [slab.at[aligned((1 - side) * half, half)] for slab in whole],
        )

    def halve(number, step):
        if step == 0:
            arrived(("core", number))
            for side, slab in enumerate(slabs(number, 0)):
                start, rows, _ = chunks[number]
                add_rows(slab, partial.at[2 * side + core, pl.ds(start, rows)])
        else:
            join(number, step)
        axis = chunks[number][2][step]
        _, gone = split(number, step)
        start, rows, _ = chunks[number]
        waits[step, number] = copies.send_all(
            [(slab, target, peers[axis]) for slab, target in zip(gone, slabs(number, step + 1))],
            (got_first, got_second, got_third)[step].at[pl.ds(start >> step, rows >> step)],
        )

    def join(number, step):
        arrived((step - 1, number))
        kept, _ = split(number, step - 1)
        for target, slab in zip(slabs(number, step), kept):
            add_rows(target, slab)

    def cross(number):
        join(number, 3)
        start, rows, _ = chunks[number]
        here = pl.ds(start // 4, rows // 4)
        waits["cross", number] = copies.send(got_third.at[here], got_far.at[here], ctx_peer(6))

    def place_of(number, count):
        start, rows, order = chunks[number]
        for axis in order.replace("x", "")[: 2 - count]:
            rows = rows // 2
            start = start + sides[axis] * rows
        return aligned(start, rows)

    def gather(number, count):
        start, rows, order = chunks[number]
        if count == 0:
            arrived(("cross", number))
            here = pl.ds(start // 4, rows // 4)
            final[place_of(number, 0), :] = (
                got_third[here, :].astype(f32) + got_far[here, :].astype(f32)
            ).astype(bf16)
        else:
            arrived(("gather", number))
        place = final.at[place_of(number, count)]
        waits["gather", number] = copies.send(
            place, place, peers[order.replace("x", "")[1 - count]]
        )

    def write_out(number):
        start, rows, _ = chunks[number]
        arrived(("gather", number))
        place = pl.ds(start, rows)
        pltpu.make_async_copy(final.at[place], o_fin.at[place], final_out.semaphore).start()

    def outer_part(number):
        start, rows, _ = chunks[number]
        done = 0
        while done < rows:
            row = start + done
            if row < width:
                size = min(rows - done, width - row)
                for owner in range(4):
                    columns = slice(owner * width + row, owner * width + row + size)
                    partial[owner, row : row + size, :] = outer_sum(
                        hidden[:, columns], held.d_ffn
                    ).astype(bf16)
            else:
                size = LANES
                if row < 2 * width:
                    chunk = (row - width) // LANES
                    grad = outer_sum(
                        held.normed, d_pre[:, chunk * width : (chunk + 1) * width]
                    ).astype(bf16)
                else:
                    grad = outer_sum(att[...], d_branch[...]).astype(bf16)
                for owner in range(4):
                    partial[owner, row : row + size, :] = grad[owner * LANES : (owner + 1) * LANES]
            done += size
        core_send(number)

    held = Held()
    held.normed = normed_low


    def second_norm():
        cotangent = own_g[...].reshape(local_rows, width).astype(f32)
        held.two, held.second_gain, held.second_bias = norm_backward(
            cotangent, unit_two, inverse_two, full_vec(6)
        )
        held.d_ffn = held.two.astype(bf16)

    def first_norm():
        d_normed = held.two
        for chunk in range(4):
            columns = pl.ds(chunk * width, width)
            d_hidden = back_product(held.d_ffn, w_down[columns, :])
            d_chunk = (d_hidden * act_slope[:, columns]).astype(bf16)
            d_pre[:, columns] = d_chunk
            d_normed = d_normed + back_product(d_chunk, w_up[:, columns])
        d_one, held.first_gain, held.first_bias = norm_backward(
            d_normed, unit_one, inverse_one, full_vec(4)
        )
        in_grad[...] = d_one
        d_branch[...] = d_one.astype(bf16)

    def attended_grad():
        held.d_att = []
        for rows_of_seq, offsets in ((1 - upper, (6, 7, 4, 5)), (upper, (2, 3, 1, 0))):
            rows = span_rows(rows_of_seq)
            d_att[rows, :] = back_product(d_branch[rows, :], w_out[...]).astype(bf16)
            items = []
            for offset in offsets:
                peer = flipped(ctx, offset, 3)
                source = d_att.at[rows, pair_lanes(lax.rem(peer, 4))]
                target = d_mixed.at[span_rows(ctx)]
                if offset:
                    items.append((source, target, ctx_peer(offset)))
                else:
                    held.own_d_att = copies.keep([(source, target)], target)
            held.d_att.append(copies.send_all(items, d_mixed.at[pl.ds(0, span * len(items))]))

    def square_sums():
        row_id = lax.broadcasted_iota(jnp.int32, (8, LANES), 0)
        tile = jnp.zeros((8, LANES), f32)
        for seq in range(seqs):
            position = ctx * span + lax.broadcasted_iota(jnp.int32, (span, 1), 0)
            valid = jnp.where(position < len_ref[seq], 1.0, 0.0)
            for kind, values in enumerate((own_x, branch, ffn_out)):
                piece = values[seq * span : (seq + 1) * span]
                row_sum = jnp.sum(piece * piece, axis=1, keepdims=True) * valid
                tile = tile + jnp.where(
                    row_id == seq * 3 + kind, jnp.sum(row_sum, axis=0, keepdims=True), 0.0
                )
        squares[ctx] = tile
        held.squares = copies.send_all(
            [
                (squares.at[ctx], squares.at[ctx], ctx_peer(offset))
                for offset in (6, 7, 4, 5, 2, 3, 1)
            ],
            squares.at[pl.ds(0, 7)],
        )

    def narrow_grads():
        vec_part[...] = jnp.zeros_like(vec_part)
        wide_grads = (
            jnp.sum(d_branch[...].astype(f32), axis=0, keepdims=True),
            jnp.sum(held.d_ffn.astype(f32), axis=0, keepdims=True),
            held.first_gain,
            held.first_bias,
            held.second_gain,
            held.second_bias,
        )
        for owner in range(4):
            for kind, values in enumerate(wide_grads):
                vec_part[owner, 2 + kind : 3 + kind, :] = values.reshape(1, width)[
                    :, owner * LANES : (owner + 1) * LANES
                ]
            columns = pl.ds(owner * width, width)
            bias = jnp.sum(d_pre[:, columns].astype(f32), axis=0, keepdims=True)
            for part in range(4):
                vec_part[owner, 8 + part : 9 + part, :] = bias[
                    :, part * LANES : (part + 1) * LANES
                ]

    def deltas():
        held.own_d_att.wait()
        for copy in held.d_att:
            copy.wait()
        turned = d_mixed[...].astype(f32).T
        products = turned * mixed_t[...]
        held.deltas = []
        for head in range(2):
            half = slice(head * HEAD_DIM, (head + 1) * HEAD_DIM)
            inverse = inverse_total[head : head + 1, :]
            held.deltas.append(jnp.sum(products[half], axis=0, keepdims=True) * inverse)
            d_scaled_t[half, :] = (turned[half] * inverse).astype(bf16)
        d_scaled[...] = d_scaled_t[...].astype(f32).T.astype(bf16)

    def score_grads(head):
        delta = held.deltas[head]
        for block in range(4):
            rows = slice(block * span * 2, (block + 1) * span * 2)
            dots = matmul(v_mask[head], d_scaled_t[:, rows])
            weights = probs[head, :, rows].astype(f32)
            d_scores[head, :, rows] = (weights * (dots - delta[:, rows])).astype(bf16)

    def scores_0():
        score_grads(0)

    def scores_1():
        score_grads(1)

    def key_value_grads():
        key_lane = lax.broadcasted_iota(jnp.int32, (keys, LANES), 1)
        grad_value = jnp.where(
            key_lane < HEAD_DIM, matmul(probs[0], d_scaled[...]), matmul(probs[1], d_scaled[...])
        ).astype(bf16)
        grad_key = jnp.where(
            key_lane < HEAD_DIM,
            matmul(d_scores[0], q_scaled[...]),
            matmul(d_scores[1], q_scaled[...]),
        ).astype(bf16)
        joined[:, LANES : 2 * LANES] = grad_key[:length_all]
        joined[:, 2 * LANES :] = grad_value[:length_all]
        held.memory = jnp.concatenate([grad_key[length_all:], grad_value[length_all:]], axis=1)
        held.value = jnp.sum(grad_value.astype(f32), axis=0, keepdims=True)

    def query_grads():
        grad_query = jnp.concatenate(
            [
                matmul(k_turned[:HEAD_DIM, :], d_scores[0]),
                matmul(k_turned[HEAD_DIM:, :], d_scores[1]),
            ],
            axis=0,
        ) * (HEAD_DIM**-0.5)
        grad_query = grad_query.T.astype(bf16)
        joined[:, :LANES] = grad_query
        held.query = jnp.sum(grad_query.astype(f32), axis=0, keepdims=True)

    def input_part(mirror, order):
        for place, offset in enumerate(order):
            rows = span_rows(flipped(ctx, offset ^ mirror, 3))
            dx_part[
                4 * (mirror == 0) + place
            ] = back_product(joined[rows, :], w_heads[...]).astype(bf16)

    def two(ref, first):
        return ref.at[pl.ds(first, 2)]

    def input_far():
        input_part(6, (0, 2, 1, 3))
        held.far_y = copies.send(two(dx_part, 2), two(dx_got, 0), ctx_peer(1))

    def input_near():
        input_part(0, (0, 2, 1, 3))
        held.near_y = copies.send(two(dx_part, 6), two(dx_got, 2), ctx_peer(1))

    def input_far_z():
        held.far_y.wait()
        add_rows(two(dx_part, 0), two(dx_got, 0))
        held.far_z = copies.send(dx_part.at[1], dx_got.at[4], ctx_peer(2))

    def input_near_z():
        held.near_y.wait()
        add_rows(two(dx_part, 4), two(dx_got, 2))
        held.near_z = copies.send(dx_part.at[5], dx_got.at[5], ctx_peer(2))

    def input_cross():
        held.far_z.wait()
        add_rows(dx_got.at[4], dx_part.at[0])
        held.cross = copies.send(dx_got.at[4], dx_far, ctx_peer(6))

    def write_input_rows(index, parts):
        rows = span_rows(index)
        total = in_grad[rows, :]
        for part in parts:
            total = total + part.astype(f32)
        in_grad[rows, :] = total
        pltpu.make_async_copy(in_grad.at[rows], o_input.at[rows], input_out.semaphore).start()

    def input_near_out():
        held.near_z.wait()
        write_input_rows(upper, (dx_part[4], dx_got[5]))

    def input_far_out():
        held.cross.wait()
        write_input_rows(1 - upper, (dx_far[...],))

    def memory_part():
        mem_part[pair] = back_product(held.memory, w_heads[:, LANES:]).astype(bf16)
        held.mem = copies.send_all(
            [(mem_part.at[pair], mem_part.at[pair], ctx_peer(offset)) for offset in (3, 2, 1)],
            mem_part.at[pl.ds(0, 3)],
        )

    def memory_cross():
        held.mem.wait()
        mem_far[upper] = (
            mem_part[0].astype(f32)
            + mem_part[1].astype(f32)
            + mem_part[2].astype(f32)
            + mem_part[3].astype(f32)
        ).astype(bf16)
        held.mem_far = copies.send(mem_far.at[upper], mem_far.at[upper], ctx_peer(6))

    def memory_out():
        held.mem_far.wait()
        out_copies.append(copies.keep([(mem_far, o_mem)], mem_far))

    def head_grads():
        grad_heads = matmul(tokens_t[...], joined[...])
        mem_grad = outer_sum(own_mem[upper], held.memory)
        for owner in range(4):
            rows = slice(owner * LANES, (owner + 1) * LANES)
            head_part[owner, :LANES, :LANES] = grad_heads[rows, :LANES].astype(bf16)
            head_part[owner, :LANES, LANES:] = (grad_heads[rows, LANES:] + mem_grad[rows]).astype(
                bf16
            )
            mine = pair == owner
            vec_part[owner, 0:1, :] = jnp.where(mine, held.query, 0.0)
            vec_part[owner, 1:2, :] = jnp.where(mine, held.value, 0.0)
            head_part[owner, LANES:, :] = jnp.zeros((ROW_KINDS, 3 * LANES), bf16)
            head_part[owner, LANES:, :LANES] = vec_part[owner].astype(bf16)
        held.head_core = copies.send_all(
            [
                (head_part.at[2 * side + 1 - core], head_core.at[side], shard_peer(1))
                for side in range(2)
            ],
            head_core,
        )

    def head_x_send():
        held.head_core.wait()
        for side in range(2):
            add_rows(head_core.at[side], head_part.at[2 * side + core])
        held.head_x = copies.send(head_core.at[1 - x_half], head_x, shard_peer(2))

    def head_far_send():
        held.head_x.wait()
        add_rows(head_x, head_core.at[x_half])
        held.head_far = copies.send(head_x, head_far, ctx_peer(4))

    def head_gather():
        held.head_far.wait()
        head_all[pair] = (head_x[...].astype(f32) + head_far[...].astype(f32)).astype(bf16)
        held.heads = copies.send(head_all.at[pair], head_all.at[pair], ctx_peer(2))

    def head_spread():
        held.heads.wait()
        places = [head_all.at[index] for index in (pair, flipped(pair, 2, 2))]
        held.heads = copies.send_all(
            [(place, place, ctx_peer(1)) for place in places], head_all.at[pl.ds(0, 2)]
        )

    def head_out():
        held.heads.wait()
        out_copies.append(copies.keep([(head_all, o_heads)], head_all))

    def rms_out():
        held.squares.wait()
        row_id = lax.broadcasted_iota(jnp.int32, (8, LANES), 0)
        total = squares[0]
        for other in range(1, spans):
            total = total + squares[other]
        valid_tokens = jnp.where(row_id < 3, len_ref[0], len_ref[1]).astype(f32)
        rms_rows[...] = jnp.sqrt(total / (valid_tokens * width))
        out_copies.append(copies.keep([(rms_rows, o_rms)], rms_rows))

    second_norm()
    outer_part(0)
    outer_part(1)
    outer_part(2)
    outer_part(3)
    first_norm()
    attended_grad()
    outer_part(4)
    outer_part(5)
    outer_part(6)
    square_sums()
    narrow_grads()
    halve(0, 0)
    halve(1, 0)
    halve(2, 0)
    halve(3, 0)
    halve(4, 0)
    halve(5, 0)
    halve(0, 1)
    halve(6, 0)
    halve(2, 1)
    deltas()
    scores_0()
    halve(1, 1)
    scores_1()
    halve(3, 1)
    key_value_grads()
    halve(0, 2)
    halve(4, 1)
    query_grads()
    halve(2, 2)
    input_far()
    halve(3, 2)
    halve(5, 1)
    halve(6, 1)
    input_near()
    memory_part()
    cross(0)
    head_grads()
    halve(1, 2)
    cross(2)
    cross(3)
    halve(6, 2)
    halve(4, 2)
    gather(0, 0)
    head_x_send()
    cross(1)
    cross(6)
    gather(2, 0)
    gather(3, 0)
    cross(4)
    gather(0, 1)
    gather(1, 0)
    head_far_send()
    input_far_z()
    gather(6, 0)
    gather(2, 1)
    gather(3, 1)
    halve(5, 2)
    gather(4, 0)
    cross(5)
    input_cross()
    head_gather()
    input_near_z()
    gather(6, 1)
    memory_cross()
    gather(4, 1)
    write_out(0)
    gather(1, 1)
    gather(5, 0)
    write_out(2)
    write_out(3)
    write_out(6)
    input_far_out()
    head_spread()
    write_out(4)
    gather(5, 1)
    input_near_out()
    memory_out()
    rms_out()
    write_out(1)
    head_out()
    write_out(5)
    for copy in out_copies:
        copy.wait()
    copies.finish()
    assert (len(copies.sent), copies.received, copies.kept) == (SENDS, ARRIVALS, KEPT)


def outputs_kernel(layer, input_grad, mem_grad, weights, heads, rms, *outs):
    f32 = jnp.float32
    (
        o_layer,
        o_input,
        o_mem,
        o_query,
        o_key,
        o_value,
        o_out,
        o_up,
        o_down,
        o_b_query,
        o_b_value,
        o_b_out,
        o_b_up,
        o_b_down,
        o_first_gain,
        o_first_bias,
        o_second_gain,
        o_second_bias,
        o_rms,
    ) = outs
    width = weights.shape[1]
    o_layer[...] = layer[...].reshape(o_layer.shape)
    o_input[...] = input_grad[...].reshape(o_input.shape)
    for seq in range(o_mem.shape[1]):
        o_mem[:, seq, :] = mem_grad[seq].astype(f32)[:MEM_ROWS]
    o_down[...] = weights[:width, :].astype(f32)
    for chunk in range(4):
        o_up[:, chunk * width : (chunk + 1) * width] = weights[
            width + chunk * LANES : width + (chunk + 1) * LANES, :
        ].astype(f32)
    o_out[...] = weights[2 * width :, :].astype(f32)
    for owner in range(4):
        for part, ref in enumerate((o_query, o_key, o_value)):
            ref[:, owner * LANES : (owner + 1) * LANES] = heads[
                owner, :LANES, part * LANES : (part + 1) * LANES
            ].astype(f32)
    vec = (
        heads[0, LANES:, :LANES].astype(f32)
        + heads[1, LANES:, :LANES].astype(f32)
        + heads[2, LANES:, :LANES].astype(f32)
        + heads[3, LANES:, :LANES].astype(f32)
    )
    narrow = (
        o_b_query,
        o_b_value,
        o_b_out,
        o_b_down,
        o_first_gain,
        o_first_bias,
        o_second_gain,
        o_second_bias,
    )
    for kind, ref in enumerate(narrow):
        ref[...] = vec[kind]
    for piece in range(4):
        o_b_up[piece * LANES : (piece + 1) * LANES] = vec[8 + piece]
    for seq in range(o_rms.shape[0]):
        for kind in range(3):
            o_rms[seq : seq + 1, kind : kind + 1] = rms[seq * 3 + kind : seq * 3 + kind + 1, :1]


def fast_layer(
    inputs,
    memory,
    lengths,
    w_query,
    w_key,
    w_value,
    w_out,
    w_up,
    w_down,
    b_query,
    b_value,
    b_out,
    b_up,
    b_down,
    first_gain,
    first_bias,
    second_gain,
    second_bias,
    out_grad,
):
    bf16, f32 = jnp.bfloat16, jnp.float32
    seqs, span, width = inputs.shape
    length_all, keys = 8 * span, 8 * span + MEM_PAD
    hidden_width = w_up.shape[1]
    narrow = (b_query, b_value, b_out, b_down, first_gain, first_bias, second_gain, second_bias)
    vmem, anywhere = pl.BlockSpec(memory_space=pltpu.VMEM), pl.BlockSpec(memory_space=pl.ANY)
    smem = pl.BlockSpec(memory_space=pltpu.SMEM)
    stacked = 2 * width + LANES
    scratch = [
        ((seqs, span, width), bf16),
        ((seqs, span, width), bf16),
        ((seqs, MEM_PAD, width), bf16),
        ((memory.shape[1], seqs, width), bf16),
        *[(ref.shape, bf16) for ref in (*narrow, b_up)],
        ((8, LANES), f32),
        ((seqs * span, width), bf16),
        ((length_all, 3 * LANES), bf16),
        ((seqs * span, width), bf16),
        ((seqs * span, width), f32),
        ((length_all, width), bf16),
        ((width, length_all), bf16),
        ((width, 3 * LANES), bf16),
        ((width, width), bf16),
        ((width, hidden_width), bf16),
        ((hidden_width, width), bf16),
        ((4, ROW_KINDS, LANES), f32),
        ((length_all, LANES), bf16),
        ((2, length_all, LANES), bf16),
        ((2, keys, LANES), bf16),
        ((2, keys, LANES), bf16),
        ((LANES, keys), bf16),
        ((LANES, keys), bf16),
        ((2, keys, length_all), bf16),
        ((2, keys, length_all), bf16),
        ((LANES, length_all), f32),
        ((8, length_all), f32),
        ((length_all, LANES), bf16),
        ((LANES, length_all), bf16),
        ((length_all, LANES), bf16),
        ((seqs * span, width), bf16),
        ((seqs * span, hidden_width), bf16),
        ((seqs * span, hidden_width), f32),
        ((seqs * span, hidden_width), bf16),
        ((seqs * span, width), bf16),
        ((length_all, LANES), bf16),
        ((4, stacked, width), bf16),
        ((2, stacked, width), bf16),
        ((stacked, width), bf16),
        ((stacked // 2, width), bf16),
        ((stacked // 4, width), bf16),
        ((stacked // 4, width), bf16),
        ((stacked, width), bf16),
        ((4, LANES + ROW_KINDS, 3 * LANES), bf16),
        ((2, LANES + ROW_KINDS, 3 * LANES), bf16),
        ((LANES + ROW_KINDS, 3 * LANES), bf16),
        ((LANES + ROW_KINDS, 3 * LANES), bf16),
        ((4, LANES + ROW_KINDS, 3 * LANES), bf16),
        ((4, ROW_KINDS, LANES), f32),
        ((8, span, width), bf16),
        ((6, span, width), bf16),
        ((span, width), bf16),
        ((4, MEM_PAD, width), bf16),
        ((2, MEM_PAD, width), bf16),
        ((8, 8, LANES), f32),
    ]
    made = pl.pallas_call(
        layer_kernel,
        out_shape=[
            jax.ShapeDtypeStruct((seqs * span, width), bf16),
            jax.ShapeDtypeStruct((seqs * span, width), f32),
            jax.ShapeDtypeStruct((seqs, MEM_PAD, width), bf16),
            jax.ShapeDtypeStruct((stacked, width), bf16),
            jax.ShapeDtypeStruct((4, LANES + ROW_KINDS, 3 * LANES), bf16),
            jax.ShapeDtypeStruct((8, LANES), f32),
        ],
        in_specs=[anywhere] * 3 + [smem] + [anywhere] * 15,
        out_specs=[anywhere] * 6,
        scratch_shapes=[pltpu.VMEM(shape, kind) for shape, kind in scratch]
        + [pltpu.SemaphoreType.DMA((count,)) for count in (SENDS, ARRIVALS, KEPT)],
        compiler_params=pltpu.CompilerParams(
            collective_id=0, has_side_effects=True, vmem_limit_bytes=60 * 2**20
        ),
        name="layer",
    )(
        inputs,
        out_grad,
        memory.transpose(1, 0, 2),
        lengths,
        w_query,
        w_key,
        w_value,
        w_out,
        w_up,
        w_down,
        *narrow,
        b_up,
    )
    mem_rows = memory.shape[1]
    shapes = (
        ((seqs, span, width), bf16),
        ((seqs, span, width), f32),
        ((mem_rows, seqs, width), f32),
        (w_query.shape, f32),
        (w_key.shape, f32),
        (w_value.shape, f32),
        (w_out.shape, f32),
        (w_up.shape, f32),
        (w_down.shape, f32),
        (b_query.shape, f32),
        (b_value.shape, f32),
        (b_out.shape, f32),
        (b_up.shape, f32),
        (b_down.shape, f32),
        (first_gain.shape, f32),
        (first_bias.shape, f32),
        (second_gain.shape, f32),
        (second_bias.shape, f32),
        ((seqs, 3), f32),
    )
    outs = pl.pallas_call(
        outputs_kernel,
        out_shape=[jax.ShapeDtypeStruct(shape, kind) for shape, kind in shapes],
        in_specs=[vmem] * 6,
        out_specs=[vmem] * len(shapes),
        compiler_params=pltpu.CompilerParams(vmem_limit_bytes=60 * 2**20),
        name="outputs",
    )(*made)
    return (*outs[:2], outs[2].transpose(1, 0, 2), *outs[3:])


def takes_fast_plan(mesh, inputs, memory, w_up):
    return (
        mesh.shape["shard"] == 4
        and mesh.shape["ctx"] == 8
        and inputs.shape == (2, LANES, HEADS * HEAD_DIM)
        and memory.shape[1] == MEM_ROWS
        and w_up.shape == (LANES, 4 * HEADS * HEAD_DIM)
    )


def solution(mesh):
    in_specs = (
        P("shard", "ctx", None),
        P("shard", None, None),
        P("shard"),
        P("shard", None),
        P("shard", None),
        P("shard", None),
        P("shard", None),
        P("shard", None),
        P("shard", None),
        P("shard"),
        P("shard"),
        P("shard"),
        P("shard"),
        P("shard"),
        P("shard"),
        P("shard"),
        P("shard"),
        P("shard"),
        P("shard", "ctx", None),
    )
    out_specs = (
        P("shard", "ctx", None),
        P("shard", "ctx", None),
        P("shard", None, None),
        P("shard", None),
        P("shard", None),
        P("shard", None),
        P("shard", None),
        P("shard", None),
        P("shard", None),
        P("shard"),
        P("shard"),
        P("shard"),
        P("shard"),
        P("shard"),
        P("shard"),
        P("shard"),
        P("shard"),
        P("shard"),
        P("shard", None),
    )

    def layer(*arrays):
        if takes_fast_plan(mesh, arrays[0], arrays[1], arrays[7]):
            return fast_layer(*arrays)
        return local(*arrays)

    return jax.shard_map(layer, mesh=mesh, in_specs=in_specs, out_specs=out_specs, check_vma=False)
```
